32 devices in a mesh: blk: 2 (over x), theta: 4 (over z), radial: 4 (over y, core).
Axes of the slice: x: 2, y: 2, z: 4, core: 2. Of those that a mesh axis runs over, the one named last changes fastest.
Arguments:
- base_state: float32 [5, 12, 32, 4096], P(None, 'blk', 'radial', 'theta'), may hold values from -4 to 12, as said below
- section_state: float32 [5, 12, 32, 4096], P(None, 'blk', 'radial', 'theta'), may hold values from -4 to 12, as said below
- rotor_step: int32 [1], replicated, may hold values from 4096 to 16383
Outputs:
- next_state: float32 [5, 12, 32, 4096], P(None, 'blk', 'radial', 'theta')
The draws below stay inside these ranges and needn't reach their ends.
Inputs may be any that keep to these rules, and one draw needn't show every extreme that they name: `base_state`: density between 0.5 and 2, pressure between 0.5 and 2, every velocity component under 2 in magnitude. `section_state`: density between 0.5 and 2, pressure between 0.5 and 2, every velocity component under 2 in magnitude.
All inputs are finite; a program needn't handle non-finite values.
Results may differ from the reference program's by a relative error of at most 0.0003.
Values sent between devices are 32-bit elements; how exact they have to be, the bound alone decides.
No kernel may reach another device: no remote copies, remote signals or barrier semaphores. Data moves between devices by JAX's collectives and lax.ppermute only.
A program may use at most 64 MiB of HBM per device.

```python
import math
import jax
import jax.numpy as jnp
from jax import lax

ZD = 6
TD = 1024
NZ = 12
NR = 32
NT = 4096


gamma_ratio = 1.4


def physical_state(key):
    density_key, velocity_key, pressure_key = jax.random.split(key, 3)
    shape = (NZ, NR, NT)
    density = jnp.exp(jax.random.uniform(density_key, shape, jnp.float32, math.log(0.5), math.log(2.0)))
    velocity = jnp.clip(0.5 * jax.random.normal(velocity_key, (3, NZ, NR, NT), jnp.float32), -1.5, 1.5)
    pressure = jnp.exp(jax.random.uniform(pressure_key, shape, jnp.float32, math.log(0.5), math.log(2.0)))
    energy = pressure / (gamma_ratio - 1.0) + 0.5 * density * jnp.sum(jnp.square(velocity), axis=0)
    return jnp.concatenate([density[None], density[None] * velocity, energy[None]], axis=0)


def draw_base_state(key, part):
    return physical_state(jax.random.fold_in(key, 11))


def draw_section_state(key, part):
    return physical_state(jax.random.fold_in(key, 23))


def setup_inputs(seed: int = 0) -> dict:
    key_list = jax.random.split(jax.random.key(seed), 4)
    base_state = draw_base_state(jax.random.fold_in(key_list[3], 71), 0)
    section_state = draw_section_state(jax.random.fold_in(key_list[3], 71), 0)
    rotor_step = jax.random.randint(key_list[2], (1,), 4 * TD, 4 * NT).astype(jnp.int32)
    return {"base_state": base_state, "section_state": section_state, "rotor_step": rotor_step}


gamma_ratio = 1.4
weno_epsilon = 1e-06
step_ratio = 0.12

def pressure_of(state):
    kinetic = 0.5 * (jnp.square(state[1]) + jnp.square(state[2]) + jnp.square(state[3])) / state[0]
    return (gamma_ratio - 1.0) * (state[4] - kinetic)

def euler_flux(state, normal):
    pressure = pressure_of(state)
    velocity = state[normal] / state[0]
    flux = state * velocity[None]
    flux = flux.at[normal].add(pressure)
    flux = flux.at[4].add(pressure * velocity)
    return flux

def wave_speed(state, normal):
    pressure = pressure_of(state)
    return jnp.abs(state[normal] / state[0]) + jnp.sqrt(gamma_ratio * pressure / state[0])

def weno_side(far_left, left_cell, centre, right_cell, far_right):
    smooth_low = 13.0 / 12.0 * jnp.square(far_left - 2.0 * left_cell + centre) + 0.25 * jnp.square(far_left - 4.0 * left_cell + 3.0 * centre)
    smooth_mid = 13.0 / 12.0 * jnp.square(left_cell - 2.0 * centre + right_cell) + 0.25 * jnp.square(left_cell - right_cell)
    smooth_high = 13.0 / 12.0 * jnp.square(centre - 2.0 * right_cell + far_right) + 0.25 * jnp.square(3.0 * centre - 4.0 * right_cell + far_right)
    weight_low = 0.1 / jnp.square(weno_epsilon + smooth_low)
    weight_mid = 0.6 / jnp.square(weno_epsilon + smooth_mid)
    weight_high = 0.3 / jnp.square(weno_epsilon + smooth_high)
    guess_low = (2.0 * far_left - 7.0 * left_cell + 11.0 * centre) / 6.0
    guess_mid = (-left_cell + 5.0 * centre + 2.0 * right_cell) / 6.0
    guess_high = (2.0 * centre + 5.0 * right_cell - far_right) / 6.0
    return (weight_low * guess_low + weight_mid * guess_mid + weight_high * guess_high) / (weight_low + weight_mid + weight_high)

def face_flux(padded, fluxes, axis, count, normal, first, second):
    states = [lax.slice_in_dim(padded, shift_index, shift_index + count + 1, axis=axis) for shift_index in range(6)]
    physical = [lax.slice_in_dim(fluxes, shift_index, shift_index + count + 1, axis=axis) for shift_index in range(6)]
    mean = 0.5 * (states[2] + states[3])
    density = mean[0]
    normal_speed = mean[normal] / density
    speed_first = mean[first] / density
    speed_second = mean[second] / density
    kinetic = 0.5 * (jnp.square(normal_speed) + jnp.square(speed_first) + jnp.square(speed_second))
    pressure = pressure_of(mean)
    sound = jnp.sqrt(gamma_ratio * pressure / density)
    enthalpy = (mean[4] + pressure) / density
    inv_sound = 1.0 / sound
    factor_one = (gamma_ratio - 1.0) * jnp.square(inv_sound)
    factor_two = factor_one * kinetic
    dissipation = jnp.maximum(wave_speed(states[2], normal), wave_speed(states[3], normal))

    def project(vector):
        dens_part = vector[0]
        norm_part = vector[normal]
        first_part = vector[first]
        second_part = vector[second]
        energy_part = vector[4]
        tangent_sum = factor_one * (speed_first * first_part + speed_second * second_part - energy_part)
        wave_minus = 0.5 * ((factor_two + normal_speed * inv_sound) * dens_part - (factor_one * normal_speed + inv_sound) * norm_part - tangent_sum)
        entropy = (1.0 - factor_two) * dens_part + factor_one * normal_speed * norm_part + tangent_sum
        shear_first = first_part - speed_first * dens_part
        shear_second = second_part - speed_second * dens_part
        wave_plus = 0.5 * ((factor_two - normal_speed * inv_sound) * dens_part - (factor_one * normal_speed - inv_sound) * norm_part - tangent_sum)
        return (wave_minus, entropy, shear_first, shear_second, wave_plus)
    state_chars = [project(cell_state) for cell_state in states]
    flux_chars = [project(cell_flux) for cell_flux in physical]
    recon = []
    for field_index in range(5):
        plus_vals = [0.5 * (flux_chars[cell][field_index] + dissipation * state_chars[cell][field_index]) for cell in range(6)]
        minus_vals = [0.5 * (flux_chars[cell][field_index] - dissipation * state_chars[cell][field_index]) for cell in range(6)]
        recon.append(weno_side(plus_vals[0], plus_vals[1], plus_vals[2], plus_vals[3], plus_vals[4]) + weno_side(minus_vals[5], minus_vals[4], minus_vals[3], minus_vals[2], minus_vals[1]))
    wave_minus, entropy, shear_first, shear_second, wave_plus = recon
    acoustic = wave_minus + entropy + wave_plus
    parts = {}
    parts[0] = acoustic
    parts[normal] = (normal_speed - sound) * wave_minus + normal_speed * entropy + (normal_speed + sound) * wave_plus
    parts[first] = speed_first * acoustic + shear_first
    parts[second] = speed_second * acoustic + shear_second
    parts[4] = (enthalpy - normal_speed * sound) * wave_minus + kinetic * entropy + speed_first * shear_first + speed_second * shear_second + (enthalpy + normal_speed * sound) * wave_plus
    return jnp.stack([parts[index_part] for index_part in range(5)])

def divergence(padded, axis, count, normal, first, second):
    faces = face_flux(padded, euler_flux(padded, normal), axis, count, normal, first, second)
    return lax.slice_in_dim(faces, 1, count + 1, axis=axis) - lax.slice_in_dim(faces, 0, count, axis=axis)

def flip_radial(cells):
    turned = cells[:, :, ::-1]
    return jnp.concatenate([turned[:3], -turned[3:4], turned[4:]], axis=0)

def flip_theta(cells):
    return jnp.concatenate([cells[:2], -cells[2:3], cells[3:]], axis=0)

def mortar(planes, offset, fraction):
    count = planes.shape[3]
    cells = jnp.arange(count, dtype=jnp.int32)
    lower_index = ((offset - cells - 1) % count).astype(jnp.int32)
    upper_index = ((offset - cells) % count).astype(jnp.int32)
    blended = (1.0 - fraction) * jnp.take(planes, lower_index, axis=3) + fraction * jnp.take(planes, upper_index, axis=3)
    return flip_theta(blended)

def reference(base_state, section_state, rotor_step):
    state = section_state
    offset = rotor_step[0] // 4
    fraction = (rotor_step[0] % 4).astype(jnp.float32) / 4.0
    theta_padded = jnp.concatenate([state[..., -3:], state, state[..., :3]], axis=3)
    radial_padded = jnp.concatenate([flip_radial(state[:, :, :3]), state, flip_radial(state[:, :, -3:])], axis=2)
    front = state[:, :ZD]
    aft = state[:, ZD:]
    front_padded = jnp.concatenate([front[:, :1], front[:, :1], front[:, :1], front, mortar(aft[:, :3], offset, fraction)], axis=1)
    aft_padded = jnp.concatenate([mortar(front[:, -3:], offset, fraction), aft, aft[:, -1:], aft[:, -1:], aft[:, -1:]], axis=1)
    axial = jnp.concatenate([divergence(front_padded, 1, ZD, 1, 2, 3), divergence(aft_padded, 1, ZD, 1, 2, 3)], axis=1)
    radial = divergence(radial_padded, 2, NR, 3, 1, 2)
    azimuthal = divergence(theta_padded, 3, NT, 2, 1, 3)
    change = -step_ratio * (axial + radial + azimuthal)
    return 0.75 * base_state + 0.25 * (state + change)
```

```python
import functools

import jax
import jax.numpy as jnp
from jax import lax
from jax.experimental import pallas as pl
from jax.experimental.pallas import tpu as pltpu
from jax.sharding import PartitionSpec as P

gamma_ratio = 1.4
weno_epsilon = 1e-06
step_ratio = 0.12
lanes = 128
ghosts = 3
group = 16
flux_scale = 12.0
vmem_bytes = 48 * 1024 * 1024

axial_order = (0, 1, 2, 3, 4)
radial_order = (0, 3, 1, 2, 4)
theta_order = (0, 2, 1, 3, 4)


def inverse(value):
    guess = pl.reciprocal(value, approx=True)
    return guess * (2.0 - value * guess)


def cell_terms(state):
    density, normal, first, second, energy = state
    inv = inverse(density)
    speed = normal * inv
    kinetic = 0.5 * (normal * normal + first * first + second * second) * inv
    pressure = (gamma_ratio - 1.0) * (energy - kinetic)
    square = gamma_ratio * pressure * inv
    wave = jnp.abs(speed) + square * lax.rsqrt(square)
    flux = (normal, normal * speed + pressure, first * speed, second * speed, (energy + pressure) * speed)
    return flux, wave


def interface_terms(left, right):
    (state_l, flux_l, wave_l), (state_r, flux_r, wave_r) = left, right
    return (
        [r - l for l, r in zip(state_l, state_r)]
        + [r - l for l, r in zip(flux_l, flux_r)]
        + [r + l for l, r in zip(state_l, state_r)]
        + [r + l for l, r in zip(flux_l, flux_r)]
        + [jnp.maximum(wave_l, wave_r)]
    )


def weno_terms(d0, d1, d2, d3, epsilon):
    e0 = d1 - d0
    e1 = d2 - d1
    e2 = d3 - d2
    t1 = 0.75 * d1
    t2 = 0.75 * d2
    q1 = t1 * d1 + epsilon
    q2 = t2 * d2 + epsilon
    low = (e0 + t1) * e0 + q1
    mid = (e1 + t1) * e1 + q1
    high = (e2 - t2) * e2 + q2
    x = mid * pl.reciprocal(low, approx=True)
    y = mid * pl.reciprocal(high, approx=True)
    weight_low = x * x
    weight_high = 1.5 * (y * y)
    total = 0.5 * weight_low + (weight_high + 3.0)
    return (weight_low * (e0 - e1) + weight_high * (e1 - e2)) * pl.reciprocal(total, approx=True)


def face_terms(diff_state, diff_flux, sum_state, sum_flux, wave):
    inv = inverse(sum_state[0])
    un, va, vb, specific = (inv * part for part in sum_state[1:])
    half = 0.5 * (un * un + va * va + vb * vb)
    internal = specific - half
    square = gamma_ratio * (gamma_ratio - 1.0) * internal
    inv_sound = lax.rsqrt(square)
    sound = square * inv_sound
    factor = (gamma_ratio - 1.0) * inv_sound * inv_sound
    enthalpy = specific + (gamma_ratio - 1.0) * internal

    def project(dens, norm, first, second, energy):
        sn = norm - un * dens
        sa = first - va * dens
        sb = second - vb * dens
        even = factor * (energy - half * dens - un * sn - va * sa - vb * sb)
        odd = inv_sound * sn
        return even - odd, dens - even, sa, sb, even + odd

    damped = [[wave * part for part in parts] for parts in diff_state]
    plus = [project(*(f + d for f, d in zip(diff_flux[s], damped[s]))) for s in range(4)]
    minus = [project(*(f - d for f, d in zip(diff_flux[s], damped[s]))) for s in range(1, 5)]
    fields = []
    for k in range(5):
        epsilon = weno_epsilon * (12.0 if k in (0, 4) else 3.0)
        p0, p1, p2, p3 = (plus[s][k] for s in range(4))
        m1, m2, m3, m4 = (minus[s][k] for s in range(4))
        linear = (p1 - m3) + 2.0 * (p2 - m2)
        fields.append(linear + weno_terms(p0, p1, p2, p3, epsilon) - weno_terms(m4, m3, m2, m1, epsilon))
    wave_minus, entropy, sa, sb, wave_plus = fields
    even = 0.5 * (wave_plus + wave_minus)
    odd = sound * (0.5 * (wave_plus - wave_minus))
    carried = even + entropy
    central = [0.5 * flux_scale * (f - d) for f, d in zip(sum_flux, damped[2])]
    return (
        central[0] + carried,
        central[1] + un * carried + odd,
        central[2] + va * carried + sa,
        central[3] + vb * carried + sb,
        central[4] + enthalpy * even + un * odd + half * entropy + va * sa + vb * sb,
    )


def with_terms(state):
    return (state, *cell_terms(state))


def lane_index(shape):
    return lax.broadcasted_iota(jnp.int32, shape, len(shape) - 1)


def pack_kernel(section, theta_low, theta_high, radial_low, radial_high, rows):
    planes, bands, width = section.shape[1:]
    tiles = width // lanes
    lane = lane_index((bands, lanes))
    for c in range(5):
        first = jnp.zeros((bands, lanes), jnp.float32)
        last = jnp.zeros((bands, lanes), jnp.float32)
        for p in range(planes):
            here = (lane >= group * p) & (lane < group * p + ghosts)
            head = section[c, p, :, 0:lanes]
            tail = section[c, p, :, width - lanes : width]
            first = jnp.where(here, pltpu.roll(head, group * p, 1) if p else head, first)
            last = jnp.where(here, pltpu.roll(tail, group * p + ghosts, 1), last)
        theta_low[c] = first
        theta_high[c] = last
    for c in range(5):

        def plane(p, carry):
            for j in range(tiles):
                rows[j * bands : (j + 1) * bands] = section[c, p, :, j * lanes : (j + 1) * lanes]
            for k in range(ghosts):
                radial_low[c, p, k] = rows[pl.ds(k, tiles, stride=bands)]
                radial_high[c, p, k] = rows[pl.ds(bands - ghosts + k, tiles, stride=bands)]
            return carry

        lax.fori_loop(0, planes, plane, 0)


def pack(section):
    _, planes, bands, width = section.shape
    tiles = width // lanes
    theta = jax.ShapeDtypeStruct((5, bands, lanes), jnp.float32)
    radial = jax.ShapeDtypeStruct((5, planes, ghosts, tiles, lanes), jnp.float32)
    return pl.pallas_call(
        pack_kernel,
        out_shape=(theta, theta, radial, radial),
        scratch_shapes=[pltpu.VMEM((bands * tiles, lanes), jnp.float32)],
        compiler_params=pltpu.CompilerParams(vmem_limit_bytes=vmem_bytes),
        name="pack",
    )(section)


batch = 2


def main_kernel(
    ids, section, own_low, left_high, right_low, low_radial, high_radial, acc, rows, turned, terms, side, strip
):
    planes, bands, width = section.shape[1:]
    tiles = width // lanes
    radial_pass(ids, section, low_radial, high_radial, rows, turned, terms)
    theta_pass(section, own_low, left_high, right_low, acc, rows, terms, side, strip)
    axial_inner(ids, section, acc, terms)


def radial_pass(ids, section, low_radial, high_radial, rows, turned, terms):
    planes, bands, width = section.shape[1:]
    tiles = width // lanes
    at_inner = ids[1] == 0
    at_outer = ids[1] == ids[2] - 1

    def spread(p, carry):
        for c in range(5):
            for j in range(tiles):
                rows[c, p, j * bands : (j + 1) * bands] = section[c, p, :, j * lanes : (j + 1) * lanes]
            for r in range(bands):
                turned[c, r + ghosts, p] = rows[c, p, pl.ds(r, tiles, stride=bands)]
            sign = -1.0 if c == 3 else 1.0
            for k in range(ghosts):
                wall_low = sign * rows[c, p, pl.ds(ghosts - 1 - k, tiles, stride=bands)]
                wall_high = sign * rows[c, p, pl.ds(bands - 1 - k, tiles, stride=bands)]
                turned[c, k, p] = jnp.where(at_inner, wall_low, low_radial[c, p, k])
                turned[c, bands + ghosts + k, p] = jnp.where(at_outer, wall_high, high_radial[c, p, k])
        return carry

    lax.fori_loop(0, planes, spread, 0)

    def pair(g, carry):
        p = g * batch

        def cell(r):
            return with_terms([turned[c, r, pl.ds(p, batch)] for c in radial_order])

        def interface(r, left):
            right = cell(r + 1)
            for n, value in enumerate(interface_terms(left, right)):
                terms[n, r] = value
            return right

        lax.fori_loop(0, bands + 2 * ghosts - 1, interface, cell(0))

        def face(r, before):
            flux = face_at(terms, r)
            for c, now, old in zip(radial_order, flux, before):

                @pl.when(r > 0)
                def _():
                    change = now - old
                    for b in range(batch):
                        rows[c, p + b, pl.ds(r - 1, tiles, stride=bands)] = change[b]

            return flux

        zero = tuple(jnp.zeros((batch, tiles, lanes), jnp.float32) for _ in range(5))
        lax.fori_loop(0, bands + 1, face, zero)
        return carry

    lax.fori_loop(0, planes // batch, pair, 0)


def face_at(terms, first):
    load = lambda n, r: terms[n, first + r]
    return face_terms(
        [[load(c, s) for c in range(5)] for s in range(5)],
        [[load(5 + c, s) for c in range(5)] for s in range(5)],
        [load(10 + c, 2) for c in range(5)],
        [load(15 + c, 2) for c in range(5)],
        load(20, 2),
    )


def shifted(before, here, after, shift, lane):
    if shift == 0:
        return here
    axis = here.ndim - 1
    if shift > 0:
        return pltpu.roll(jnp.where(lane < shift, after, here), lanes - shift, axis)
    return pltpu.roll(jnp.where(lane >= lanes + shift, before, here), -shift, axis)


def theta_pass(section, own_low, left_high, right_low, acc, rows, terms, side, strip):
    planes, bands, width = section.shape[1:]
    tiles = width // lanes
    lane = lane_index((bands, lanes))
    within = lane % group
    ends = with_terms(
        [jnp.where(within < ghosts, left_high[c], pltpu.roll(own_low[c], ghosts, 1)) for c in theta_order]
    )
    turn = lambda value: pltpu.roll(value, lanes - 1, 1)
    after = ([turn(v) for v in ends[0]], [turn(v) for v in ends[1]], turn(ends[2]))
    edge = interface_terms(ends, after)
    at = lambda n, s: edge[n] if s == 2 else pltpu.roll(edge[n], (2 - s) % lanes, 1)
    corner = face_terms(
        [[at(c, s) for c in range(5)] for s in range(5)],
        [[at(5 + c, s) for c in range(5)] for s in range(5)],
        [at(10 + c, 2) for c in range(5)],
        [at(15 + c, 2) for c in range(5)],
        at(20, 2),
    )
    for n, c in enumerate(theta_order):
        for p in range(planes):
            side[n, p] = pltpu.roll(corner[n], (lanes - 1 - (group * p + 2)) % lanes, 1)
            strip[n, 0, p] = pltpu.roll(left_high[c], (lanes - ghosts - group * p) % lanes, 1)
            strip[n, 1, p] = pltpu.roll(right_low[c], (-group * p) % lanes, 1)
    lane = lane_index((batch, bands, lanes))

    def pair(g, carry):
        p = g * batch

        def tile(t):
            start = pl.multiple_of(t * lanes, lanes)
            return [section[c, pl.ds(p, batch), :, pl.ds(start, lanes)] for c in theta_order]

        def store(t, left, right):
            shift = lambda a, b: shifted(None, a, b, 1, lane)
            moved = (
                [shift(a, b) for a, b in zip(left[0], right[0])],
                [shift(a, b) for a, b in zip(left[1], right[1])],
                shift(left[2], right[2]),
            )
            for n, value in enumerate(interface_terms(left, moved)):
                terms[n, t] = value

        def interface(t, left):
            right = with_terms(tile(t))
            store(t, left, right)
            return right

        low = with_terms([strip[n, 0, pl.ds(p, batch)] for n in range(5)])
        high = with_terms([strip[n, 1, pl.ds(p, batch)] for n in range(5)])
        last = lax.fori_loop(0, tiles, interface, low)
        store(tiles, last, high)
        store(tiles + 1, high, high)

        def face(t, before):
            def at(n, s):
                here = terms[n, t + 1]
                if s < 2:
                    return shifted(terms[n, t], here, None, s - 2, lane)
                return shifted(None, here, terms[n, t + 2] if s > 2 else None, s - 2, lane)

            flux = face_terms(
                [[at(c, s) for c in range(5)] for s in range(5)],
                [[at(5 + c, s) for c in range(5)] for s in range(5)],
                [at(10 + c, 2) for c in range(5)],
                [at(15 + c, 2) for c in range(5)],
                at(20, 2),
            )
            start = pl.multiple_of(t * lanes, lanes)
            row = pl.multiple_of(t * bands, bands)
            for c, now, old in zip(theta_order, flux, before):
                change = now - shifted(old, now, None, -1, lane)
                other = rows[c, pl.ds(p, batch), pl.ds(row, bands)]
                acc[c, pl.ds(p + 1, batch), :, pl.ds(start, lanes)] = change + other
            return flux

        lax.fori_loop(0, tiles, face, tuple(side[n, pl.ds(p, batch)] for n in range(5)))
        return carry

    lax.fori_loop(0, planes // batch, pair, 0)


def axial_faces(get, count, first, acc, terms, width):
    step = batch * lanes

    def columns(g, carry):
        start = pl.multiple_of(g * step, step)

        def cell(i):
            return with_terms([get(c, i, start) for c in axial_order])

        def interface(i, left):
            right = cell(i + 1)
            for n, value in enumerate(interface_terms(left, right)):
                for b in range(batch):
                    terms[n, i, b] = value[:, b * lanes : (b + 1) * lanes]
            return right

        lax.fori_loop(0, count + 4, interface, cell(0))

        def face(i, carry):
            flux = face_at(terms, i)
            for c, value in zip(axial_order, flux):
                for b in range(batch):
                    place = pl.ds(pl.multiple_of(start + b * lanes, lanes), lanes)
                    acc[c, first + i, :, place] += value[b]
                    acc[c, first + i + 1, :, place] -= value[b]
            return carry

        lax.fori_loop(0, count, face, 0)
        return carry

    lax.fori_loop(0, width // step, columns, 0)


def axial_inner(ids, section, acc, terms):
    planes, bands, width = section.shape[1:]
    first = jnp.where(ids[0] == 0, 0, ghosts)
    for c in range(5):
        acc[c, 0] = jnp.zeros((bands, width), jnp.float32)
        acc[c, planes + 1] = jnp.zeros((bands, width), jnp.float32)

    def get(c, i, start):
        plane = jnp.clip(first + i - ghosts, 0, planes - 1)
        return section[c, plane, :, pl.ds(start, batch * lanes)]

    axial_faces(get, planes + 1 - ghosts, first, acc, terms, width)


def main(ids, section, own_low, left_high, right_low, low_radial, high_radial):
    _, planes, bands, width = section.shape
    tiles = width // lanes
    depth = max(bands + 2 * ghosts, tiles + 2, planes + 2 * ghosts)
    vmem = pl.BlockSpec(memory_space=pltpu.VMEM)
    faces = (planes + 1) * tiles + planes * (tiles + bands + 1)
    return pl.pallas_call(
        main_kernel,
        in_specs=[pl.BlockSpec(memory_space=pltpu.SMEM)] + [vmem] * 6,
        out_shape=jax.ShapeDtypeStruct((5, planes + 2, bands, width), jnp.float32),
        scratch_shapes=[
            pltpu.VMEM((5, planes, bands * tiles, lanes), jnp.float32),
            pltpu.VMEM((5, bands + 2 * ghosts, planes, tiles, lanes), jnp.float32),
            pltpu.VMEM((21, depth, batch, 8, lanes), jnp.float32),
            pltpu.VMEM((5, planes, bands, lanes), jnp.float32),
            pltpu.VMEM((5, 2, planes, bands, lanes), jnp.float32),
        ],
        compiler_params=pltpu.CompilerParams(vmem_limit_bytes=vmem_bytes),
        cost_estimate=pl.CostEstimate(
            flops=faces * 8 * lanes * 700, bytes_accessed=section.size * 16, transcendentals=faces * 8 * lanes * 30
        ),
        name="inner",
    )(ids, section, own_low, left_high, right_low, low_radial, high_radial)


def tail_kernel(ids, section, base, acc, ghost, out, padded, total, terms):
    planes, bands, width = section.shape[1:]
    front = ids[0] == 0
    kept = planes - 1
    own = jnp.where(front, 1, 0)
    own_at = jnp.where(front, 0, ghosts)
    ghost_at = jnp.where(front, kept, 0)
    first = jnp.where(front, planes + 1 - ghosts, 0)
    for c in range(5):

        def copy_plane(i, carry):
            padded[c, own_at + i] = section[c, own + i]
            return carry

        lax.fori_loop(0, kept, copy_plane, 0)

        def copy_ghost(i, carry):
            padded[c, ghost_at + i] = ghost[c, i]
            return carry

        lax.fori_loop(0, ghosts, copy_ghost, 0)

        def copy_total(i, carry):
            total[c, i] = acc[c, i]
            return carry

        lax.fori_loop(0, planes + 2, copy_total, 0)

    def get(c, i, start):
        return padded[c, i, :, pl.ds(start, batch * lanes)]

    axial_faces(get, ghosts, first, total, terms, width)
    for c in range(5):

        def update(p, carry):
            change = (-0.25 * step_ratio / flux_scale) * total[c, p + 1]
            out[c, p] = 0.75 * base[c, p] + (0.25 * section[c, p] + change)
            return carry

        lax.fori_loop(0, planes, update, 0)


def tail(ids, section, base, acc, ghost):
    _, planes, bands, width = section.shape
    vmem = pl.BlockSpec(memory_space=pltpu.VMEM)
    return pl.pallas_call(
        tail_kernel,
        in_specs=[pl.BlockSpec(memory_space=pltpu.SMEM)] + [vmem] * 4,
        out_shape=jax.ShapeDtypeStruct(section.shape, jnp.float32),
        scratch_shapes=[
            pltpu.VMEM((5, planes - 1 + ghosts, bands, width), jnp.float32),
            pltpu.VMEM((5, planes + 2, bands, width), jnp.float32),
            pltpu.VMEM((21, 2 * ghosts + 1, batch, 8, lanes), jnp.float32),
        ],
        compiler_params=pltpu.CompilerParams(vmem_limit_bytes=vmem_bytes),
        name="tail",
    )(ids, section, base, acc, ghost)


def mortar_ghost(section, rotor_step, block_index):
    width = section.shape[3]
    offset = rotor_step[0] // 4
    fraction = (rotor_step[0] % 4).astype(jnp.float32) / 4.0
    outgoing = jnp.where(block_index == 0, section[:, -ghosts:], section[:, :ghosts])
    slab_count = lax.axis_size("theta")
    slab_index = lax.axis_index("theta")
    turns = offset // width
    facing = lax.ppermute(outgoing, "blk", [(0, 1), (1, 0)])
    whole = lax.all_gather(facing, "theta", axis=3, tiled=True)
    doubled = jnp.concatenate([whole, whole], axis=3)
    start = (turns - 1 - slab_index) % slab_count * width
    window = lax.dynamic_slice_in_dim(doubled, start, 2 * width, 3)
    reversed_window = window[..., ::-1]
    remainder = offset % width
    low_part = lax.dynamic_slice_in_dim(reversed_window, width - remainder, width, 3)
    high_part = lax.dynamic_slice_in_dim(reversed_window, width - remainder - 1, width, 3)
    ghost = (1.0 - fraction) * low_part + fraction * high_part
    return jnp.concatenate([ghost[:2], -ghost[2:3], ghost[3:]], axis=0)


def shards(base_state, section_state, rotor_step):
    block_index = lax.axis_index("blk")
    slab_count = lax.axis_size("theta")
    band_count = lax.axis_size("radial")
    ids = jnp.stack([block_index, lax.axis_index("radial"), band_count]).astype(jnp.int32)
    ghost = mortar_ghost(section_state, rotor_step, block_index)
    theta_low, theta_high, radial_low, radial_high = pack(section_state)
    up = [(i, (i + 1) % slab_count) for i in range(slab_count)]
    down = [((i + 1) % slab_count, i) for i in range(slab_count)]
    left_high = lax.ppermute(theta_high, "theta", up)
    right_low = lax.ppermute(theta_low, "theta", down)
    low_radial = lax.ppermute(radial_high, "radial", [(i, i + 1) for i in range(band_count - 1)])
    high_radial = lax.ppermute(radial_low, "radial", [(i + 1, i) for i in range(band_count - 1)])
    acc = main(ids, section_state, theta_low, left_high, right_low, low_radial, high_radial)
    return tail(ids, section_state, base_state, acc, ghost)


def solution(mesh):
    in_specs = (P(None, "blk", "radial", "theta"), P(None, "blk", "radial", "theta"), P())
    out_specs = P(None, "blk", "radial", "theta")
    return jax.shard_map(shards, mesh=mesh, in_specs=in_specs, out_specs=out_specs, check_vma=False)
```

```python
import functools

import jax
import jax.numpy as jnp
from jax import lax
from jax.experimental import pallas as pl
from jax.experimental.pallas import tpu as pltpu
from jax.sharding import PartitionSpec as P

gamma_ratio = 1.4
weno_epsilon = 1e-06
step_ratio = 0.12
lanes = 128
ghosts = 3
group = 16
flux_scale = 12.0
chunk = 256
most_slabs = 8
vmem_bytes = 48 * 1024 * 1024

axial_order = (0, 1, 2, 3, 4)
radial_order = (0, 3, 1, 2, 4)
theta_order = (0, 2, 1, 3, 4)


def inverse(value):
    guess = pl.reciprocal(value, approx=True)
    return guess * (2.0 - value * guess)


def cell_terms(state):
    density, normal, first, second, energy = state
    inv = inverse(density)
    speed = normal * inv
    kinetic = 0.5 * (normal * normal + first * first + second * second) * inv
    pressure = (gamma_ratio - 1.0) * (energy - kinetic)
    square = gamma_ratio * pressure * inv
    wave = jnp.abs(speed) + square * lax.rsqrt(square)
    flux = (normal, normal * speed + pressure, first * speed, second * speed, (energy + pressure) * speed)
    return flux, wave


def interface_terms(left, right):
    (state_l, flux_l, wave_l), (state_r, flux_r, wave_r) = left, right
    return (
        [r - l for l, r in zip(state_l, state_r)]
        + [r - l for l, r in zip(flux_l, flux_r)]
        + [r + l for l, r in zip(state_l, state_r)]
        + [0.5 * flux_scale * (r + l) for l, r in zip(flux_l, flux_r)]
        + [jnp.maximum(wave_l, wave_r)]
    )


def weno_terms(d0, d1, d2, d3, epsilon):
    e0 = d1 - d0
    e1 = d2 - d1
    e2 = d3 - d2
    f0 = e0 - e1
    f1 = e1 - e2
    t1 = 0.75 * d1
    t2 = 0.75 * d2
    shared = t1 * d2 + epsilon
    low = e0 * e0 + (t1 * f0 + shared)
    mid = e1 * e1 + shared
    high = e2 * e2 + (t2 * f1 + shared)
    x = mid * pl.reciprocal(low, approx=True)
    y = mid * pl.reciprocal(high, approx=True)
    weight_low = x * x
    weight_high = 1.5 * (y * y)
    total = 0.5 * weight_low + (weight_high + 3.0)
    return (weight_low * f0 + weight_high * f1) * pl.reciprocal(total, approx=True)


def face_terms(diff_state, diff_flux, sum_state, sum_flux, wave):
    inv = inverse(sum_state(0))
    un, va, vb, specific = (inv * sum_state(k) for k in range(1, 5))
    half = 0.5 * (un * un + va * va + vb * vb)
    internal = specific - half
    square = gamma_ratio * (gamma_ratio - 1.0) * internal
    inv_sound = lax.rsqrt(square)
    sound = square * inv_sound
    factor = (gamma_ratio - 1.0) * inv_sound * inv_sound
    enthalpy = specific + (gamma_ratio - 1.0) * internal

    def project(dens, norm, first, second, energy):
        sn = norm - un * dens
        sa = first - va * dens
        sb = second - vb * dens
        even = factor * (energy - half * dens - un * sn - va * sa - vb * sb)
        odd = inv_sound * sn
        return even - odd, dens - even, sa, sb, even + odd

    def side(vectors):
        chars = [project(*vector) for vector in vectors]
        return [weno_terms(*(c[k] for c in chars), weno_epsilon * (12.0 if k in (0, 4) else 3.0)) for k in range(5)]

    plus = [[diff_flux[s](c) + wave * diff_state[s](c) for c in range(5)] for s in range(4)]
    forward = side(plus)
    minus = [[diff_flux[s](c) - wave * diff_state[s](c) for c in range(5)] for s in range(4, 0, -1)]
    backward = side(minus)
    central = [sum_flux(c) + (plus[1][c] - plus[2][c]) + (minus[2][c] - minus[1][c]) for c in range(5)]
    wave_minus, entropy, sa, sb, wave_plus = (f - b for f, b in zip(forward, backward))
    even = 0.5 * (wave_plus + wave_minus)
    odd = sound * (0.5 * (wave_plus - wave_minus))
    carried = even + entropy
    return (
        central[0] + carried,
        central[1] + un * carried + odd,
        central[2] + va * carried + sa,
        central[3] + vb * carried + sb,
        central[4] + enthalpy * even + un * odd + half * entropy + va * sa + vb * sb,
    )


def face_from(load):
    return face_terms(
        [functools.partial(lambda s, c: load(c, s), s) for s in range(5)],
        [functools.partial(lambda s, c: load(5 + c, s), s) for s in range(5)],
        lambda c: load(10 + c, 2),
        lambda c: load(15 + c, 2),
        load(20, 2),
    )


def with_terms(state):
    return (state, *cell_terms(state))


def lane_index(shape):
    return lax.broadcasted_iota(jnp.int32, shape, len(shape) - 1)


def pack_kernel(ids, section, theta_low, theta_high, radial_low, radial_high, near, far, rows):
    planes, bands, width = section.shape[1:]
    tiles = width // lanes
    facing = jnp.where(ids[0] == 0, planes - ghosts, 0)
    for c in range(5):
        for i in range(ghosts):
            near[c, i] = section[c, facing + i, :, width - near.shape[3] :]
            far[c, i] = section[c, facing + i, :, : far.shape[3]]
    lane = lane_index((bands, lanes))
    for c in range(5):
        first = jnp.zeros((bands, lanes), jnp.float32)
        last = jnp.zeros((bands, lanes), jnp.float32)
        for p in range(planes):
            here = (lane >= group * p) & (lane < group * p + ghosts)
            head = section[c, p, :, 0:lanes]
            tail = section[c, p, :, width - lanes : width]
            first = jnp.where(here, pltpu.roll(head, group * p, 1) if p else head, first)
            last = jnp.where(here, pltpu.roll(tail, group * p + ghosts, 1), last)
        theta_low[c] = first
        theta_high[c] = last
    for c in range(5):

        def plane(p, carry):
            for j in range(tiles):
                rows[j * bands : (j + 1) * bands] = section[c, p, :, j * lanes : (j + 1) * lanes]
            for k in range(ghosts):
                radial_low[c, p, k] = rows[pl.ds(k, tiles, stride=bands)]
                radial_high[c, p, k] = rows[pl.ds(bands - ghosts + k, tiles, stride=bands)]
            return carry

        lax.fori_loop(0, planes, plane, 0)


def pack(ids, section, near, far):
    _, planes, bands, width = section.shape
    tiles = width // lanes
    vmem = pl.BlockSpec(memory_space=pltpu.VMEM)
    array = lambda *shape: jax.ShapeDtypeStruct(shape, jnp.float32)
    theta = array(5, bands, lanes)
    radial = array(5, planes, ghosts, tiles, lanes)
    mortar = [array(5, ghosts, bands, part) for part in (near, far)]
    return pl.pallas_call(
        pack_kernel,
        in_specs=[pl.BlockSpec(memory_space=pltpu.SMEM), vmem],
        out_shape=(theta, theta, radial, radial, *mortar),
        scratch_shapes=[pltpu.VMEM((bands * tiles, lanes), jnp.float32)],
        compiler_params=pltpu.CompilerParams(vmem_limit_bytes=vmem_bytes),
        name="pack",
    )(ids, section)


batch = 2


def main_kernel(
    ids, section, own_low, left_high, right_low, low_radial, high_radial, acc, rows, turned, terms, moved, side, turns
):
    radial_pass(ids, section, low_radial, high_radial, rows, turned, terms)
    theta_pass(section, own_low, left_high, right_low, acc, rows, terms, moved, side, turns)
    axial_inner(ids, section, acc, terms)


def radial_pass(ids, section, low_radial, high_radial, rows, turned, terms):
    planes, bands, width = section.shape[1:]
    tiles = width // lanes
    at_inner = ids[1] == 0
    at_outer = ids[1] == ids[2] - 1

    def spread(p, carry):
        for c in range(5):
            for j in range(tiles):
                rows[c, p, j * bands : (j + 1) * bands] = section[c, p, :, j * lanes : (j + 1) * lanes]
            for r in range(bands):
                turned[c, r + ghosts, p] = rows[c, p, pl.ds(r, tiles, stride=bands)]
            sign = -1.0 if c == 3 else 1.0
            for k in range(ghosts):
                wall_low = sign * rows[c, p, pl.ds(ghosts - 1 - k, tiles, stride=bands)]
                wall_high = sign * rows[c, p, pl.ds(bands - 1 - k, tiles, stride=bands)]
                turned[c, k, p] = jnp.where(at_inner, wall_low, low_radial[c, p, k])
                turned[c, bands + ghosts + k, p] = jnp.where(at_outer, wall_high, high_radial[c, p, k])
        return carry

    lax.fori_loop(0, planes, spread, 0)

    def interface(r, carry):
        left = with_terms([turned[c, r] for c in radial_order])
        right = with_terms([turned[c, r + 1] for c in radial_order])
        for n, value in enumerate(interface_terms(left, right)):
            terms[n, r, 0:value.shape[0]] = value
        return carry

    lax.fori_loop(0, bands + 2 * ghosts - 1, interface, 0)

    def pair(g, carry):
        p = g * batch

        def face(r, before):
            flux = face_from(lambda n, s: terms[n, r + s, pl.ds(p, batch)])
            for c, now, old in zip(radial_order, flux, before):
                change = now - old

                @pl.when(r > 0)
                def _():
                    for b in range(batch):
                        rows[c, p + b, pl.ds(r - 1, tiles, stride=bands)] = change[b]

            return flux

        zero = tuple(jnp.zeros((batch, tiles, lanes), jnp.float32) for _ in range(5))
        lax.fori_loop(0, bands + 1, face, zero)
        return carry

    lax.fori_loop(0, planes // batch, pair, 0)


def turn_matrix(shifts):
    rows = lax.broadcasted_iota(jnp.int32, (2 * lanes, len(shifts) * lanes), 0) % lanes
    columns = lax.broadcasted_iota(jnp.int32, (2 * lanes, len(shifts) * lanes), 1)
    source = columns % lanes
    for k, shift in enumerate(shifts):
        source = jnp.where(columns // lanes == k, (columns + shift) % lanes, source)
    return jnp.where(rows == source, 1.0, 0.0).astype(jnp.bfloat16)


def turned_tiles(values, matrix):
    shape = values[0].shape
    flat = jnp.concatenate([v.reshape(-1, lanes) for v in values], axis=0)
    high = flat.astype(jnp.bfloat16)
    low = (flat - high.astype(jnp.float32)).astype(jnp.bfloat16)
    both = jnp.dot(jnp.concatenate([high, low], axis=1), matrix, preferred_element_type=jnp.float32)
    count = flat.shape[0] // len(values)
    return [
        [both[n * count : (n + 1) * count, k * lanes : (k + 1) * lanes].reshape(shape) for n in range(len(values))]
        for k in range(matrix.shape[1] // lanes)
    ]


face_shifts = (-2, -1, 1, 2)


def theta_pass(section, own_low, left_high, right_low, acc, rows, terms, moved, side, turns):
    planes, bands, width = section.shape[1:]
    tiles = width // lanes
    lane = lane_index((bands, lanes))
    within = lane % group
    ends = with_terms(
        [jnp.where(within < ghosts, left_high[c], pltpu.roll(own_low[c], ghosts, 1)) for c in theta_order]
    )
    turn = lambda value: pltpu.roll(value, lanes - 1, 1)
    after = ([turn(v) for v in ends[0]], [turn(v) for v in ends[1]], turn(ends[2]))
    edge = interface_terms(ends, after)
    corner = face_from(lambda n, s: edge[n] if s == 2 else pltpu.roll(edge[n], (2 - s) % lanes, 1))
    for n in range(5):
        for p in range(planes):
            side[n, p] = pltpu.roll(corner[n], (lanes - 1 - (group * p + 2)) % lanes, 1)
    lane = lane_index((planes, bands, lanes))
    turns[...] = turn_matrix(face_shifts)

    def spread(value, start):
        return jnp.stack([pltpu.roll(value, (start - group * p) % lanes, 1) for p in range(planes)])

    def tile(t):
        return [section[c, :, :, pl.ds(pl.multiple_of(t * lanes, lanes), lanes)] for c in theta_order]

    def store(t, left, right):
        joined = [jnp.where(lane < 1, r, l) for l, r in zip(left, right)]
        (moved_on,) = turned_tiles(joined, turns[:, 2 * lanes : 3 * lanes])
        values = interface_terms(with_terms(left), with_terms(moved_on))
        for n, value in enumerate(values):
            terms[n, t, 0:planes] = value
        for k, parts in enumerate(turned_tiles(values[:10], turns[...])):
            for n, part in enumerate(parts):
                moved[k, n, t] = part

    def interface(t, carry):
        store(t + 1, tile(t), tile(t + 1))
        return carry

    low = [spread(left_high[c], lanes - ghosts) for c in theta_order]
    high = [spread(right_low[c], 0) for c in theta_order]
    low = [jnp.where(lane >= lanes - ghosts, v, 1.0) for v in low]
    high = [jnp.where(lane < ghosts, v, 1.0) for v in high]
    store(0, low, tile(0))
    lax.fori_loop(0, tiles - 1, interface, 0)
    store(tiles, tile(tiles - 1), high)
    store(tiles + 1, high, high)
    lane = lane_index((batch, bands, lanes))

    def pair(g, carry):
        p = g * batch

        def face(t, before):
            def load(n, s):
                if s == 2:
                    return terms[n, t + 1, pl.ds(p, batch)]
                k = s if s < 2 else s - 1
                here = moved[k, n, t + 1, pl.ds(p, batch)]
                if s < 2:
                    return jnp.where(lane < 2 - s, moved[k, n, t, pl.ds(p, batch)], here)
                return jnp.where(lane >= lanes + 2 - s, moved[k, n, t + 2, pl.ds(p, batch)], here)

            flux = face_from(load)
            start = pl.multiple_of(t * lanes, lanes)
            row = pl.multiple_of(t * bands, bands)
            for c, now, old in zip(theta_order, flux, before):
                change = now - pltpu.roll(jnp.where(lane >= lanes - 1, old, now), 1, 2)
                other = rows[c, pl.ds(p, batch), pl.ds(row, bands)]
                acc[c, pl.ds(p + 1, batch), :, pl.ds(start, lanes)] = change + other
            return flux

        lax.fori_loop(0, tiles, face, tuple(side[n, pl.ds(p, batch)] for n in range(5)))
        return carry

    lax.fori_loop(0, planes // batch, pair, 0)


def axial_interfaces(left, right, i, terms):
    for n, value in enumerate(interface_terms(left, right)):
        for b in range(value.shape[1] // lanes):
            terms[n, i, b] = value[:, b * lanes : (b + 1) * lanes]


def axial_faces(count, first, acc, terms, width):
    def columns(g, carry):
        b0 = g * batch

        def face(i, carry):
            flux = face_from(lambda n, s: terms[n, i + s, pl.ds(b0, batch)])
            for c, value in zip(axial_order, flux):
                for b in range(batch):
                    place = pl.ds(pl.multiple_of((b0 + b) * lanes, lanes), lanes)
                    acc[c, first + i, :, place] += value[b]
                    acc[c, first + i + 1, :, place] -= value[b]
            return carry

        lax.fori_loop(0, count, face, 0)
        return carry

    lax.fori_loop(0, width // (batch * lanes), columns, 0)


def axial_inner(ids, section, acc, terms):
    planes, bands, width = section.shape[1:]
    first = jnp.where(ids[0] == 0, 0, ghosts)
    count = planes + 1 - ghosts
    for c in range(5):
        acc[c, 0] = jnp.zeros((bands, width), jnp.float32)
        acc[c, planes + 1] = jnp.zeros((bands, width), jnp.float32)

    def cell(i):
        plane = jnp.clip(first + i - ghosts, 0, planes - 1)
        return with_terms([section[c, plane] for c in axial_order])

    def interface(i, carry):
        axial_interfaces(cell(i), cell(i + 1), i, terms)
        return carry

    lax.fori_loop(0, count + 4, interface, 0)
    axial_faces(count, first, acc, terms, width)


def main(ids, section, own_low, left_high, right_low, low_radial, high_radial):
    _, planes, bands, width = section.shape
    tiles = width // lanes
    depth = max(bands + 2 * ghosts, tiles + 2, planes + 2 * ghosts)
    vmem = pl.BlockSpec(memory_space=pltpu.VMEM)
    faces = (planes + 1) * tiles + planes * (tiles + bands + 1)
    return pl.pallas_call(
        main_kernel,
        in_specs=[pl.BlockSpec(memory_space=pltpu.SMEM)] + [vmem] * 6,
        out_shape=jax.ShapeDtypeStruct((5, planes + 2, bands, width), jnp.float32),
        scratch_shapes=[
            pltpu.VMEM((5, planes, bands * tiles, lanes), jnp.float32),
            pltpu.VMEM((5, bands + 2 * ghosts, planes, tiles, lanes), jnp.float32),
            pltpu.VMEM((21, depth, max(planes, tiles), 8, lanes), jnp.float32),
            pltpu.VMEM((4, 10, tiles + 2, planes, bands, lanes), jnp.float32),
            pltpu.VMEM((5, planes, bands, lanes), jnp.float32),
            pltpu.VMEM((2 * lanes, len(face_shifts) * lanes), jnp.bfloat16),
        ],
        compiler_params=pltpu.CompilerParams(vmem_limit_bytes=vmem_bytes),
        cost_estimate=pl.CostEstimate(
            flops=faces * 8 * lanes * 700, bytes_accessed=section.size * 16, transcendentals=faces * 8 * lanes * 30
        ),
        name="inner",
    )(ids, section, own_low, left_high, right_low, low_radial, high_radial)


def mortar_planes(turn, near, far, window, write):
    _, _, bands, width = window.shape
    window[:, :, :, : near.shape[3]] = near[...]
    window[:, :, :, near.shape[3] :] = far[...]
    whole_tiles = turn[0] // lanes
    rest = turn[0] % lanes
    fraction = 0.25 * turn[1].astype(jnp.float32)
    source = lax.broadcasted_iota(jnp.int32, (2 * lanes, lanes), 0)
    target = lax.broadcasted_iota(jnp.int32, (2 * lanes, lanes), 1)
    gap = source + target - (lanes - 1 + rest)
    blend = jnp.where(gap == 0, 1.0 - fraction, jnp.where(gap == 1, fraction, 0.0)).astype(jnp.bfloat16)
    blend = jnp.concatenate([blend] * 3, axis=0)
    tiles = (width - chunk) // lanes
    for t in range(tiles):
        start = pl.multiple_of((tiles - 1 - t + whole_tiles) * lanes, lanes)
        cells = window[:, :, :, pl.ds(start, 2 * lanes)].reshape(5 * ghosts * bands, 2 * lanes)
        parts = []
        for _ in range(3):
            part = cells.astype(jnp.bfloat16)
            parts.append(part)
            cells = cells - part.astype(jnp.float32)
        mixed = jnp.dot(jnp.concatenate(parts, axis=1), blend, preferred_element_type=jnp.float32)
        mixed = mixed.reshape(5, ghosts, bands, lanes)
        for c in range(5):
            write(c, t, -mixed[c] if c == 2 else mixed[c])


def tail_kernel(ids, turn, section, base, acc, near, far, out, padded, terms, window):
    planes, bands, width = section.shape[1:]
    front = ids[0] == 0
    kept = planes - 1
    own = jnp.where(front, 1, 0)
    own_at = jnp.where(front, 0, ghosts)
    ghost_at = jnp.where(front, kept, 0)
    first = jnp.where(front, planes + 1 - ghosts, 0)
    for c in range(5):
        for i in range(kept):
            padded[c, own_at + i] = section[c, own + i]

    def write(c, t, values):
        padded[c, pl.ds(ghost_at, ghosts), :, t * lanes : (t + 1) * lanes] = values

    mortar_planes(turn, near, far, window, write)

    def cell(i):
        return with_terms([padded[c, i] for c in axial_order])

    def interface(i, carry):
        axial_interfaces(cell(i), cell(i + 1), i, terms)
        return carry

    lax.fori_loop(0, ghosts + 4, interface, 0)
    axial_faces(ghosts, first, acc, terms, width)
    for c in range(5):

        def update(p, carry):
            change = (-0.25 * step_ratio / flux_scale) * acc[c, p + 1]
            out[c, p] = 0.75 * base[c, p] + (0.25 * section[c, p] + change)
            return carry

        lax.fori_loop(0, planes, update, 0)


def tail(ids, turn, section, base, acc, near, far):
    _, planes, bands, width = section.shape
    smem = pl.BlockSpec(memory_space=pltpu.SMEM)
    vmem = pl.BlockSpec(memory_space=pltpu.VMEM)

    def kernel(ids, turn, section, base, acc_in, near, far, out, acc, padded, terms, window, sem):
        copy = pltpu.make_async_copy(acc_in, acc, sem)
        copy.start()
        copy.wait()
        tail_kernel(ids, turn, section, base, acc, near, far, out, padded, terms, window)

    return pl.pallas_call(
        kernel,
        in_specs=[smem, smem, vmem, vmem, pl.BlockSpec(memory_space=pl.ANY), vmem, vmem],
        out_shape=jax.ShapeDtypeStruct(section.shape, jnp.float32),
        scratch_shapes=[
            pltpu.VMEM(acc.shape, jnp.float32),
            pltpu.VMEM((5, planes - 1 + ghosts, bands, width), jnp.float32),
            pltpu.VMEM((21, 2 * ghosts + 1, width // lanes, 8, lanes), jnp.float32),
            pltpu.VMEM((5, ghosts, bands, near.shape[3] + far.shape[3]), jnp.float32),
            pltpu.SemaphoreType.DMA(()),
        ],
        compiler_params=pltpu.CompilerParams(vmem_limit_bytes=vmem_bytes),
        name="tail",
    )(ids, turn, section, base, acc, near, far)


def slab_routes(turns, slabs):
    both = []
    for ahead in (1, 0):
        both.append(
            [
                (block * slabs + slab, (1 - block) * slabs + (turns - ahead - slab) % slabs)
                for block in range(2)
                for slab in range(slabs)
            ]
        )
    return both


def exchange_and_step(ids, turn, base, section, near, far, transfer):
    slabs = lax.axis_size("theta")
    bands = lax.axis_size("radial")
    theta_low, theta_high, radial_low, radial_high, near, far = pack(ids, section, near, far)
    near, far = transfer(near, far)
    low_radial = lax.ppermute(radial_high, "radial", [(i, i + 1) for i in range(bands - 1)])
    high_radial = lax.ppermute(radial_low, "radial", [(i + 1, i) for i in range(bands - 1)])
    left_high = lax.ppermute(theta_high, "theta", [(i, (i + 1) % slabs) for i in range(slabs)])
    right_low = lax.ppermute(theta_low, "theta", [((i + 1) % slabs, i) for i in range(slabs)])
    acc = main(ids, section, theta_low, left_high, right_low, low_radial, high_radial)
    return tail(ids, turn, section, base, acc, near, far)


def shards(base_state, section_state, rotor_step):
    width = section_state.shape[3]
    slabs = lax.axis_size("theta")
    slab = lax.axis_index("theta")
    ids = jnp.stack([lax.axis_index("blk"), lax.axis_index("radial"), lax.axis_size("radial")]).astype(jnp.int32)
    step = rotor_step[0]
    offset = step // 4
    turns = offset // width
    start = offset % width
    cuts = width // chunk
    turn = jnp.stack([start % chunk, step % 4])

    if slabs > most_slabs:

        def gathered(near, far):
            facing = lax.ppermute(far, "blk", [(0, 1), (1, 0)])
            whole = lax.all_gather(facing, "theta", axis=3, tiled=True)
            doubled = jnp.concatenate([whole, whole, whole[..., :chunk]], axis=3)
            begin = (turns - 1 - slab) % slabs * width + start // chunk * chunk
            window = lax.dynamic_slice_in_dim(doubled, begin, width + chunk, 3)
            return window[..., :width], window[..., width:]

        return exchange_and_step(ids, turn, base_state, section_state, chunk, width, gathered)

    def branch(case):
        turned, cut = divmod(case, cuts)
        near_route, far_route = slab_routes(turned, slabs)

        def transfer(near, far):
            return (
                lax.ppermute(near, ("blk", "theta"), near_route),
                lax.ppermute(far, ("blk", "theta"), far_route),
            )

        def run(ids, turn, base, section):
            return exchange_and_step(
                ids, turn, base, section, width - cut * chunk, (cut + 1) * chunk, transfer
            )

        return run

    case = turns * cuts + start // chunk
    return lax.switch(case, [branch(i) for i in range(slabs * cuts)], ids, turn, base_state, section_state)


def solution(mesh):
    in_specs = (P(None, "blk", "radial", "theta"), P(None, "blk", "radial", "theta"), P())
    out_specs = P(None, "blk", "radial", "theta")
    return jax.shard_map(shards, mesh=mesh, in_specs=in_specs, out_specs=out_specs, check_vma=False)
```

```python
import functools

import jax
import jax.numpy as jnp
import numpy as np
from jax import lax
from jax.experimental import pallas as pl
from jax.experimental.pallas import tpu as pltpu
from jax.sharding import PartitionSpec as P

gamma_ratio = 1.4
weno_epsilon = 1e-06
step_ratio = 0.12
lanes = 128
ghosts = 3
group = 16
flux_scale = 12.0
chunk = 512
most_slabs = 8
vmem_bytes = 48 * 1024 * 1024

axial_order = (0, 1, 2, 3, 4)
radial_order = (0, 3, 1, 2, 4)
theta_order = (0, 2, 1, 3, 4)


def inverse(value):
    guess = pl.reciprocal(value, approx=True)
    return guess * (2.0 - value * guess)


def cell_terms(state):
    density, normal, first, second, energy = state
    inv = inverse(density)
    speed = normal * inv
    kinetic = 0.5 * (normal * normal + first * first + second * second) * inv
    pressure = (gamma_ratio - 1.0) * (energy - kinetic)
    square = gamma_ratio * pressure * inv
    wave = jnp.abs(speed) + square * lax.rsqrt(square)
    flux = (normal, normal * speed + pressure, first * speed, second * speed, (energy + pressure) * speed)
    return flux, wave


def interface_terms(left, right):
    (state_l, flux_l, wave_l), (state_r, flux_r, wave_r) = left, right
    return (
        [r - l for l, r in zip(state_l, state_r)]
        + [r - l for l, r in zip(flux_l, flux_r)]
        + [0.5 * flux_scale * (r + l) for l, r in zip(flux_l, flux_r)]
        + [jnp.maximum(wave_l, wave_r)]
    )


def weno_terms(d0, d1, d2, d3, epsilon):
    e0 = d1 - d0
    e1 = d2 - d1
    e2 = d3 - d2
    f0 = e0 - e1
    f1 = e1 - e2
    t1 = 0.75 * d1
    t2 = 0.75 * d2
    shared = t1 * d2 + epsilon
    low = e0 * e0 + (t1 * f0 + shared)
    mid = e1 * e1 + shared
    high = e2 * e2 + (t2 * f1 + shared)
    x = mid * pl.reciprocal(low, approx=True)
    y = mid * pl.reciprocal(high, approx=True)
    weight_low = x * x
    weight_high = 1.5 * (y * y)
    total = 0.5 * weight_low + (weight_high + 3.0)
    return (weight_low * f0 + weight_high * f1) * pl.reciprocal(total, approx=True)


def face_terms(diff_state, diff_flux, sum_state, sum_flux, wave):
    inv = inverse(sum_state(0))
    un, va, vb, specific = (inv * sum_state(k) for k in range(1, 5))
    half = 0.5 * (un * un + va * va + vb * vb)
    internal = specific - half
    square = gamma_ratio * (gamma_ratio - 1.0) * internal
    inv_sound = lax.rsqrt(square)
    sound = square * inv_sound
    factor = (gamma_ratio - 1.0) * inv_sound * inv_sound
    enthalpy = specific + (gamma_ratio - 1.0) * internal

    def project(dens, norm, first, second, energy):
        sn = norm - un * dens
        sa = first - va * dens
        sb = second - vb * dens
        even = factor * (energy - half * dens - un * sn - va * sa - vb * sb)
        odd = inv_sound * sn
        return even - odd, dens - even, sa, sb, even + odd

    def side(vectors):
        chars = [project(*vector) for vector in vectors]
        return [weno_terms(*(c[k] for c in chars), weno_epsilon * (12.0 if k in (0, 4) else 3.0)) for k in range(5)]

    plus = [[diff_flux[s](c) + wave * diff_state[s](c) for c in range(5)] for s in range(4)]
    forward = side(plus)
    minus = [[diff_flux[s](c) - wave * diff_state[s](c) for c in range(5)] for s in range(4, 0, -1)]
    backward = side(minus)
    central = [sum_flux(c) + (plus[1][c] - plus[2][c]) + (minus[2][c] - minus[1][c]) for c in range(5)]
    wave_minus, entropy, sa, sb, wave_plus = (f - b for f, b in zip(forward, backward))
    even = 0.5 * (wave_plus + wave_minus)
    odd = sound * (0.5 * (wave_plus - wave_minus))
    carried = even + entropy
    return (
        central[0] + carried,
        central[1] + un * carried + odd,
        central[2] + va * carried + sa,
        central[3] + vb * carried + sb,
        central[4] + enthalpy * even + un * odd + half * entropy + va * sa + vb * sb,
    )


def face_from(load, sum_state):
    return face_terms(
        [functools.partial(lambda s, c: load(c, s), s) for s in range(5)],
        [functools.partial(lambda s, c: load(5 + c, s), s) for s in range(5)],
        sum_state,
        lambda c: load(10 + c, 2),
        load(15, 2),
    )


def with_terms(state):
    return (state, *cell_terms(state))


def lane_index(shape):
    return lax.broadcasted_iota(jnp.int32, shape, len(shape) - 1)


def pack_kernel(ids, section, theta_low, theta_high, theta_own, radial_low, radial_high, near, far, rows):
    planes, bands, width = section.shape[1:]
    tiles = width // lanes
    facing = jnp.where(ids[0] == 0, planes - ghosts, 0)
    for c in range(5):
        for i in range(ghosts):
            near[c, i] = section[c, facing + i, :, width - near.shape[3] :]
            far[c, i] = section[c, facing + i, :, : far.shape[3]]
    lane = lane_index((bands, lanes))
    for c in range(5):
        own = jnp.full((bands, lanes), (1.0, 0.0, 0.0, 0.0, 3.0)[c], jnp.float32)
        low = high = own
        for p in range(planes):
            at = lane - group * p
            head = section[c, p, :, 0:lanes]
            tail = section[c, p, :, width - lanes : width]
            turned_head = pltpu.roll(head, group * p + ghosts, 1)
            turned_tail = pltpu.roll(tail, group * p + group - ghosts, 1)
            own = jnp.where((at >= ghosts) & (at < group // 2), turned_head, own)
            own = jnp.where((at >= group // 2) & (at < group - ghosts), turned_tail, own)
            low = jnp.where((at >= group - ghosts) & (at < group), pltpu.roll(head, group * p + group - ghosts, 1), low)
            high = jnp.where((at >= 0) & (at < ghosts), pltpu.roll(tail, group * p + ghosts, 1), high)
        theta_own[c] = own
        theta_low[c] = low
        theta_high[c] = high
    for c in range(5):

        def plane(p, carry):
            for j in range(tiles):
                rows[j * bands : (j + 1) * bands] = section[c, p, :, j * lanes : (j + 1) * lanes]
            for k in range(ghosts):
                radial_low[c, p, k] = rows[pl.ds(k, tiles, stride=bands)]
                radial_high[c, p, k] = rows[pl.ds(bands - ghosts + k, tiles, stride=bands)]
            return carry

        lax.fori_loop(0, planes, plane, 0)


def pack(ids, section, near, far):
    _, planes, bands, width = section.shape
    tiles = width // lanes
    vmem = pl.BlockSpec(memory_space=pltpu.VMEM)
    array = lambda *shape: jax.ShapeDtypeStruct(shape, jnp.float32)
    theta = array(5, bands, lanes)
    radial = array(5, planes, ghosts, tiles, lanes)
    mortar = [array(5, ghosts, bands, part) for part in (near, far)]
    return pl.pallas_call(
        pack_kernel,
        in_specs=[pl.BlockSpec(memory_space=pltpu.SMEM), vmem],
        out_shape=(theta, theta, theta, radial, radial, *mortar),
        scratch_shapes=[pltpu.VMEM((bands * tiles, lanes), jnp.float32)],
        compiler_params=pltpu.CompilerParams(vmem_limit_bytes=vmem_bytes),
        name="pack",
    )(ids, section)


batch = 2


def inner_kernel(ids, section, order, low_radial, high_radial, acc, rows, lead, terms, fluxes):
    radial_pass(ids, section, low_radial, high_radial, rows, lead, terms, fluxes)
    theta_pass(section, order, acc, rows, lead, terms, fluxes)
    axial_inner(ids, section, acc, lead, terms)


def lead_faces(lead, terms, fluxes, columns):
    count = lead.shape[1] - 1

    def interface(r, carry):
        left = with_terms([lead[n, r, 0:columns] for n in range(5)])
        right = with_terms([lead[n, r + 1, 0:columns] for n in range(5)])
        for n, value in enumerate(interface_terms(left, right)):
            terms[n, r, 0:columns] = value
        return carry

    lax.fori_loop(0, count, interface, 0)

    def group_of(g, carry):
        p = g * batch

        def face(r, carry):
            flux = face_from(
                lambda n, s: terms[n, r + s, pl.ds(p, batch)],
                lambda n: lead[n, r + 2, pl.ds(p, batch)] + lead[n, r + 3, pl.ds(p, batch)],
            )
            for n, value in enumerate(flux):
                fluxes[n, r, pl.ds(p, batch)] = value
            return carry

        lax.fori_loop(0, count - 4, face, 0)
        return carry

    lax.fori_loop(0, columns // batch, group_of, 0)


def radial_pass(ids, section, low_radial, high_radial, rows, lead, terms, fluxes):
    planes, bands, width = section.shape[1:]
    tiles = width // lanes
    at_inner = ids[1] == 0
    at_outer = ids[1] == ids[2] - 1

    def spread(p, carry):
        for n, c in enumerate(radial_order):
            for j in range(tiles):
                rows[c, p, j * bands : (j + 1) * bands] = section[c, p, :, j * lanes : (j + 1) * lanes]
            for r in range(bands):
                lead[n, r + ghosts, p] = rows[c, p, pl.ds(r, tiles, stride=bands)]
            sign = -1.0 if c == 3 else 1.0
            for k in range(ghosts):
                wall_low = sign * rows[c, p, pl.ds(ghosts - 1 - k, tiles, stride=bands)]
                wall_high = sign * rows[c, p, pl.ds(bands - 1 - k, tiles, stride=bands)]
                lead[n, k, p] = jnp.where(at_inner, wall_low, low_radial[c, p, k])
                lead[n, bands + ghosts + k, p] = jnp.where(at_outer, wall_high, high_radial[c, p, k])
        return carry

    lax.fori_loop(0, planes, spread, 0)
    lead_faces(lead, terms, fluxes, planes)

    def gather(p, carry):
        for n, c in enumerate(radial_order):
            for r in range(bands):
                rows[c, p, pl.ds(r, tiles, stride=bands)] = fluxes[n, r + 1, p] - fluxes[n, r, p]
        return carry

    lax.fori_loop(0, planes, gather, 0)


def two_parts(values):
    high = values.astype(jnp.bfloat16)
    low = (values - high.astype(jnp.float32)).astype(jnp.bfloat16)
    return jnp.concatenate([high, low], axis=0)


def azimuthal_order(width):
    tiles = width // lanes
    cell = np.arange(width)
    matrix = np.zeros((width, width), np.float32)
    matrix[cell, cell % tiles * lanes + cell // tiles] = 1.0
    return jnp.asarray(matrix, jnp.bfloat16)


def theta_pass(section, order, acc, rows, lead, terms, fluxes):
    planes, bands, width = section.shape[1:]
    tiles = width // lanes
    half = 5 * planes * bands
    cells = jnp.concatenate([section[c].reshape(planes * bands, width) for c in theta_order], axis=0)
    both = jnp.dot(two_parts(cells), order[...], preferred_element_type=jnp.float32)
    both = (both[:half] + both[half:]).reshape(5, planes, bands, width)
    for n in range(5):
        for j in range(tiles):
            row = both[n, :, :, j * lanes : (j + 1) * lanes]
            lead[n, ghosts + j, 0:planes] = row
            if j < ghosts:
                lead[n, ghosts + tiles + j, 0:planes] = pltpu.roll(row, lanes - 1, 2)
            if j >= tiles - ghosts:
                lead[n, j + ghosts - tiles, 0:planes] = pltpu.roll(row, 1, 2)
    lead_faces(lead, terms, fluxes, planes)
    lane = lane_index((planes, bands, lanes))

    def flux(n, r):
        value = fluxes[n, r, 0:planes]
        if r < ghosts:
            return jnp.where(lane == 0, 0.0, value)
        if r > tiles - ghosts:
            return jnp.where(lane == lanes - 1, 0.0, value)
        return value

    changes = []
    for n in range(5):
        values = [flux(n, r) for r in range(tiles + 1)]
        parts = [values[r + 1] - values[r] for r in range(tiles)]
        changes.append(jnp.concatenate([v.reshape(planes * bands, lanes) for v in parts], axis=1))
    changes = two_parts(jnp.concatenate(changes, axis=0))
    both = lax.dot_general(changes, order[...], (((1,), (1,)), ((), ())), preferred_element_type=jnp.float32)
    both = (both[:half] + both[half:]).reshape(5, planes, bands, width)
    for n, c in enumerate(theta_order):
        for j in range(tiles):
            place = slice(j * lanes, (j + 1) * lanes)
            acc[c, 1 : planes + 1, :, place] = both[n, :, :, place] + rows[c, :, j * bands : (j + 1) * bands]


def axial_faces(count, first, acc, lead, terms):
    tiles = lead.shape[2]

    def interface(i, carry):
        left = with_terms([lead[n, i] for n in range(5)])
        right = with_terms([lead[n, i + 1] for n in range(5)])
        for n, value in enumerate(interface_terms(left, right)):
            terms[n, i] = value
        return carry

    lax.fori_loop(0, count + 4, interface, 0)

    def columns(g, carry):
        b0 = g * batch

        def face(i, carry):
            flux = face_from(
                lambda n, s: terms[n, i + s, pl.ds(b0, batch)],
                lambda n: lead[n, i + 2, pl.ds(b0, batch)] + lead[n, i + 3, pl.ds(b0, batch)],
            )
            for c, value in zip(axial_order, flux):
                for b in range(batch):
                    place = pl.ds(pl.multiple_of((b0 + b) * lanes, lanes), lanes)
                    acc[c, first + i, :, place] += value[b]
                    acc[c, first + i + 1, :, place] -= value[b]
            return carry

        lax.fori_loop(0, count, face, 0)
        return carry

    lax.fori_loop(0, tiles // batch, columns, 0)


def fill_plane(lead, section, at, plane):
    for c in axial_order:
        for j in range(section.shape[3] // lanes):
            lead[c, at, j] = section[c, plane, :, j * lanes : (j + 1) * lanes]


def axial_inner(ids, section, acc, lead, terms):
    planes, bands, width = section.shape[1:]
    first = jnp.where(ids[0] == 0, 0, ghosts)
    count = planes + 1 - ghosts
    for c in range(5):
        acc[c, 0] = jnp.zeros((bands, width), jnp.float32)
        acc[c, planes + 1] = jnp.zeros((bands, width), jnp.float32)

    def fill(i, carry):
        fill_plane(lead, section, i, jnp.clip(first + i - ghosts, 0, planes - 1))
        return carry

    lax.fori_loop(0, count + 5, fill, 0)
    axial_faces(count, first, acc, lead, terms)


def inner(ids, section, order, low_radial, high_radial):
    _, planes, bands, width = section.shape
    tiles = width // lanes
    depth = max(bands, tiles) + 2 * ghosts
    across = max(planes, tiles)
    vmem = pl.BlockSpec(memory_space=pltpu.VMEM)
    faces = (planes + 1) * tiles + planes * (tiles + bands + 2)
    return pl.pallas_call(
        inner_kernel,
        in_specs=[pl.BlockSpec(memory_space=pltpu.SMEM)] + [vmem] * 4,
        out_shape=jax.ShapeDtypeStruct((5, planes + 2, bands, width), jnp.float32),
        scratch_shapes=[
            pltpu.VMEM((5, planes, bands * tiles, lanes), jnp.float32),
            pltpu.VMEM((5, depth, across, 8, lanes), jnp.float32),
            pltpu.VMEM((16, depth - 1, across, 8, lanes), jnp.float32),
            pltpu.VMEM((5, depth - 5, planes, 8, lanes), jnp.float32),
        ],
        compiler_params=pltpu.CompilerParams(vmem_limit_bytes=vmem_bytes),
        cost_estimate=pl.CostEstimate(
            flops=faces * 8 * lanes * 700, bytes_accessed=section.size * 16, transcendentals=faces * 8 * lanes * 30
        ),
        name="inner",
    )(ids, section, order, low_radial, high_radial)


def mortar_planes(turn, near, far, window, write):
    _, _, bands, width = window.shape
    window[:, :, :, : near.shape[3]] = near[...]
    window[:, :, :, near.shape[3] :] = far[...]
    whole_tiles = turn[0] // lanes
    rest = turn[0] % lanes
    fraction = 0.25 * turn[1].astype(jnp.float32)
    source = lax.broadcasted_iota(jnp.int32, (2 * lanes, lanes), 0)
    target = lax.broadcasted_iota(jnp.int32, (2 * lanes, lanes), 1)
    gap = source + target - (lanes - 1 + rest)
    blend = jnp.where(gap == 0, 1.0 - fraction, jnp.where(gap == 1, fraction, 0.0)).astype(jnp.bfloat16)
    blend = jnp.concatenate([blend] * 3, axis=0)
    tiles = (width - chunk) // lanes
    for t in range(tiles):
        start = pl.multiple_of((tiles - 1 - t + whole_tiles) * lanes, lanes)
        cells = window[:, :, :, pl.ds(start, 2 * lanes)].reshape(5 * ghosts * bands, 2 * lanes)
        parts = []
        for _ in range(3):
            part = cells.astype(jnp.bfloat16)
            parts.append(part)
            cells = cells - part.astype(jnp.float32)
        mixed = jnp.dot(jnp.concatenate(parts, axis=1), blend, preferred_element_type=jnp.float32)
        mixed = mixed.reshape(5, ghosts, bands, lanes)
        for c in range(5):
            write(c, t, -mixed[c] if c == 2 else mixed[c])


def theta_edges(theta_own, left_high, right_low, acc):
    planes, bands, width = acc.shape[1] - 2, acc.shape[2], acc.shape[3]
    lane = lane_index((bands, lanes))
    at = lane % group
    inside = lane < group * planes
    cells = [
        jnp.where(inside & (at < ghosts), left_high[c], jnp.where(inside & (at >= group - ghosts), right_low[c], theta_own[c]))
        for c in theta_order
    ]
    turn = lambda value, shift: pltpu.roll(value, -shift % lanes, 1) if shift else value
    after = [turn(v, 1) for v in cells]
    terms = interface_terms(with_terms(cells), with_terms(after))
    flux = face_from(lambda n, s: turn(terms[n], s - 2), lambda n: cells[n] + after[n])
    low, high = ghosts - 1, group // 2 + 2
    wanted = inside & (((at >= low) & (at < low + 3)) | ((at >= high) & (at < high + 3)))
    for c, value in zip(theta_order, flux):
        value = jnp.where(wanted, value, 0.0)
        change = value - turn(value, -1)
        for p in range(planes):
            first = turn(change, group * p + ghosts)
            last = turn(change, group * p + high + ghosts - lanes)
            acc[c, p + 1, :, 0:lanes] += jnp.where(lane < ghosts, first, 0.0)
            acc[c, p + 1, :, width - lanes : width] += jnp.where(lane >= lanes - ghosts, last, 0.0)


def tail_kernel(ids, turn, section, base, acc, near, far, theta_own, left_high, right_low, out, lead, terms, window):
    planes, bands, width = section.shape[1:]
    front = ids[0] == 0
    kept = planes - 1
    own = jnp.where(front, 1, 0)
    own_at = jnp.where(front, 0, ghosts)
    ghost_at = jnp.where(front, kept, 0)
    first = jnp.where(front, planes + 1 - ghosts, 0)

    def fill(i, carry):
        fill_plane(lead, section, own_at + i, own + i)
        return carry

    lax.fori_loop(0, kept, fill, 0)

    def write(c, t, values):
        lead[c, pl.ds(ghost_at, ghosts), t] = values

    mortar_planes(turn, near, far, window, write)
    theta_edges(theta_own, left_high, right_low, acc)
    axial_faces(ghosts, first, acc, lead, terms)
    for c in range(5):

        def update(p, carry):
            change = (-0.25 * step_ratio / flux_scale) * acc[c, p + 1]
            out[c, p] = 0.75 * base[c, p] + (0.25 * section[c, p] + change)
            return carry

        lax.fori_loop(0, planes, update, 0)


def tail(ids, turn, section, base, acc, near, far, theta_own, left_high, right_low):
    _, planes, bands, width = section.shape
    tiles = width // lanes
    smem = pl.BlockSpec(memory_space=pltpu.SMEM)
    vmem = pl.BlockSpec(memory_space=pltpu.VMEM)
    anywhere = pl.BlockSpec(memory_space=pl.ANY)

    def kernel(ids, turn, section, base, acc_in, near, far, own, left, right, out, acc, lead, terms, window, sem):
        copy = pltpu.make_async_copy(acc_in, acc, sem)
        copy.start()
        copy.wait()
        tail_kernel(ids, turn, section, base, acc, near, far, own, left, right, out, lead, terms, window)

    return pl.pallas_call(
        kernel,
        in_specs=[smem, smem, vmem, vmem, anywhere] + [vmem] * 5,
        out_shape=jax.ShapeDtypeStruct(section.shape, jnp.float32),
        scratch_shapes=[
            pltpu.VMEM(acc.shape, jnp.float32),
            pltpu.VMEM((5, planes - 1 + ghosts, tiles, bands, lanes), jnp.float32),
            pltpu.VMEM((16, 2 * ghosts + 1, tiles, bands, lanes), jnp.float32),
            pltpu.VMEM((5, ghosts, bands, near.shape[3] + far.shape[3]), jnp.float32),
            pltpu.SemaphoreType.DMA(()),
        ],
        compiler_params=pltpu.CompilerParams(vmem_limit_bytes=vmem_bytes),
        name="tail",
    )(ids, turn, section, base, acc, near, far, theta_own, left_high, right_low)


def slab_routes(turns, slabs):
    both = []
    for ahead in (1, 0):
        both.append(
            [
                (block * slabs + slab, (1 - block) * slabs + (turns - ahead - slab) % slabs)
                for block in range(2)
                for slab in range(slabs)
            ]
        )
    return both


def exchange_and_step(ids, turn, order, base, section, near, far, transfer):
    slabs = lax.axis_size("theta")
    bands = lax.axis_size("radial")
    theta_low, theta_high, theta_own, radial_low, radial_high, near, far = pack(ids, section, near, far)
    near, far = transfer(near, far)
    low_radial = lax.ppermute(radial_high, "radial", [(i, i + 1) for i in range(bands - 1)])
    high_radial = lax.ppermute(radial_low, "radial", [(i + 1, i) for i in range(bands - 1)])
    left_high = lax.ppermute(theta_high, "theta", [(i, (i + 1) % slabs) for i in range(slabs)])
    right_low = lax.ppermute(theta_low, "theta", [((i + 1) % slabs, i) for i in range(slabs)])
    acc = inner(ids, section, order, low_radial, high_radial)
    return tail(ids, turn, section, base, acc, near, far, theta_own, left_high, right_low)


def shards(base_state, section_state, rotor_step):
    width = section_state.shape[3]
    slabs = lax.axis_size("theta")
    slab = lax.axis_index("theta")
    ids = jnp.stack([lax.axis_index("blk"), lax.axis_index("radial"), lax.axis_size("radial")]).astype(jnp.int32)
    step = rotor_step[0]
    offset = step // 4
    turns = offset // width
    start = offset % width
    cuts = width // chunk
    turn = jnp.stack([start % chunk, step % 4])
    order = azimuthal_order(width)

    if slabs > most_slabs:

        def gathered(near, far):
            facing = lax.ppermute(far, "blk", [(0, 1), (1, 0)])
            whole = lax.all_gather(facing, "theta", axis=3, tiled=True)
            doubled = jnp.concatenate([whole, whole, whole[..., :chunk]], axis=3)
            begin = (turns - 1 - slab) % slabs * width + start // chunk * chunk
            window = lax.dynamic_slice_in_dim(doubled, begin, width + chunk, 3)
            return window[..., :width], window[..., width:]

        return exchange_and_step(ids, turn, order, base_state, section_state, chunk, width, gathered)

    def branch(case):
        turned, cut = divmod(case, cuts)
        near_route, far_route = slab_routes(turned, slabs)

        def transfer(near, far):
            return (
                lax.ppermute(near, ("blk", "theta"), near_route),
                lax.ppermute(far, ("blk", "theta"), far_route),
            )

        def run(ids, turn, order, base, section):
            return exchange_and_step(
                ids, turn, order, base, section, width - cut * chunk, (cut + 1) * chunk, transfer
            )

        return run

    case = turns * cuts + start // chunk
    return lax.switch(case, [branch(i) for i in range(slabs * cuts)], ids, turn, order, base_state, section_state)


def solution(mesh):
    in_specs = (P(None, "blk", "radial", "theta"), P(None, "blk", "radial", "theta"), P())
    out_specs = P(None, "blk", "radial", "theta")
    return jax.shard_map(shards, mesh=mesh, in_specs=in_specs, out_specs=out_specs, check_vma=False)
```

```python
import functools

import jax
import jax.numpy as jnp
from jax import lax
from jax.experimental import pallas as pl
from jax.experimental.pallas import tpu as pltpu
from jax.sharding import PartitionSpec as P

gamma_ratio = 1.4
weno_epsilon = 1e-06
step_ratio = 0.12
lanes = 128
ghosts = 3
group = 16
batch = 2
flux_scale = 12.0
most_slabs = 8
vmem_bytes = 48 * 1024 * 1024

axial_order = (0, 1, 2, 3, 4)
radial_order = (0, 3, 1, 2, 4)
theta_order = (0, 2, 1, 3, 4)


def inverse(value):
    guess = pl.reciprocal(value, approx=True)
    return guess * (2.0 - value * guess)


def cell_terms(state):
    density, normal, first, second, energy = state
    inv = inverse(density)
    speed = normal * inv
    kinetic = 0.5 * (normal * normal + first * first + second * second) * inv
    pressure = (gamma_ratio - 1.0) * (energy - kinetic)
    square = gamma_ratio * pressure * inv
    wave = jnp.abs(speed) + square * lax.rsqrt(square)
    flux = (normal, normal * speed + pressure, first * speed, second * speed, (energy + pressure) * speed)
    return flux, wave


def interface_terms(left, right):
    (state_l, flux_l, wave_l), (state_r, flux_r, wave_r) = left, right
    return (
        [r - l for l, r in zip(state_l, state_r)]
        + [r - l for l, r in zip(flux_l, flux_r)]
        + [0.5 * flux_scale * (r + l) for l, r in zip(flux_l, flux_r)]
        + [jnp.maximum(wave_l, wave_r)]
    )


def weno_terms(d0, d1, d2, d3, epsilon):
    e0 = d1 - d0
    e1 = d2 - d1
    e2 = d3 - d2
    f0 = e0 - e1
    f1 = e1 - e2
    t1 = 0.75 * d1
    t2 = 0.75 * d2
    shared = t1 * d2 + epsilon
    low = e0 * e0 + (t1 * f0 + shared)
    mid = e1 * e1 + shared
    high = e2 * e2 + (t2 * f1 + shared)
    x = mid * pl.reciprocal(low, approx=True)
    y = mid * pl.reciprocal(high, approx=True)
    weight_low = x * x
    weight_high = 1.5 * (y * y)
    total = 0.5 * weight_low + (weight_high + 3.0)
    return (weight_low * f0 + weight_high * f1) * pl.reciprocal(total, approx=True)


def face_terms(diff_state, diff_flux, sum_state, sum_flux, wave):
    inv = inverse(sum_state(0))
    un, va, vb, specific = (inv * sum_state(k) for k in range(1, 5))
    half = 0.5 * (un * un + va * va + vb * vb)
    internal = specific - half
    square = gamma_ratio * (gamma_ratio - 1.0) * internal
    inv_sound = lax.rsqrt(square)
    sound = square * inv_sound
    factor = (gamma_ratio - 1.0) * inv_sound * inv_sound
    enthalpy = specific + (gamma_ratio - 1.0) * internal

    def project(dens, norm, first, second, energy):
        sn = norm - un * dens
        sa = first - va * dens
        sb = second - vb * dens
        even = factor * (energy - half * dens - un * sn - va * sa - vb * sb)
        odd = inv_sound * sn
        return even - odd, dens - even, sa, sb, even + odd

    def side(vectors):
        chars = [project(*vector) for vector in vectors]
        return [weno_terms(*(c[k] for c in chars), weno_epsilon * (12.0 if k in (0, 4) else 3.0)) for k in range(5)]

    plus = [[diff_flux[s](c) + wave * diff_state[s](c) for c in range(5)] for s in range(4)]
    forward = side(plus)
    minus = [[diff_flux[s](c) - wave * diff_state[s](c) for c in range(5)] for s in range(4, 0, -1)]
    backward = side(minus)
    central = [sum_flux(c) + (plus[1][c] - plus[2][c]) + (minus[2][c] - minus[1][c]) for c in range(5)]
    wave_minus, entropy, sa, sb, wave_plus = (f - b for f, b in zip(forward, backward))
    even = 0.5 * (wave_plus + wave_minus)
    odd = sound * (0.5 * (wave_plus - wave_minus))
    carried = even + entropy
    return (
        central[0] + carried,
        central[1] + un * carried + odd,
        central[2] + va * carried + sa,
        central[3] + vb * carried + sb,
        central[4] + enthalpy * even + un * odd + half * entropy + va * sa + vb * sb,
    )


def face_from(load, sum_state):
    return face_terms(
        [functools.partial(lambda s, c: load(c, s), s) for s in range(5)],
        [functools.partial(lambda s, c: load(5 + c, s), s) for s in range(5)],
        sum_state,
        lambda c: load(10 + c, 2),
        load(15, 2),
    )


def with_terms(state):
    return (state, *cell_terms(state))


def lane_index(shape):
    return lax.broadcasted_iota(jnp.int32, shape, len(shape) - 1)


def tile_rows(state):
    components, planes, bands, width = state.shape
    split = state.reshape(components, planes, bands, width // lanes, lanes)
    return split.transpose(0, 1, 3, 2, 4).reshape(components, planes, -1, lanes)


def from_tile_rows(rows, bands):
    components, planes, count, _ = rows.shape
    split = rows.reshape(components, planes, count // bands, bands, lanes)
    return split.transpose(0, 1, 3, 2, 4).reshape(components, planes, bands, -1)


def loop(count, body):
    def step(i, carry):
        body(i)
        return carry

    lax.fori_loop(0, count, step, 0)


def make_order(order):
    width = order.shape[0]
    tiles = width // lanes

    def order_rows(t):
        row = lax.broadcasted_iota(jnp.int32, (lanes, width), 0) + t * lanes
        column = lax.broadcasted_iota(jnp.int32, (lanes, width), 1)
        target = row % tiles * lanes + row // tiles
        order[pl.ds(pl.multiple_of(t * lanes, lanes), lanes)] = jnp.where(column == target, 1.0, 0.0).astype(jnp.bfloat16)

    loop(tiles, order_rows)


def store_split(split, n, tile, values):
    high = values.astype(jnp.bfloat16)
    low = (values - high.astype(jnp.float32)).astype(jnp.bfloat16)
    flat = values.shape[0]
    start = pl.multiple_of(n * flat, 16)
    split[pl.ds(start, flat), tile * lanes : (tile + 1) * lanes] = high
    split[pl.ds(5 * flat + start, flat), tile * lanes : (tile + 1) * lanes] = low


def reorder(section, cells, split, order):
    _, tiles, planes, bands, _ = cells.shape
    flat = planes * bands
    for n, c in enumerate(theta_order):
        for t in range(tiles):
            store_split(split, n, t, section[c, :, t * bands : (t + 1) * bands].reshape(flat, lanes))
    both = jnp.dot(split[...], order[...], preferred_element_type=jnp.float32)
    both = both[: 5 * flat] + both[5 * flat :]
    for n in range(5):
        for j in range(tiles):
            part = both[n * flat : (n + 1) * flat, j * lanes : (j + 1) * lanes]
            cells[n, j] = part.reshape(planes, bands, lanes)


def restore(split, order, planes, acc):
    tiles = order.shape[0] // lanes
    flat = split.shape[0] // 10
    bands = flat // planes
    both = lax.dot_general(split[...], order[...], (((1,), (1,)), ((), ())), preferred_element_type=jnp.float32)
    both = both[: 5 * flat] + both[5 * flat :]
    for n, c in enumerate(theta_order):
        for t in range(tiles):
            part = both[n * flat : (n + 1) * flat, t * lanes : (t + 1) * lanes]
            acc[c, 1 : planes + 1, t * bands : (t + 1) * bands] = part.reshape(planes, bands, lanes)


def pack_kernel(
    bands, ids, turn, section,
    held, theta_low, theta_high, theta_own, radial_low, radial_high, whole, part, cells, order, split
):
    planes, rows = section.shape[1:3]
    tiles = rows // bands
    facing = jnp.where(ids[0] == 0, planes - ghosts, 0)
    part_at = pl.multiple_of(turn[2] * part.shape[2], bands)
    lane = lane_index((bands, lanes))

    def component(c):
        held[c] = section[c]
        for i in range(ghosts):
            whole[c, i] = section[c, facing + i]
            part[c, i] = section[c, facing + i, pl.ds(part_at, part.shape[2])]
        own = jnp.full((bands, lanes), (1.0, 0.0, 0.0, 0.0, 3.0)[c], jnp.float32)
        low = high = own
        for p in range(planes):
            at = lane - group * p
            first = section[c, p, 0:bands]
            last = section[c, p, rows - bands : rows]
            own_first = pltpu.roll(first, group * p + ghosts, 1)
            own_last = pltpu.roll(last, group * p + group - ghosts, 1)
            sent_low = pltpu.roll(first, group * p + group - ghosts, 1)
            sent_high = pltpu.roll(last, group * p + ghosts, 1)
            own = jnp.where((at >= ghosts) & (at < group // 2), own_first, own)
            own = jnp.where((at >= group // 2) & (at < group - ghosts), own_last, own)
            low = jnp.where((at >= group - ghosts) & (at < group), sent_low, low)
            high = jnp.where((at >= 0) & (at < ghosts), sent_high, high)
        theta_own[c] = own
        theta_low[c] = low
        theta_high[c] = high

        for p in range(planes):
            for k in range(ghosts):
                radial_low[c, p, k] = section[c, p, pl.ds(k, tiles, stride=bands)]
                radial_high[c, p, k] = section[c, p, pl.ds(bands - ghosts + k, tiles, stride=bands)]

    for c in range(5):
        component(c)
    make_order(order)
    reorder(section, cells, split, order)


def pack(ids, turn, section, bands):
    _, planes, rows, _ = section.shape
    smem = pl.BlockSpec(memory_space=pltpu.SMEM)
    vmem = pl.BlockSpec(memory_space=pltpu.VMEM)
    array = lambda *shape: jax.ShapeDtypeStruct(shape, jnp.float32)
    theta = array(5, bands, lanes)
    radial = array(5, planes, ghosts, rows // bands, lanes)
    mortar = [array(5, ghosts, rows, lanes), array(5, ghosts, rows // 2, lanes)]
    width = rows // bands * lanes
    cells = array(5, rows // bands, planes, bands, lanes)
    order = jax.ShapeDtypeStruct((width, width), jnp.bfloat16)
    return pl.pallas_call(
        functools.partial(pack_kernel, bands),
        in_specs=[smem, smem, vmem],
        out_specs=[vmem] * 10,
        out_shape=(array(*section.shape), theta, theta, theta, radial, radial, *mortar, cells, order),
        scratch_shapes=[pltpu.VMEM((10 * planes * bands, width), jnp.bfloat16)],
        compiler_params=pltpu.CompilerParams(vmem_limit_bytes=vmem_bytes),
        name="pack",
    )(ids, turn, section)


def inner_kernel(bands, ids, section, cells, low_radial, high_radial, acc, split, lead, terms, fluxes):
    radial_pass(bands, ids, section, low_radial, high_radial, acc, lead, terms, fluxes)
    theta_pass(cells, lead, terms, fluxes, split)
    axial_inner(ids, section, acc, lead, terms)


def lead_faces(lead, cells, columns, terms, emit):
    def column_group(g):
        p = g * batch

        def state(r):
            return [lead[n, r, pl.ds(p, batch)] for n in range(5)]

        def cell(r):
            here = state(r)
            flux, wave = cell_terms(here)
            return here, flux, wave

        def keep(r, values):
            for n, value in enumerate((*values[1], values[2])):
                terms[16 + n, r] = value

        def interface(r, right):
            left = (state(r), [terms[16 + n, r] for n in range(5)], terms[21, r])
            for n, value in enumerate(interface_terms(left, right)):
                terms[n, r] = value

        left = cell(0)
        for r in range(5):
            right = cell(r + 1)
            for n, value in enumerate(interface_terms(left, right)):
                terms[n, r] = value
            left = right
        keep(5, left)

        def face(r):
            flux = face_from(
                lambda n, s: terms[n, r + s],
                lambda n: lead[n, r + 2, pl.ds(p, batch)] + lead[n, r + 3, pl.ds(p, batch)],
            )
            emit(r, p, flux)
            right = cell(jnp.minimum(r + 6, cells - 1))
            interface(r + 5, right)
            keep(r + 6, right)

        loop(cells - 5, face)

    loop(columns // batch, column_group)


def keep_flux(fluxes, r, p, flux):
    for n, value in enumerate(flux):
        fluxes[n, r, pl.ds(p, batch)] = value


def radial_pass(bands, ids, section, low_radial, high_radial, acc, lead, terms, fluxes):
    planes, rows = section.shape[1:3]
    tiles = rows // bands
    at_inner = ids[1] == 0
    at_outer = ids[1] == ids[2] - 1

    def spread(p):
        for n, c in enumerate(radial_order):
            band = [section[c, p, pl.ds(r, tiles, stride=bands)] for r in range(bands)]
            sign = -1.0 if c == 3 else 1.0
            for r in range(bands):
                lead[n, r + ghosts, p] = band[r]
            for k in range(ghosts):
                lead[n, k, p] = jnp.where(at_inner, sign * band[ghosts - 1 - k], low_radial[c, p, k])
                lead[n, bands + ghosts + k, p] = jnp.where(at_outer, sign * band[bands - 1 - k], high_radial[c, p, k])

    loop(planes, spread)
    lead_faces(lead, bands + 2 * ghosts, planes, terms, functools.partial(keep_flux, fluxes))

    def gather(p):
        for n, c in enumerate(radial_order):
            for r in range(bands):
                acc[c, p + 1, pl.ds(r, tiles, stride=bands)] = fluxes[n, r + 1, p] - fluxes[n, r, p]

    loop(planes, gather)


def theta_pass(cells, lead, terms, fluxes, split):
    _, tiles, planes, bands, _ = cells.shape

    def fill(n):
        for j in range(tiles):
            lead[n, ghosts + j, 0:planes] = cells[n, j]
        for k in range(ghosts):
            lead[n, k, 0:planes] = pltpu.roll(cells[n, tiles - ghosts + k], 1, 2)
            lead[n, ghosts + tiles + k, 0:planes] = pltpu.roll(cells[n, k], lanes - 1, 2)

    loop(5, fill)
    lead_faces(lead, tiles + 2 * ghosts, planes, terms, functools.partial(keep_flux, fluxes))
    lane = lane_index((planes, bands, lanes))

    def changes(n):
        before = None
        for r in range(tiles + 1):
            flux = fluxes[n, r, 0:planes]
            if r < ghosts:
                flux = jnp.where(lane == 0, 0.0, flux)
            if r > tiles - ghosts:
                flux = jnp.where(lane == lanes - 1, 0.0, flux)
            if r > 0:
                store_split(split, n, r - 1, (flux - before).reshape(planes * bands, lanes))
            before = flux

    loop(5, changes)


def axial_faces(count, first, acc, lead, terms):
    tiles, bands = lead.shape[2:4]

    def emit(i, p, flux):
        place = pl.ds(pl.multiple_of(p * bands, bands), batch * bands)
        for c, value in zip(axial_order, flux):
            value = value.reshape(batch * bands, lanes)
            acc[c, first + i, place] += value
            acc[c, first + i + 1, place] -= value

    lead_faces(lead, count + 5, tiles, terms, emit)


def axial_inner(ids, section, acc, lead, terms):
    planes = section.shape[1]
    tiles, bands = lead.shape[2:4]
    first = jnp.where(ids[0] == 0, 0, ghosts)
    count = planes + 1 - ghosts
    for c in range(5):
        acc[c, 0] = jnp.zeros(acc.shape[2:], jnp.float32)
        acc[c, planes + 1] = jnp.zeros(acc.shape[2:], jnp.float32)

    def fill(i):
        plane = jnp.clip(first + i - ghosts, 0, planes - 1)
        for c in axial_order:
            lead[c, i] = section[c, plane].reshape(tiles, bands, lanes)

    loop(count + 5, fill)
    axial_faces(count, first, acc, lead, terms)


def inner(ids, section, cells, bands, low_radial, high_radial):
    _, planes, rows, _ = section.shape
    tiles = rows // bands
    depth = max(bands, tiles) + 2 * ghosts
    across = max(planes, tiles)
    vmem = pl.BlockSpec(memory_space=pltpu.VMEM)
    faces = (planes + 1) * tiles + planes * (tiles + bands + 2)
    return pl.pallas_call(
        functools.partial(inner_kernel, bands),
        in_specs=[pl.BlockSpec(memory_space=pltpu.SMEM)] + [vmem] * 4,
        out_shape=(
            jax.ShapeDtypeStruct((5, planes + 2, rows, lanes), jnp.float32),
            jax.ShapeDtypeStruct((10 * planes * bands, tiles * lanes), jnp.bfloat16),
        ),
        scratch_shapes=[
            pltpu.VMEM((5, depth, across, 8, lanes), jnp.float32),
            pltpu.VMEM((22, depth + 1, batch, 8, lanes), jnp.float32),
            pltpu.VMEM((5, depth - 5, planes, 8, lanes), jnp.float32),
        ],
        compiler_params=pltpu.CompilerParams(vmem_limit_bytes=vmem_bytes),
        cost_estimate=pl.CostEstimate(
            flops=faces * 8 * lanes * 700, bytes_accessed=section.size * 16, transcendentals=faces * 8 * lanes * 30
        ),
        name="inner",
    )(ids, section, cells, low_radial, high_radial)


def mortar_planes(turn, whole, part, window, lead, at):
    tiles, bands = lead.shape[2:4]
    whole_at = pl.multiple_of(jnp.where(turn[2] == 0, 0, part.shape[2]), bands)
    part_at = pl.multiple_of(jnp.where(turn[2] == 0, whole.shape[2], 0), bands)
    for c in range(5):
        window[c, :, pl.ds(whole_at, whole.shape[2])] = whole[c]
        window[c, :, pl.ds(part_at, part.shape[2])] = part[c]
    skipped = turn[0] // lanes
    rest = turn[0] % lanes
    fraction = 0.25 * turn[1].astype(jnp.float32)
    source = lax.broadcasted_iota(jnp.int32, (2 * lanes, lanes), 0)
    target = lax.broadcasted_iota(jnp.int32, (2 * lanes, lanes), 1)
    gap = source + target - (lanes - 1 + rest)
    blend = jnp.where(gap == 0, 1.0 - fraction, jnp.where(gap == 1, fraction, 0.0)).astype(jnp.bfloat16)
    blend = jnp.concatenate([blend[:lanes]] * 3 + [blend[lanes:]] * 3, axis=0)

    def parts_of(tile):
        start = pl.multiple_of((tile + skipped) * bands, bands)
        cells = window[:, :, pl.ds(start, bands)].reshape(5 * ghosts * bands, lanes)
        parts = []
        for _ in range(3):
            parts.append(cells.astype(jnp.bfloat16))
            cells = cells - parts[-1].astype(jnp.float32)
        return parts

    after = parts_of(tiles)
    for t in range(tiles):
        here = parts_of(tiles - 1 - t)
        mixed = jnp.dot(jnp.concatenate(here + after, axis=1), blend, preferred_element_type=jnp.float32)
        mixed = mixed.reshape(5, ghosts, bands, lanes)
        for c in range(5):
            lead[c, pl.ds(at, ghosts), t] = -mixed[c] if c == 2 else mixed[c]
        after = here


def theta_edges(theta_own, left_high, right_low, acc):
    planes, rows = acc.shape[1] - 2, acc.shape[2]
    bands = theta_own.shape[1]
    lane = lane_index((bands, lanes))
    at = lane % group
    inside = lane < group * planes
    cells = [
        jnp.where(inside & (at < ghosts), left_high[c], jnp.where(inside & (at >= group - ghosts), right_low[c], theta_own[c]))
        for c in theta_order
    ]
    turn = lambda value, shift: pltpu.roll(value, -shift % lanes, 1) if shift else value
    after = [turn(v, 1) for v in cells]
    terms = interface_terms(with_terms(cells), with_terms(after))
    flux = face_from(lambda n, s: turn(terms[n], s - 2), lambda n: cells[n] + after[n])
    low, high = ghosts - 1, group // 2 + 2
    wanted = inside & (((at >= low) & (at < low + 3)) | ((at >= high) & (at < high + 3)))
    flux = [jnp.where(wanted, value, 0.0) for value in flux]
    changes = [value - turn(value, -1) for value in flux]

    for p in range(planes):
        for c, change in zip(theta_order, changes):
            first = turn(change, group * p + ghosts)
            last = turn(change, group * p + high + ghosts - lanes)
            acc[c, p + 1, 0:bands] += jnp.where(lane < ghosts, first, 0.0)
            acc[c, p + 1, rows - bands : rows] += jnp.where(lane >= lanes - ghosts, last, 0.0)


def tail_kernel(
    ids, turn, section, base_state, acc, split, order, whole, part, theta_own, left_high, right_low, out_state,
    more, lead, terms, window, base, out, sems
):
    loading = pltpu.make_async_copy(base_state, base, sems.at[0])
    loading.start()
    planes = section.shape[1]
    tiles, bands = lead.shape[2:4]
    front = ids[0] == 0
    kept = planes - 1
    own = jnp.where(front, 1, 0)
    own_at = jnp.where(front, 0, ghosts)
    ghost_at = jnp.where(front, kept, 0)
    first = jnp.where(front, planes + 1 - ghosts, 0)

    def fill(i):
        for c in axial_order:
            lead[c, own_at + i] = section[c, own + i].reshape(tiles, bands, lanes)

    loop(kept, fill)

    for c in range(5):
        more[c, 0] = jnp.zeros(more.shape[2:], jnp.float32)
        more[c, planes + 1] = jnp.zeros(more.shape[2:], jnp.float32)
    restore(split, order, planes, more)
    mortar_planes(turn, whole, part, window, lead, ghost_at)
    theta_edges(theta_own, left_high, right_low, more)
    axial_faces(ghosts, first, more, lead, terms)

    loading.wait()
    storing = [pltpu.make_async_copy(out.at[c], out_state.at[c], sems.at[c]) for c in range(5)]
    for c in range(5):
        change = (-0.25 * step_ratio / flux_scale) * (acc[c, 1 : planes + 1] + more[c, 1 : planes + 1])
        out[c] = 0.75 * base[c] + (0.25 * section[c] + change)
        storing[c].start()
    for copy in storing:
        copy.wait()


def tail(ids, turn, section, base, acc, split, order, whole, part, theta_own, left_high, right_low):
    _, planes, rows, _ = section.shape
    bands = theta_own.shape[1]
    tiles = rows // bands
    smem = pl.BlockSpec(memory_space=pltpu.SMEM)
    vmem = pl.BlockSpec(memory_space=pltpu.VMEM)
    anywhere = pl.BlockSpec(memory_space=pl.ANY)
    return pl.pallas_call(
        tail_kernel,
        in_specs=[smem, smem, vmem, anywhere] + [vmem] * 8,
        out_specs=anywhere,
        out_shape=jax.ShapeDtypeStruct(section.shape, jnp.float32),
        scratch_shapes=[
            pltpu.VMEM(acc.shape, jnp.float32),
            pltpu.VMEM((5, planes - 1 + ghosts, tiles, bands, lanes), jnp.float32),
            pltpu.VMEM((22, 2 * ghosts + 3, batch, bands, lanes), jnp.float32),
            pltpu.VMEM((5, ghosts, whole.shape[2] + part.shape[2], lanes), jnp.float32),
            pltpu.VMEM(section.shape, jnp.float32),
            pltpu.VMEM(section.shape, jnp.float32),
            pltpu.SemaphoreType.DMA((5,)),
        ],
        compiler_params=pltpu.CompilerParams(vmem_limit_bytes=vmem_bytes),
        name="tail",
    )(ids, turn, section, base, acc, split, order, whole, part, theta_own, left_high, right_low)


def slab_routes(turns, slabs):
    both = []
    for ahead in (1, 0):
        both.append(
            [
                (block * slabs + slab, (1 - block) * slabs + (turns - ahead - slab) % slabs)
                for block in range(2)
                for slab in range(slabs)
            ]
        )
    return both


def shards(base_state, section_state, rotor_step):
    bands, width = section_state.shape[2:]
    rows = width // lanes * bands
    slabs = lax.axis_size("theta")
    slab = lax.axis_index("theta")
    parts = lax.axis_size("radial")
    ids = jnp.stack([lax.axis_index("blk"), lax.axis_index("radial"), parts]).astype(jnp.int32)
    step = rotor_step[0]
    offset = step // 4
    turns = offset // width
    start = offset % width
    second_half = start // (width // 2)
    turn = jnp.stack([start % (width // 2), step % 4, second_half])
    base, section = tile_rows(base_state), tile_rows(section_state)
    section, theta_low, theta_high, theta_own, radial_low, radial_high, whole, part, cells, order = pack(
        ids, turn, section, bands
    )

    def halos(radial_low, radial_high, theta_low, theta_high):
        return (
            lax.ppermute(radial_high, "radial", [(i, i + 1) for i in range(parts - 1)]),
            lax.ppermute(radial_low, "radial", [(i + 1, i) for i in range(parts - 1)]),
            lax.ppermute(theta_high, "theta", [(i, (i + 1) % slabs) for i in range(slabs)]),
            lax.ppermute(theta_low, "theta", [((i + 1) % slabs, i) for i in range(slabs)]),
        )

    if slabs > most_slabs:
        low_radial, high_radial, left_high, right_low = halos(radial_low, radial_high, theta_low, theta_high)
        facing = lax.ppermute(whole, "blk", [(0, 1), (1, 0)])
        ring = lax.all_gather(facing, "theta", axis=2, tiled=True)
        ring = jnp.concatenate([ring, ring, ring[:, :, : rows // 2]], axis=2)
        begin = (turns - 1 - slab) % slabs * rows + second_half * (rows // 2)
        whole = lax.dynamic_slice_in_dim(ring, begin, rows, 2)
        part = lax.dynamic_slice_in_dim(ring, begin + rows, rows // 2, 2)
        turn = turn.at[2].set(0)
        acc, split = inner(ids, section, cells, bands, low_radial, high_radial)
    else:

        def branch(case):
            near, far = slab_routes(case // 2 + 1, slabs)
            whole_route, part_route = (near, far) if case % 2 == 0 else (far, near)

            def run(ids, section, cells, whole, part, *ends):
                whole = lax.ppermute(whole, ("blk", "theta"), whole_route)
                part = lax.ppermute(part, ("blk", "theta"), part_route)
                low_radial, high_radial, left_high, right_low = halos(*ends)
                acc, split = inner(ids, section, cells, bands, low_radial, high_radial)
                return acc, split, whole, part, left_high, right_low

            return run

        case = (turns - 1) * 2 + second_half
        branches = [branch(i) for i in range((slabs - 1) * 2)]
        ends = (radial_low, radial_high, theta_low, theta_high)
        acc, split, whole, part, left_high, right_low = lax.switch(
            case, branches, ids, section, cells, whole, part, *ends
        )
    out = tail(ids, turn, section, base, acc, split, order, whole, part, theta_own, left_high, right_low)
    return from_tile_rows(out, bands)


def solution(mesh):
    in_specs = (P(None, "blk", "radial", "theta"), P(None, "blk", "radial", "theta"), P())
    out_specs = P(None, "blk", "radial", "theta")
    return jax.shard_map(shards, mesh=mesh, in_specs=in_specs, out_specs=out_specs, check_vma=False)
```

```python
import functools

import jax
import jax.numpy as jnp
from jax import lax
from jax.experimental import pallas as pl
from jax.experimental.pallas import tpu as pltpu
from jax.sharding import PartitionSpec as P

gamma_ratio = 1.4
weno_epsilon = 1e-06
step_ratio = 0.12
lanes = 128
ghosts = 3
group = 16
batch = 2
flux_scale = 12.0
flux_factor = -0.25 * step_ratio / flux_scale
most_slabs = 8
vmem_bytes = 32 * 1024 * 1024

axial_order = (0, 1, 2, 3, 4)
radial_order = (0, 3, 1, 2, 4)
theta_order = (0, 2, 1, 3, 4)


def inverse(value):
    guess = pl.reciprocal(value, approx=True)
    return guess * (2.0 - value * guess)


def cell_terms(state):
    density, normal, first, second, energy = state
    inv = inverse(density)
    speed = normal * inv
    kinetic = 0.5 * (normal * normal + first * first + second * second) * inv
    pressure = (gamma_ratio - 1.0) * (energy - kinetic)
    square = gamma_ratio * pressure * inv
    wave = jnp.abs(speed) + square * lax.rsqrt(square)
    flux = (normal, normal * speed + pressure, first * speed, second * speed, (energy + pressure) * speed)
    return flux, wave


def interface_terms(left, right):
    (state_l, flux_l, wave_l), (state_r, flux_r, wave_r) = left, right
    return (
        [r - l for l, r in zip(state_l, state_r)]
        + [r - l for l, r in zip(flux_l, flux_r)]
        + [0.5 * flux_scale * (r + l) for l, r in zip(flux_l, flux_r)]
        + [jnp.maximum(wave_l, wave_r)]
    )


def weno_terms(d0, d1, d2, d3, epsilon):
    e0 = d1 - d0
    e1 = d2 - d1
    e2 = d3 - d2
    f0 = e0 - e1
    f1 = e1 - e2
    t1 = 0.75 * d1
    t2 = 0.75 * d2
    shared = t1 * d2 + epsilon
    low = e0 * e0 + (t1 * f0 + shared)
    mid = e1 * e1 + shared
    high = e2 * e2 + (t2 * f1 + shared)
    x = mid * pl.reciprocal(low, approx=True)
    y = mid * pl.reciprocal(high, approx=True)
    weight_low = x * x
    weight_high = 1.5 * (y * y)
    total = 0.5 * weight_low + (weight_high + 3.0)
    return (weight_low * f0 + weight_high * f1) * pl.reciprocal(total, approx=True)


def face_terms(diff_state, diff_flux, sum_state, sum_flux, wave):
    inv = inverse(sum_state(0))
    un, va, vb, specific = (inv * sum_state(k) for k in range(1, 5))
    half = 0.5 * (un * un + va * va + vb * vb)
    internal = specific - half
    square = gamma_ratio * (gamma_ratio - 1.0) * internal
    inv_sound = lax.rsqrt(square)
    sound = square * inv_sound
    factor = (gamma_ratio - 1.0) * inv_sound * inv_sound
    enthalpy = specific + (gamma_ratio - 1.0) * internal

    def project(dens, norm, first, second, energy):
        sn = norm - un * dens
        sa = first - va * dens
        sb = second - vb * dens
        even = factor * (energy - half * dens - un * sn - va * sa - vb * sb)
        odd = inv_sound * sn
        return even - odd, dens - even, sa, sb, even + odd

    def side(vectors):
        chars = [project(*vector) for vector in vectors]
        return [weno_terms(*(c[k] for c in chars), weno_epsilon * (12.0 if k in (0, 4) else 3.0)) for k in range(5)]

    fluxes = [[diff_flux[s](c) for c in range(5)] for s in range(5)]
    damped = [[wave * diff_state[s](c) for c in range(5)] for s in range(5)]
    plus = [[f + d for f, d in zip(fluxes[s], damped[s])] for s in range(4)]
    forward = side(plus)
    minus = [[f - d for f, d in zip(fluxes[s], damped[s])] for s in range(4, 0, -1)]
    backward = side(minus)
    central = [sum_flux(c) + (plus[1][c] - plus[2][c]) + (minus[2][c] - minus[1][c]) for c in range(5)]
    wave_minus, entropy, sa, sb, wave_plus = (f - b for f, b in zip(forward, backward))
    even = 0.5 * (wave_plus + wave_minus)
    odd = sound * (0.5 * (wave_plus - wave_minus))
    carried = even + entropy
    return (
        central[0] + carried,
        central[1] + un * carried + odd,
        central[2] + va * carried + sa,
        central[3] + vb * carried + sb,
        central[4] + enthalpy * even + un * odd + half * entropy + va * sa + vb * sb,
    )


def face_from(load, sum_state):
    return face_terms(
        [functools.partial(lambda s, c: load(c, s), s) for s in range(5)],
        [functools.partial(lambda s, c: load(5 + c, s), s) for s in range(5)],
        sum_state,
        lambda c: load(10 + c, 2),
        load(15, 2),
    )


def with_terms(state):
    return (state, *cell_terms(state))


def lane_index(shape):
    return lax.broadcasted_iota(jnp.int32, shape, len(shape) - 1)


def tile_rows(state):
    components, planes, bands, width = state.shape
    split = state.reshape(components, planes, bands, width // lanes, lanes)
    return split.transpose(0, 1, 3, 2, 4).reshape(components, planes, -1, lanes)


def from_tile_rows(rows, bands):
    components, planes, count, _ = rows.shape
    split = rows.reshape(components, planes, count // bands, bands, lanes)
    return split.transpose(0, 1, 3, 2, 4).reshape(components, planes, bands, -1)


def loop(count, body):
    def step(i, carry):
        body(i)
        return carry

    lax.fori_loop(0, count, step, 0)


def make_order(order):
    tiles = order.shape[0] // lanes
    row = lax.broadcasted_iota(jnp.int32, (lanes, lanes), 0)
    column = lax.broadcasted_iota(jnp.int32, (lanes, lanes), 1)
    for t in range(tiles):
        meets = column - row // tiles == t * lanes // tiles
        key = jnp.where(meets, row % tiles, -1).astype(jnp.float32).astype(jnp.bfloat16)
        for j in range(tiles):
            block = jnp.where(key == j, 1.0, 0.0).astype(jnp.bfloat16)
            order[t * lanes : (t + 1) * lanes, j * lanes : (j + 1) * lanes] = block


def store_split(split, n, tile, values):
    high = values.astype(jnp.bfloat16)
    low = (values - high.astype(jnp.float32)).astype(jnp.bfloat16)
    flat = values.shape[0]
    start = pl.multiple_of(n * flat, 16)
    split[pl.ds(start, flat), tile * lanes : (tile + 1) * lanes] = high
    split[pl.ds(5 * flat + start, flat), tile * lanes : (tile + 1) * lanes] = low


def reorder(section, cells, split, order):
    _, tiles, planes, bands, _ = cells.shape
    flat = planes * bands
    for n, c in enumerate(theta_order):
        for t in range(tiles):
            store_split(split, n, t, section[c, :, t * bands : (t + 1) * bands].reshape(flat, lanes))
    both = jnp.dot(split[...], order[...], preferred_element_type=jnp.float32)
    both = both[: 5 * flat] + both[5 * flat :]
    for n in range(5):
        for j in range(tiles):
            part = both[n * flat : (n + 1) * flat, j * lanes : (j + 1) * lanes]
            cells[n, j] = part.reshape(planes, bands, lanes)


def restore(split, order, planes, acc):
    tiles = order.shape[0] // lanes
    flat = split.shape[0] // 10
    bands = flat // planes
    both = lax.dot_general(split[...], order[...], (((1,), (1,)), ((), ())), preferred_element_type=jnp.float32)
    both = both[: 5 * flat] + both[5 * flat :]
    for n, c in enumerate(theta_order):
        for t in range(tiles):
            part = both[n * flat : (n + 1) * flat, t * lanes : (t + 1) * lanes]
            acc[c, 1 : planes + 1, t * bands : (t + 1) * bands] = part.reshape(planes, bands, lanes)


def pack_kernel(
    bands, ids, turn, section,
    held, even_theta, odd_theta, theta_own, even_radial, odd_radial, whole, part, cells, order, split
):
    planes, rows = section.shape[1:3]
    tiles = rows // bands
    facing = jnp.where(ids[0] == 0, planes - ghosts, 0)
    part_at = pl.multiple_of(turn[2] * part.shape[2], bands)
    even = ids[1] % 2 == 0
    even_slab = ids[3] % 2 == 0
    lane = lane_index((bands, lanes))

    def component(c):
        held[c] = section[c]
        for i in range(ghosts):
            whole[c, i] = section[c, facing + i]
            part[c, i] = section[c, facing + i, pl.ds(part_at, part.shape[2])]
        own = jnp.full((bands, lanes), (1.0, 0.0, 0.0, 0.0, 3.0)[c], jnp.float32)
        low = high = own
        for p in range(planes):
            at = lane - group * p
            first = section[c, p, 0:bands]
            last = section[c, p, rows - bands : rows]
            own_first = pltpu.roll(first, group * p + ghosts, 1)
            own_last = pltpu.roll(last, group * p + group - ghosts, 1)
            sent_low = pltpu.roll(first, group * p + group - ghosts, 1)
            sent_high = pltpu.roll(last, group * p + ghosts, 1)
            own = jnp.where((at >= ghosts) & (at < group // 2), own_first, own)
            own = jnp.where((at >= group // 2) & (at < group - ghosts), own_last, own)
            low = jnp.where((at >= group - ghosts) & (at < group), sent_low, low)
            high = jnp.where((at >= 0) & (at < ghosts), sent_high, high)
        theta_own[c] = own
        even_theta[c] = jnp.where(even_slab, high, low)
        odd_theta[c] = jnp.where(even_slab, low, high)

        for p in range(planes):
            for k in range(ghosts):
                low = section[c, p, pl.ds(k, tiles, stride=bands)]
                high = section[c, p, pl.ds(bands - ghosts + k, tiles, stride=bands)]
                even_radial[c, p, k] = jnp.where(even, high, low)
                odd_radial[c, p, k] = jnp.where(even, low, high)

    for c in range(5):
        component(c)
    make_order(order)
    reorder(section, cells, split, order)


def pack(ids, turn, section, bands):
    _, planes, rows, _ = section.shape
    smem = pl.BlockSpec(memory_space=pltpu.SMEM)
    vmem = pl.BlockSpec(memory_space=pltpu.VMEM)
    array = lambda *shape: jax.ShapeDtypeStruct(shape, jnp.float32)
    theta = array(5, bands, lanes)
    radial = array(5, planes, ghosts, rows // bands, lanes)
    mortar = [array(5, ghosts, rows, lanes), array(5, ghosts, rows // 2, lanes)]
    width = rows // bands * lanes
    cells = array(5, rows // bands, planes, bands, lanes)
    order = jax.ShapeDtypeStruct((width, width), jnp.bfloat16)
    return pl.pallas_call(
        functools.partial(pack_kernel, bands),
        in_specs=[smem, smem, vmem],
        out_specs=[vmem] * 10,
        out_shape=(array(*section.shape), theta, theta, theta, radial, radial, *mortar, cells, order),
        scratch_shapes=[pltpu.VMEM((10 * planes * bands, width), jnp.bfloat16)],
        compiler_params=pltpu.CompilerParams(vmem_limit_bytes=vmem_bytes),
        name="pack",
    )(ids, turn, section)


def inner_kernel(
    bands, ids, section, cells, even_radial, odd_radial, base_state, acc, split, lead, terms, fluxes, base, sem
):
    planes = section.shape[1]
    loading = pltpu.make_async_copy(base_state, base, sem)
    loading.start()
    radial_pass(bands, ids, section, even_radial, odd_radial, acc, lead, terms, fluxes)
    theta_pass(cells, lead, terms, fluxes, split)
    axial_inner(ids, section, acc, lead, terms)
    loading.wait()
    for c in range(5):
        change = flux_factor * acc[c, 1 : planes + 1]
        acc[c, 1 : planes + 1] = 0.75 * base[c] + (0.25 * section[c] + change)


def lead_faces(lead, cells, columns, terms, emit):
    def column_group(g):
        p = g * batch

        def state(r):
            return [lead[n, r, pl.ds(p, batch)] for n in range(5)]

        def cell(r):
            here = state(r)
            flux, wave = cell_terms(here)
            return here, flux, wave

        def keep(r, values):
            for n, value in enumerate((*values[1], values[2])):
                terms[16 + n, r] = value

        def interface(r, right):
            left = (state(r), [terms[16 + n, r] for n in range(5)], terms[21, r])
            for n, value in enumerate(interface_terms(left, right)):
                terms[n, r] = value

        left = cell(0)
        for r in range(5):
            right = cell(r + 1)
            for n, value in enumerate(interface_terms(left, right)):
                terms[n, r] = value
            left = right
        keep(5, left)

        def face(r):
            flux = face_from(
                lambda n, s: terms[n, r + s],
                lambda n: lead[n, r + 2, pl.ds(p, batch)] + lead[n, r + 3, pl.ds(p, batch)],
            )
            emit(r, p, flux)
            right = cell(jnp.minimum(r + 6, cells - 1))
            interface(r + 5, right)
            keep(r + 6, right)

        loop(cells - 5, face)

    loop(columns // batch, column_group)


def keep_flux(fluxes, r, p, flux):
    for n, value in enumerate(flux):
        fluxes[n, r, pl.ds(p, batch)] = value


def radial_pass(bands, ids, section, even_radial, odd_radial, acc, lead, terms, fluxes):
    planes, rows = section.shape[1:3]
    tiles = rows // bands
    at_inner = ids[1] == 0
    at_outer = ids[1] == ids[2] - 1
    even = ids[1] % 2 == 0

    def spread(p):
        for n, c in enumerate(radial_order):
            band = [section[c, p, pl.ds(r, tiles, stride=bands)] for r in range(bands)]
            sign = -1.0 if c == 3 else 1.0
            for r in range(bands):
                lead[n, r + ghosts, p] = band[r]
            for k in range(ghosts):
                one, two = even_radial[c, p, k], odd_radial[c, p, k]
                low, high = jnp.where(even, two, one), jnp.where(even, one, two)
                lead[n, k, p] = jnp.where(at_inner, sign * band[ghosts - 1 - k], low)
                lead[n, bands + ghosts + k, p] = jnp.where(at_outer, sign * band[bands - 1 - k], high)

    loop(planes, spread)
    lead_faces(lead, bands + 2 * ghosts, planes, terms, functools.partial(keep_flux, fluxes))

    def gather(p):
        for n, c in enumerate(radial_order):
            for r in range(bands):
                acc[c, p + 1, pl.ds(r, tiles, stride=bands)] = fluxes[n, r + 1, p] - fluxes[n, r, p]

    loop(planes, gather)


def theta_pass(cells, lead, terms, fluxes, split):
    _, tiles, planes, bands, _ = cells.shape

    def fill(n):
        for j in range(tiles):
            lead[n, ghosts + j, 0:planes] = cells[n, j]
        for k in range(ghosts):
            lead[n, k, 0:planes] = pltpu.roll(cells[n, tiles - ghosts + k], 1, 2)
            lead[n, ghosts + tiles + k, 0:planes] = pltpu.roll(cells[n, k], lanes - 1, 2)

    loop(5, fill)
    lead_faces(lead, tiles + 2 * ghosts, planes, terms, functools.partial(keep_flux, fluxes))
    lane = lane_index((planes, bands, lanes))

    def changes(n):
        before = None
        for r in range(tiles + 1):
            flux = fluxes[n, r, 0:planes]
            if r < ghosts:
                flux = jnp.where(lane == 0, 0.0, flux)
            if r > tiles - ghosts:
                flux = jnp.where(lane == lanes - 1, 0.0, flux)
            if r > 0:
                store_split(split, n, r - 1, (flux - before).reshape(planes * bands, lanes))
            before = flux

    loop(5, changes)


def axial_faces(count, first, acc, lead, terms):
    tiles, bands = lead.shape[2:4]

    def emit(i, p, flux):
        place = pl.ds(pl.multiple_of(p * bands, bands), batch * bands)
        for c, value in zip(axial_order, flux):
            value = value.reshape(batch * bands, lanes)
            acc[c, first + i, place] += value
            acc[c, first + i + 1, place] -= value

    lead_faces(lead, count + 5, tiles, terms, emit)


def axial_inner(ids, section, acc, lead, terms):
    planes = section.shape[1]
    tiles, bands = lead.shape[2:4]
    first = jnp.where(ids[0] == 0, 0, ghosts)
    count = planes + 1 - ghosts
    for c in range(5):
        acc[c, 0] = jnp.zeros(acc.shape[2:], jnp.float32)
        acc[c, planes + 1] = jnp.zeros(acc.shape[2:], jnp.float32)

    def fill(i):
        plane = jnp.clip(first + i - ghosts, 0, planes - 1)
        for c in axial_order:
            lead[c, i] = section[c, plane].reshape(tiles, bands, lanes)

    loop(count + 5, fill)
    axial_faces(count, first, acc, lead, terms)


def inner(ids, section, cells, bands, even_radial, odd_radial, base):
    _, planes, rows, _ = section.shape
    tiles = rows // bands
    depth = max(bands, tiles) + 2 * ghosts
    across = max(planes, tiles)
    vmem = pl.BlockSpec(memory_space=pltpu.VMEM)
    faces = (planes + 1) * tiles + planes * (tiles + bands + 2)
    return pl.pallas_call(
        functools.partial(inner_kernel, bands),
        in_specs=[pl.BlockSpec(memory_space=pltpu.SMEM)] + [vmem] * 4 + [pl.BlockSpec(memory_space=pl.ANY)],
        out_shape=(
            jax.ShapeDtypeStruct((5, planes + 2, rows, lanes), jnp.float32),
            jax.ShapeDtypeStruct((10 * planes * bands, tiles * lanes), jnp.bfloat16),
        ),
        scratch_shapes=[
            pltpu.VMEM((5, depth, across, 8, lanes), jnp.float32),
            pltpu.VMEM((22, depth + 1, batch, 8, lanes), jnp.float32),
            pltpu.VMEM((5, depth - 5, planes, 8, lanes), jnp.float32),
            pltpu.VMEM(section.shape, jnp.float32),
            pltpu.SemaphoreType.DMA(()),
        ],
        compiler_params=pltpu.CompilerParams(vmem_limit_bytes=vmem_bytes),
        cost_estimate=pl.CostEstimate(
            flops=faces * 8 * lanes * 700, bytes_accessed=section.size * 16, transcendentals=faces * 8 * lanes * 30
        ),
        name="inner",
    )(ids, section, cells, even_radial, odd_radial, base)


def mortar_planes(turn, window, lead, at):
    tiles, bands = lead.shape[2:4]
    skipped = turn[0] // lanes
    rest = turn[0] % lanes
    fraction = 0.25 * turn[1].astype(jnp.float32)
    source = lax.broadcasted_iota(jnp.int32, (2 * lanes, lanes), 0)
    target = lax.broadcasted_iota(jnp.int32, (2 * lanes, lanes), 1)
    gap = source + target - (lanes - 1 + rest)
    blend = jnp.where(gap == 0, 1.0 - fraction, jnp.where(gap == 1, fraction, 0.0)).astype(jnp.bfloat16)
    blend = jnp.concatenate([blend[:lanes]] * 3 + [blend[lanes:]] * 3, axis=0)

    def parts_of(tile):
        start = pl.multiple_of((tile + skipped) * bands, bands)
        cells = window[:, :, pl.ds(start, bands)].reshape(5 * ghosts * bands, lanes)
        parts = []
        for _ in range(3):
            parts.append(cells.astype(jnp.bfloat16))
            cells = cells - parts[-1].astype(jnp.float32)
        return parts

    after = parts_of(tiles)
    for t in range(tiles):
        here = parts_of(tiles - 1 - t)
        mixed = jnp.dot(jnp.concatenate(here + after, axis=1), blend, preferred_element_type=jnp.float32)
        mixed = mixed.reshape(5, ghosts, bands, lanes)
        for c in range(5):
            lead[c, pl.ds(at, ghosts), t] = -mixed[c] if c == 2 else mixed[c]
        after = here


def theta_edges(even, theta_own, even_theta, odd_theta, acc):
    planes, rows = acc.shape[1] - 2, acc.shape[2]
    bands = theta_own.shape[1]
    lane = lane_index((bands, lanes))
    at = lane % group
    inside = lane < group * planes
    cells = []
    for c in theta_order:
        left = jnp.where(even, odd_theta[c], even_theta[c])
        right = jnp.where(even, even_theta[c], odd_theta[c])
        own = jnp.where(inside & (at >= group - ghosts), right, theta_own[c])
        cells.append(jnp.where(inside & (at < ghosts), left, own))
    turn = lambda value, shift: pltpu.roll(value, -shift % lanes, 1) if shift else value
    after = [turn(v, 1) for v in cells]
    terms = interface_terms(with_terms(cells), with_terms(after))
    flux = face_from(lambda n, s: turn(terms[n], s - 2), lambda n: cells[n] + after[n])
    low, high = ghosts - 1, group // 2 + 2
    wanted = inside & (((at >= low) & (at < low + 3)) | ((at >= high) & (at < high + 3)))
    flux = [jnp.where(wanted, value, 0.0) for value in flux]
    changes = [value - turn(value, -1) for value in flux]

    for p in range(planes):
        for c, change in zip(theta_order, changes):
            first = turn(change, group * p + ghosts)
            last = turn(change, group * p + high + ghosts - lanes)
            acc[c, p + 1, 0:bands] += jnp.where(lane < ghosts, first, 0.0)
            acc[c, p + 1, rows - bands : rows] += jnp.where(lane >= lanes - ghosts, last, 0.0)


def tail_kernel(
    ids, turn, section, acc, split, order, whole, part, theta_own, even_theta, odd_theta, out_state,
    more, lead, terms, window, out, sems
):
    planes = section.shape[1]
    tiles, bands = lead.shape[2:4]
    whole_at = pl.multiple_of(jnp.where(turn[2] == 0, 0, part.shape[2]), bands)
    part_at = pl.multiple_of(jnp.where(turn[2] == 0, whole.shape[2], 0), bands)
    arriving = [
        pltpu.make_async_copy(whole, window.at[:, :, pl.ds(whole_at, whole.shape[2])], sems.at[1]),
        pltpu.make_async_copy(part, window.at[:, :, pl.ds(part_at, part.shape[2])], sems.at[2]),
    ]
    for copy in arriving:
        copy.start()
    front = ids[0] == 0
    kept = planes - 1
    own = jnp.where(front, 1, 0)
    own_at = jnp.where(front, 0, ghosts)
    ghost_at = jnp.where(front, kept, 0)
    first = jnp.where(front, planes + 1 - ghosts, 0)

    def fill(i):
        for c in axial_order:
            lead[c, own_at + i] = section[c, own + i].reshape(tiles, bands, lanes)

    loop(kept, fill)

    for c in range(5):
        more[c, 0] = jnp.zeros(more.shape[2:], jnp.float32)
        more[c, planes + 1] = jnp.zeros(more.shape[2:], jnp.float32)
    restore(split, order, planes, more)
    theta_edges(ids[3] % 2 == 0, theta_own, even_theta, odd_theta, more)
    for copy in arriving:
        copy.wait()
    mortar_planes(turn, window, lead, ghost_at)
    axial_faces(ghosts, first, more, lead, terms)

    storing = [pltpu.make_async_copy(out.at[c], out_state.at[c], sems.at[c]) for c in range(5)]
    for c in range(5):
        out[c] = acc[c, 1 : planes + 1] + flux_factor * more[c, 1 : planes + 1]
        storing[c].start()
    for copy in storing:
        copy.wait()


def tail(ids, turn, section, acc, split, order, whole, part, theta_own, even_theta, odd_theta):
    _, planes, rows, _ = section.shape
    bands = theta_own.shape[1]
    tiles = rows // bands
    smem = pl.BlockSpec(memory_space=pltpu.SMEM)
    vmem = pl.BlockSpec(memory_space=pltpu.VMEM)
    anywhere = pl.BlockSpec(memory_space=pl.ANY)
    return pl.pallas_call(
        tail_kernel,
        in_specs=[smem, smem, vmem, vmem, vmem, vmem, anywhere, anywhere, vmem, vmem, vmem],
        out_specs=anywhere,
        out_shape=jax.ShapeDtypeStruct(section.shape, jnp.float32),
        scratch_shapes=[
            pltpu.VMEM(acc.shape, jnp.float32),
            pltpu.VMEM((5, planes - 1 + ghosts, tiles, bands, lanes), jnp.float32),
            pltpu.VMEM((22, 2 * ghosts + 3, batch, bands, lanes), jnp.float32),
            pltpu.VMEM((5, ghosts, whole.shape[2] + part.shape[2], lanes), jnp.float32),
            pltpu.VMEM(section.shape, jnp.float32),
            pltpu.SemaphoreType.DMA((5,)),
        ],
        compiler_params=pltpu.CompilerParams(vmem_limit_bytes=vmem_bytes),
        name="tail",
    )(ids, turn, section, acc, split, order, whole, part, theta_own, even_theta, odd_theta)


def slab_routes(turns, slabs):
    both = []
    for ahead in (1, 0):
        both.append(
            [
                (block * slabs + slab, (1 - block) * slabs + (turns - ahead - slab) % slabs)
                for block in range(2)
                for slab in range(slabs)
            ]
        )
    return both


def shards(base_state, section_state, rotor_step):
    bands, width = section_state.shape[2:]
    rows = width // lanes * bands
    slabs = lax.axis_size("theta")
    slab = lax.axis_index("theta")
    parts = lax.axis_size("radial")
    ids = jnp.stack([lax.axis_index("blk"), lax.axis_index("radial"), parts, slab]).astype(jnp.int32)
    step = rotor_step[0]
    offset = step // 4
    turns = offset // width
    start = offset % width
    second_half = start // (width // 2)
    turn = jnp.stack([start % (width // 2), step % 4, second_half])
    base, section = tile_rows(base_state), tile_rows(section_state)
    held, even_theta, odd_theta, theta_own, even_radial, odd_radial, whole, part, cells, order = pack(
        ids, turn, section, bands
    )

    def pairs(count, first, closed):
        ends = range(first, count if closed else count - 1, 2)
        return [pair for i in ends for pair in ((i, (i + 1) % count), ((i + 1) % count, i))]

    def halos(even_radial, odd_radial, even_theta, odd_theta):
        return (
            lax.ppermute(even_radial, "radial", pairs(parts, 0, False)),
            lax.ppermute(odd_radial, "radial", pairs(parts, 1, False)),
            lax.ppermute(even_theta, "theta", pairs(slabs, 0, True)),
            lax.ppermute(odd_theta, "theta", pairs(slabs, 1, True)),
        )

    if slabs > most_slabs:
        even_radial, odd_radial, even_theta, odd_theta = halos(even_radial, odd_radial, even_theta, odd_theta)
        facing = lax.ppermute(whole, "blk", [(0, 1), (1, 0)])
        ring = lax.all_gather(facing, "theta", axis=2, tiled=True)
        ring = jnp.concatenate([ring, ring, ring[:, :, : rows // 2]], axis=2)
        begin = (turns - 1 - slab) % slabs * rows + second_half * (rows // 2)
        whole = lax.dynamic_slice_in_dim(ring, begin, rows, 2)
        part = lax.dynamic_slice_in_dim(ring, begin + rows, rows // 2, 2)
        turn = turn.at[2].set(0)
        acc, split = inner(ids, held, cells, bands, even_radial, odd_radial, base)
    else:

        def branch(case):
            near, far = slab_routes(case // 2 + 1, slabs)
            whole_route, part_route = (near, far) if case % 2 == 0 else (far, near)

            def run(ids, held, cells, base, whole, part, *ends):
                whole = lax.ppermute(whole, ("blk", "theta"), whole_route)
                part = lax.ppermute(part, ("blk", "theta"), part_route)
                even_radial, odd_radial, *ends = halos(*ends)
                acc, split = inner(ids, held, cells, bands, even_radial, odd_radial, base)
                return acc, split, whole, part, *ends

            return run

        case = (turns - 1) * 2 + second_half
        branches = [branch(i) for i in range((slabs - 1) * 2)]
        ends = (even_radial, odd_radial, even_theta, odd_theta)
        acc, split, whole, part, even_theta, odd_theta = lax.switch(
            case, branches, ids, held, cells, base, whole, part, *ends
        )
    out = tail(ids, turn, section, acc, split, order, whole, part, theta_own, even_theta, odd_theta)
    return from_tile_rows(out, bands)


def solution(mesh):
    in_specs = (P(None, "blk", "radial", "theta"), P(None, "blk", "radial", "theta"), P())
    out_specs = P(None, "blk", "radial", "theta")
    return jax.shard_map(shards, mesh=mesh, in_specs=in_specs, out_specs=out_specs, check_vma=False)
```

```python
import functools

import jax
import jax.numpy as jnp
from jax import lax
from jax.experimental import pallas as pl
from jax.experimental.pallas import tpu as pltpu
from jax.sharding import PartitionSpec as P

gamma_ratio = 1.4
weno_epsilon = 1e-06
step_ratio = 0.12
lanes = 128
ghosts = 3
group = 16
plane_batch = 3
tile_batch = 2
flux_scale = 12.0
flux_factor = -0.25 * step_ratio / flux_scale
most_slabs = 8
vmem_bytes = 32 * 1024 * 1024

axial_order = (0, 1, 2, 3, 4)
radial_order = (0, 3, 1, 2, 4)
theta_order = (0, 2, 1, 3, 4)


def inverse(value):
    guess = pl.reciprocal(value, approx=True)
    return guess * (2.0 - value * guess)


def cell_terms(state):
    density, normal, first, second, energy = state
    inv = inverse(density)
    speed = normal * inv
    kinetic = 0.5 * (normal * normal + first * first + second * second) * inv
    pressure = (gamma_ratio - 1.0) * (energy - kinetic)
    square = gamma_ratio * pressure * inv
    wave = jnp.abs(speed) + square * lax.rsqrt(square)
    flux = (normal, normal * speed + pressure, first * speed, second * speed, (energy + pressure) * speed)
    return flux, wave


def interface_terms(left, right):
    (state_l, flux_l, wave_l), (state_r, flux_r, wave_r) = left, right
    return (
        [r - l for l, r in zip(state_l, state_r)]
        + [r - l for l, r in zip(flux_l, flux_r)]
        + [0.5 * flux_scale * (r + l) for l, r in zip(flux_l, flux_r)]
        + [jnp.maximum(wave_l, wave_r)]
    )


def weno_terms(d0, d1, d2, d3, epsilon):
    e0 = d1 - d0
    e1 = d2 - d1
    e2 = d3 - d2
    f0 = e0 - e1
    f1 = e1 - e2
    t1 = 0.75 * d1
    t2 = 0.75 * d2
    shared = t1 * d2 + epsilon
    low = e0 * e0 + (t1 * f0 + shared)
    mid = e1 * e1 + shared
    high = e2 * e2 + (t2 * f1 + shared)
    x = mid * pl.reciprocal(low, approx=True)
    y = mid * pl.reciprocal(high, approx=True)
    weight_low = x * x
    weight_high = 1.5 * (y * y)
    total = 0.5 * weight_low + (weight_high + 3.0)
    return (weight_low * f0 + weight_high * f1) * pl.reciprocal(total, approx=True)


def face_terms(diff_state, diff_flux, sum_state, sum_flux, wave):
    inv = inverse(sum_state(0))
    un, va, vb, specific = (inv * sum_state(k) for k in range(1, 5))
    half = 0.5 * (un * un + va * va + vb * vb)
    internal = specific - half
    square = gamma_ratio * (gamma_ratio - 1.0) * internal
    inv_sound = lax.rsqrt(square)
    sound = square * inv_sound
    factor = (gamma_ratio - 1.0) * inv_sound * inv_sound
    enthalpy = specific + (gamma_ratio - 1.0) * internal

    def project(dens, norm, first, second, energy):
        sn = norm - un * dens
        sa = first - va * dens
        sb = second - vb * dens
        even = factor * (energy - half * dens - un * sn - va * sa - vb * sb)
        odd = inv_sound * sn
        return even - odd, dens - even, sa, sb, even + odd

    def side(vectors):
        chars = [project(*vector) for vector in vectors]
        return [weno_terms(*(c[k] for c in chars), weno_epsilon * (12.0 if k in (0, 4) else 3.0)) for k in range(5)]

    fluxes = [[diff_flux[s](c) for c in range(5)] for s in range(5)]
    damped = [[wave * diff_state[s](c) for c in range(5)] for s in range(5)]
    plus = [[f + d for f, d in zip(fluxes[s], damped[s])] for s in range(4)]
    forward = side(plus)
    minus = [[f - d for f, d in zip(fluxes[s], damped[s])] for s in range(4, 0, -1)]
    backward = side(minus)
    central = [sum_flux(c) + (plus[1][c] - plus[2][c]) + (minus[2][c] - minus[1][c]) for c in range(5)]
    wave_minus, entropy, sa, sb, wave_plus = (f - b for f, b in zip(forward, backward))
    even = 0.5 * (wave_plus + wave_minus)
    odd = sound * (0.5 * (wave_plus - wave_minus))
    carried = even + entropy
    return (
        central[0] + carried,
        central[1] + un * carried + odd,
        central[2] + va * carried + sa,
        central[3] + vb * carried + sb,
        central[4] + enthalpy * even + un * odd + half * entropy + va * sa + vb * sb,
    )


def face_from(load, sum_state):
    return face_terms(
        [functools.partial(lambda s, c: load(c, s), s) for s in range(5)],
        [functools.partial(lambda s, c: load(5 + c, s), s) for s in range(5)],
        sum_state,
        lambda c: load(10 + c, 2),
        load(15, 2),
    )


def with_terms(state):
    return (state, *cell_terms(state))


def lane_index(shape):
    return lax.broadcasted_iota(jnp.int32, shape, len(shape) - 1)


def tile_rows(state):
    components, planes, bands, width = state.shape
    split = state.reshape(components, planes, bands, width // lanes, lanes)
    return split.transpose(0, 1, 3, 2, 4).reshape(components, planes, -1, lanes)


def from_tile_rows(rows, bands):
    components, planes, count, _ = rows.shape
    split = rows.reshape(components, planes, count // bands, bands, lanes)
    return split.transpose(0, 1, 3, 2, 4).reshape(components, planes, bands, -1)


def loop(count, body):
    def step(i, carry):
        body(i)
        return carry

    lax.fori_loop(0, count, step, 0)


def make_order(order):
    tiles = order.shape[0] // lanes
    one, zero = jnp.ones((lanes, lanes), jnp.bfloat16), jnp.zeros((lanes, lanes), jnp.bfloat16)
    row = lax.broadcasted_iota(jnp.int32, (lanes, lanes), 0)
    column = lax.broadcasted_iota(jnp.int32, (lanes, lanes), 1)
    for t in range(tiles):
        meets = column - row // tiles == t * lanes // tiles
        key = jnp.where(meets, row % tiles, -1).astype(jnp.float32).astype(jnp.bfloat16)
        for j in range(tiles):
            block = jnp.where(key == j, one, zero)
            order[t * lanes : (t + 1) * lanes, j * lanes : (j + 1) * lanes] = block


def store_split(split, n, tile, values):
    high = values.astype(jnp.bfloat16)
    low = (values - high.astype(jnp.float32)).astype(jnp.bfloat16)
    flat = values.shape[0]
    start = pl.multiple_of(n * flat, 16)
    split[pl.ds(start, flat), tile * lanes : (tile + 1) * lanes] = high
    split[pl.ds(5 * flat + start, flat), tile * lanes : (tile + 1) * lanes] = low


def reorder(section, cells, split, order):
    _, tiles, planes, bands, _ = cells.shape
    flat = planes * bands
    for n, c in enumerate(theta_order):
        for t in range(tiles):
            store_split(split, n, t, section[c, :, t * bands : (t + 1) * bands].reshape(flat, lanes))
    both = jnp.dot(split[...], order[...], preferred_element_type=jnp.float32)
    both = both[: 5 * flat] + both[5 * flat :]
    for n in range(5):
        for j in range(tiles):
            part = both[n * flat : (n + 1) * flat, j * lanes : (j + 1) * lanes]
            cells[n, j] = part.reshape(planes, bands, lanes)


def restore(split, order, planes, acc):
    tiles = order.shape[0] // lanes
    flat = split.shape[0] // 10
    bands = flat // planes
    both = lax.dot_general(split[...], order[...], (((1,), (1,)), ((), ())), preferred_element_type=jnp.float32)
    both = both[: 5 * flat] + both[5 * flat :]
    for n, c in enumerate(theta_order):
        for t in range(tiles):
            part = both[n * flat : (n + 1) * flat, t * lanes : (t + 1) * lanes]
            acc[c, 1 : planes + 1, t * bands : (t + 1) * bands] = part.reshape(planes, bands, lanes)


def mortar_turn(step, width):
    start = lax.rem(lax.div(step, 4), width)
    return lax.rem(start, width // 2), lax.rem(step, 4), lax.div(start, width // 2)


def pack_kernel(
    bands, rotor_step, section,
    held, even_theta, odd_theta, theta_own, even_radial, odd_radial, whole, part, cells, order, split
):
    planes, rows = section.shape[1:3]
    tiles = rows // bands
    facing = jnp.where(lax.axis_index("blk") == 0, planes - ghosts, 0)
    turn = mortar_turn(rotor_step[0], tiles * lanes)
    part_at = pl.multiple_of(turn[2] * part.shape[2], bands)
    even = lax.rem(lax.axis_index("radial"), 2) == 0
    even_slab = lax.rem(lax.axis_index("theta"), 2) == 0
    lane = lane_index((bands, lanes))

    def component(c):
        held[c] = section[c]
        for i in range(ghosts):
            whole[c, i] = section[c, facing + i]
            part[c, i] = section[c, facing + i, pl.ds(part_at, part.shape[2])]
        own = jnp.full((bands, lanes), (1.0, 0.0, 0.0, 0.0, 3.0)[c], jnp.float32)
        low = high = own
        for p in range(planes):
            at = lane - group * p
            first = section[c, p, 0:bands]
            last = section[c, p, rows - bands : rows]
            own_first = pltpu.roll(first, group * p + ghosts, 1)
            own_last = pltpu.roll(last, group * p + group - ghosts, 1)
            sent_low = pltpu.roll(first, group * p + group - ghosts, 1)
            sent_high = pltpu.roll(last, group * p + ghosts, 1)
            own = jnp.where((at >= ghosts) & (at < group // 2), own_first, own)
            own = jnp.where((at >= group // 2) & (at < group - ghosts), own_last, own)
            low = jnp.where((at >= group - ghosts) & (at < group), sent_low, low)
            high = jnp.where((at >= 0) & (at < ghosts), sent_high, high)
        theta_own[c] = own
        even_theta[c] = jnp.where(even_slab, high, low)
        odd_theta[c] = jnp.where(even_slab, low, high)

        for p in range(planes):
            for k in range(ghosts):
                low = section[c, p, pl.ds(k, tiles, stride=bands)]
                high = section[c, p, pl.ds(bands - ghosts + k, tiles, stride=bands)]
                even_radial[c, p, k] = jnp.where(even, high, low)
                odd_radial[c, p, k] = jnp.where(even, low, high)

    for c in range(5):
        component(c)
    make_order(order)
    reorder(section, cells, split, order)


def pack(rotor_step, section, bands):
    _, planes, rows, _ = section.shape
    smem = pl.BlockSpec(memory_space=pltpu.SMEM)
    vmem = pl.BlockSpec(memory_space=pltpu.VMEM)
    array = lambda *shape: jax.ShapeDtypeStruct(shape, jnp.float32)
    theta = array(5, bands, lanes)
    radial = array(5, planes, ghosts, rows // bands, lanes)
    mortar = [array(5, ghosts, rows, lanes), array(5, ghosts, rows // 2, lanes)]
    width = rows // bands * lanes
    cells = array(5, rows // bands, planes, bands, lanes)
    order = jax.ShapeDtypeStruct((width, width), jnp.bfloat16)
    return pl.pallas_call(
        functools.partial(pack_kernel, bands),
        in_specs=[smem, vmem],
        out_specs=[vmem] * 10,
        out_shape=(array(*section.shape), theta, theta, theta, radial, radial, *mortar, cells, order),
        scratch_shapes=[pltpu.VMEM((10 * planes * bands, width), jnp.bfloat16)],
        compiler_params=pltpu.CompilerParams(vmem_limit_bytes=vmem_bytes),
        name="pack",
    )(rotor_step, section)


def inner_kernel(
    bands, section, cells, even_radial, odd_radial, base_state, acc, split, lead, terms, fluxes, base, sem
):
    planes = section.shape[1]
    loading = pltpu.make_async_copy(base_state, base, sem)
    loading.start()
    radial_pass(bands, section, even_radial, odd_radial, acc, lead, terms, fluxes)
    theta_pass(cells, lead, terms, fluxes, split)
    axial_inner(section, acc, lead, terms)
    loading.wait()
    for c in range(5):
        change = flux_factor * acc[c, 1 : planes + 1]
        acc[c, 1 : planes + 1] = 0.75 * base[c] + (0.25 * section[c] + change)


def lead_faces(lead, cells, columns, batch, terms, emit):
    def column_group(g):
        p = g * batch

        def state(r):
            return [lead[n, r, pl.ds(p, batch)] for n in range(5)]

        def cell(r):
            here = state(r)
            flux, wave = cell_terms(here)
            return here, flux, wave

        def keep(r, values):
            for n, value in enumerate((*values[1], values[2])):
                terms[16 + n, r, 0:batch] = value

        def interface(r, right):
            left = (state(r), [terms[16 + n, r, 0:batch] for n in range(5)], terms[21, r, 0:batch])
            for n, value in enumerate(interface_terms(left, right)):
                terms[n, r, 0:batch] = value

        left = cell(0)
        for r in range(5):
            right = cell(r + 1)
            for n, value in enumerate(interface_terms(left, right)):
                terms[n, r, 0:batch] = value
            left = right
        keep(5, left)

        def face(r):
            flux = face_from(
                lambda n, s: terms[n, r + s, 0:batch],
                lambda n: lead[n, r + 2, pl.ds(p, batch)] + lead[n, r + 3, pl.ds(p, batch)],
            )
            emit(r, p, flux)
            right = cell(jnp.minimum(r + 6, cells - 1))
            interface(r + 5, right)
            keep(r + 6, right)

        loop(cells - 5, face)

    loop(columns // batch, column_group)


def keep_flux(fluxes, r, p, flux):
    for n, value in enumerate(flux):
        fluxes[n, r, pl.ds(p, plane_batch)] = value


def radial_pass(bands, section, even_radial, odd_radial, acc, lead, terms, fluxes):
    planes, rows = section.shape[1:3]
    tiles = rows // bands
    index = lax.axis_index("radial")
    at_inner = index == 0
    at_outer = index == lax.axis_size("radial") - 1
    even = lax.rem(index, 2) == 0

    def spread(p):
        for n, c in enumerate(radial_order):
            band = [section[c, p, pl.ds(r, tiles, stride=bands)] for r in range(bands)]
            sign = -1.0 if c == 3 else 1.0
            for r in range(bands):
                lead[n, r + ghosts, p] = band[r]
            for k in range(ghosts):
                one, two = even_radial[c, p, k], odd_radial[c, p, k]
                low, high = jnp.where(even, two, one), jnp.where(even, one, two)
                lead[n, k, p] = jnp.where(at_inner, sign * band[ghosts - 1 - k], low)
                lead[n, bands + ghosts + k, p] = jnp.where(at_outer, sign * band[bands - 1 - k], high)

    loop(planes, spread)
    lead_faces(lead, bands + 2 * ghosts, planes, plane_batch, terms, functools.partial(keep_flux, fluxes))

    def gather(p):
        for n, c in enumerate(radial_order):
            for r in range(bands):
                acc[c, p + 1, pl.ds(r, tiles, stride=bands)] = fluxes[n, r + 1, p] - fluxes[n, r, p]

    loop(planes, gather)


def theta_pass(cells, lead, terms, fluxes, split):
    _, tiles, planes, bands, _ = cells.shape

    def fill(n):
        for j in range(tiles):
            lead[n, ghosts + j, 0:planes] = cells[n, j]
        for k in range(ghosts):
            lead[n, k, 0:planes] = pltpu.roll(cells[n, tiles - ghosts + k], 1, 2)
            lead[n, ghosts + tiles + k, 0:planes] = pltpu.roll(cells[n, k], lanes - 1, 2)

    loop(5, fill)
    lead_faces(lead, tiles + 2 * ghosts, planes, plane_batch, terms, functools.partial(keep_flux, fluxes))
    lane = lane_index((planes, bands, lanes))

    def changes(n):
        before = None
        for r in range(tiles + 1):
            flux = fluxes[n, r, 0:planes]
            if r < ghosts:
                flux = jnp.where(lane == 0, 0.0, flux)
            if r > tiles - ghosts:
                flux = jnp.where(lane == lanes - 1, 0.0, flux)
            if r > 0:
                store_split(split, n, r - 1, (flux - before).reshape(planes * bands, lanes))
            before = flux

    loop(5, changes)


def axial_faces(count, first, acc, lead, terms):
    tiles, bands = lead.shape[2:4]

    def emit(i, p, flux):
        place = pl.ds(pl.multiple_of(p * bands, bands), tile_batch * bands)
        for c, value in zip(axial_order, flux):
            value = value.reshape(tile_batch * bands, lanes)
            acc[c, first + i, place] += value
            acc[c, first + i + 1, place] -= value

    lead_faces(lead, count + 5, tiles, tile_batch, terms, emit)


def axial_inner(section, acc, lead, terms):
    planes = section.shape[1]
    tiles, bands = lead.shape[2:4]
    first = jnp.where(lax.axis_index("blk") == 0, 0, ghosts)
    count = planes + 1 - ghosts
    for c in range(5):
        acc[c, 0] = jnp.zeros(acc.shape[2:], jnp.float32)
        acc[c, planes + 1] = jnp.zeros(acc.shape[2:], jnp.float32)

    def fill(i):
        plane = jnp.clip(first + i - ghosts, 0, planes - 1)
        for c in axial_order:
            lead[c, i] = section[c, plane].reshape(tiles, bands, lanes)

    loop(count + 5, fill)
    axial_faces(count, first, acc, lead, terms)


def inner(section, cells, bands, even_radial, odd_radial, base):
    _, planes, rows, _ = section.shape
    tiles = rows // bands
    depth = max(bands, tiles) + 2 * ghosts
    across = max(planes, tiles)
    vmem = pl.BlockSpec(memory_space=pltpu.VMEM)
    faces = (planes + 1) * tiles + planes * (tiles + bands + 2)
    return pl.pallas_call(
        functools.partial(inner_kernel, bands),
        in_specs=[vmem] * 4 + [pl.BlockSpec(memory_space=pl.ANY)],
        out_shape=(
            jax.ShapeDtypeStruct((5, planes + 2, rows, lanes), jnp.float32),
            jax.ShapeDtypeStruct((10 * planes * bands, tiles * lanes), jnp.bfloat16),
        ),
        scratch_shapes=[
            pltpu.VMEM((5, depth, across, 8, lanes), jnp.float32),
            pltpu.VMEM((22, depth + 1, max(plane_batch, tile_batch), 8, lanes), jnp.float32),
            pltpu.VMEM((5, depth - 5, planes, 8, lanes), jnp.float32),
            pltpu.VMEM(section.shape, jnp.float32),
            pltpu.SemaphoreType.DMA(()),
        ],
        compiler_params=pltpu.CompilerParams(vmem_limit_bytes=vmem_bytes),
        cost_estimate=pl.CostEstimate(
            flops=faces * 8 * lanes * 700, bytes_accessed=section.size * 16, transcendentals=faces * 8 * lanes * 30
        ),
        name="inner",
    )(section, cells, even_radial, odd_radial, base)


def mortar_planes(turn, window, lead, at):
    tiles, bands = lead.shape[2:4]
    skipped = turn[0] // lanes
    rest = turn[0] % lanes
    fraction = 0.25 * turn[1].astype(jnp.float32)
    source = lax.broadcasted_iota(jnp.int32, (2 * lanes, lanes), 0)
    target = lax.broadcasted_iota(jnp.int32, (2 * lanes, lanes), 1)
    gap = source + target - (lanes - 1 + rest)
    blend = jnp.where(gap == 0, 1.0 - fraction, jnp.where(gap == 1, fraction, 0.0)).astype(jnp.bfloat16)
    blend = jnp.concatenate([blend[:lanes]] * 3 + [blend[lanes:]] * 3, axis=0)

    def parts_of(tile):
        start = pl.multiple_of((tile + skipped) * bands, bands)
        cells = window[:, :, pl.ds(start, bands)].reshape(5 * ghosts * bands, lanes)
        parts = []
        for _ in range(3):
            parts.append(cells.astype(jnp.bfloat16))
            cells = cells - parts[-1].astype(jnp.float32)
        return parts

    after = parts_of(tiles)
    for t in range(tiles):
        here = parts_of(tiles - 1 - t)
        mixed = jnp.dot(jnp.concatenate(here + after, axis=1), blend, preferred_element_type=jnp.float32)
        mixed = mixed.reshape(5, ghosts, bands, lanes)
        for c in range(5):
            lead[c, pl.ds(at, ghosts), t] = -mixed[c] if c == 2 else mixed[c]
        after = here


def theta_edges(even, theta_own, even_theta, odd_theta, acc):
    planes, rows = acc.shape[1] - 2, acc.shape[2]
    bands = theta_own.shape[1]
    lane = lane_index((bands, lanes))
    at = lane % group
    inside = lane < group * planes
    cells = []
    for c in theta_order:
        left = jnp.where(even, odd_theta[c], even_theta[c])
        right = jnp.where(even, even_theta[c], odd_theta[c])
        own = jnp.where(inside & (at >= group - ghosts), right, theta_own[c])
        cells.append(jnp.where(inside & (at < ghosts), left, own))
    turn = lambda value, shift: pltpu.roll(value, -shift % lanes, 1) if shift else value
    after = [turn(v, 1) for v in cells]
    terms = interface_terms(with_terms(cells), with_terms(after))
    flux = face_from(lambda n, s: turn(terms[n], s - 2), lambda n: cells[n] + after[n])
    low, high = ghosts - 1, group // 2 + 2
    wanted = inside & (((at >= low) & (at < low + 3)) | ((at >= high) & (at < high + 3)))
    flux = [jnp.where(wanted, value, 0.0) for value in flux]
    changes = [value - turn(value, -1) for value in flux]

    for p in range(planes):
        for c, change in zip(theta_order, changes):
            first = turn(change, group * p + ghosts)
            last = turn(change, group * p + high + ghosts - lanes)
            acc[c, p + 1, 0:bands] += jnp.where(lane < ghosts, first, 0.0)
            acc[c, p + 1, rows - bands : rows] += jnp.where(lane >= lanes - ghosts, last, 0.0)


def tail_kernel(
    gathered, rotor_step, section, acc, split, order, whole, part, theta_own, even_theta, odd_theta, out_state,
    more, lead, terms, window, out, sems
):
    planes = section.shape[1]
    tiles, bands = lead.shape[2:4]
    turn = mortar_turn(rotor_step[0], tiles * lanes)
    swapped = (turn[2] == 1) & (not gathered)
    whole_at = pl.multiple_of(jnp.where(swapped, part.shape[2], 0), bands)
    part_at = pl.multiple_of(jnp.where(swapped, 0, whole.shape[2]), bands)
    arriving = [
        pltpu.make_async_copy(whole, window.at[:, :, pl.ds(whole_at, whole.shape[2])], sems.at[1]),
        pltpu.make_async_copy(part, window.at[:, :, pl.ds(part_at, part.shape[2])], sems.at[2]),
    ]
    for copy in arriving:
        copy.start()
    front = lax.axis_index("blk") == 0
    kept = planes - 1
    own = jnp.where(front, 1, 0)
    own_at = jnp.where(front, 0, ghosts)
    ghost_at = jnp.where(front, kept, 0)
    first = jnp.where(front, planes + 1 - ghosts, 0)

    def fill(i):
        for c in axial_order:
            lead[c, own_at + i] = section[c, own + i].reshape(tiles, bands, lanes)

    loop(kept, fill)

    for c in range(5):
        more[c, 0] = jnp.zeros(more.shape[2:], jnp.float32)
        more[c, planes + 1] = jnp.zeros(more.shape[2:], jnp.float32)
    restore(split, order, planes, more)
    theta_edges(lax.rem(lax.axis_index("theta"), 2) == 0, theta_own, even_theta, odd_theta, more)
    for copy in arriving:
        copy.wait()
    mortar_planes(turn, window, lead, ghost_at)
    axial_faces(ghosts, first, more, lead, terms)

    storing = [pltpu.make_async_copy(out.at[c], out_state.at[c], sems.at[c]) for c in range(5)]
    for c in range(5):
        out[c] = acc[c, 1 : planes + 1] + flux_factor * more[c, 1 : planes + 1]
        storing[c].start()
    for copy in storing:
        copy.wait()


def tail(gathered, rotor_step, section, acc, split, order, whole, part, theta_own, even_theta, odd_theta):
    _, planes, rows, _ = section.shape
    bands = theta_own.shape[1]
    tiles = rows // bands
    smem = pl.BlockSpec(memory_space=pltpu.SMEM)
    vmem = pl.BlockSpec(memory_space=pltpu.VMEM)
    anywhere = pl.BlockSpec(memory_space=pl.ANY)
    return pl.pallas_call(
        functools.partial(tail_kernel, gathered),
        in_specs=[smem, vmem, vmem, vmem, vmem, anywhere, anywhere, vmem, vmem, vmem],
        out_specs=anywhere,
        out_shape=jax.ShapeDtypeStruct(section.shape, jnp.float32),
        scratch_shapes=[
            pltpu.VMEM(acc.shape, jnp.float32),
            pltpu.VMEM((5, planes - 1 + ghosts, tiles, bands, lanes), jnp.float32),
            pltpu.VMEM((22, 2 * ghosts + 3, tile_batch, bands, lanes), jnp.float32),
            pltpu.VMEM((5, ghosts, whole.shape[2] + part.shape[2], lanes), jnp.float32),
            pltpu.VMEM(section.shape, jnp.float32),
            pltpu.SemaphoreType.DMA((5,)),
        ],
        compiler_params=pltpu.CompilerParams(vmem_limit_bytes=vmem_bytes),
        name="tail",
    )(rotor_step, section, acc, split, order, whole, part, theta_own, even_theta, odd_theta)


def slab_routes(turns, slabs):
    both = []
    for ahead in (1, 0):
        both.append(
            [
                (block * slabs + slab, (1 - block) * slabs + (turns - ahead - slab) % slabs)
                for block in range(2)
                for slab in range(slabs)
            ]
        )
    return both


def shards(base_state, section_state, rotor_step):
    bands, width = section_state.shape[2:]
    rows = width // lanes * bands
    slabs = lax.axis_size("theta")
    slab = lax.axis_index("theta")
    parts = lax.axis_size("radial")
    offset = lax.div(rotor_step[0], 4)
    turns = lax.div(offset, width)
    second_half = lax.div(lax.rem(offset, width), width // 2)
    gathered = slabs > most_slabs
    base, section = tile_rows(base_state), tile_rows(section_state)
    held, even_theta, odd_theta, theta_own, even_radial, odd_radial, whole, part, cells, order = pack(
        rotor_step, section, bands
    )

    def pairs(count, first, closed):
        ends = range(first, count if closed else count - 1, 2)
        return [pair for i in ends for pair in ((i, (i + 1) % count), ((i + 1) % count, i))]

    def halos(even_radial, odd_radial, even_theta, odd_theta):
        return (
            lax.ppermute(even_radial, "radial", pairs(parts, 0, False)),
            lax.ppermute(odd_radial, "radial", pairs(parts, 1, False)),
            lax.ppermute(even_theta, "theta", pairs(slabs, 0, True)),
            lax.ppermute(odd_theta, "theta", pairs(slabs, 1, True)),
        )

    if gathered:
        even_radial, odd_radial, even_theta, odd_theta = halos(even_radial, odd_radial, even_theta, odd_theta)
        facing = lax.ppermute(whole, "blk", [(0, 1), (1, 0)])
        ring = lax.all_gather(facing, "theta", axis=2, tiled=True)
        ring = jnp.concatenate([ring, ring, ring[:, :, : rows // 2]], axis=2)
        begin = (turns - 1 - slab) % slabs * rows + second_half * (rows // 2)
        whole = lax.dynamic_slice_in_dim(ring, begin, rows, 2)
        part = lax.dynamic_slice_in_dim(ring, begin + rows, rows // 2, 2)
        acc, split = inner(held, cells, bands, even_radial, odd_radial, base)
    else:

        def branch(case):
            near, far = slab_routes(case // 2 + 1, slabs)
            whole_route, part_route = (near, far) if case % 2 == 0 else (far, near)

            def run(held, cells, base, whole, part, *ends):
                whole = lax.ppermute(whole, ("blk", "theta"), whole_route)
                part = lax.ppermute(part, ("blk", "theta"), part_route)
                even_radial, odd_radial, *ends = halos(*ends)
                acc, split = inner(held, cells, bands, even_radial, odd_radial, base)
                return acc, split, whole, part, *ends

            return run

        case = (turns - 1) * 2 + second_half
        branches = [branch(i) for i in range((slabs - 1) * 2)]
        ends = (even_radial, odd_radial, even_theta, odd_theta)
        acc, split, whole, part, even_theta, odd_theta = lax.switch(
            case, branches, held, cells, base, whole, part, *ends
        )
    out = tail(gathered, rotor_step, section, acc, split, order, whole, part, theta_own, even_theta, odd_theta)
    return from_tile_rows(out, bands)


def solution(mesh):
    in_specs = (P(None, "blk", "radial", "theta"), P(None, "blk", "radial", "theta"), P())
    out_specs = P(None, "blk", "radial", "theta")
    return jax.shard_map(shards, mesh=mesh, in_specs=in_specs, out_specs=out_specs, check_vma=False)
```

```python
import functools

import jax
import jax.numpy as jnp
from jax import lax
from jax.experimental import pallas as pl
from jax.experimental.pallas import tpu as pltpu
from jax.sharding import PartitionSpec as P

gamma_ratio = 1.4
weno_epsilon = 1e-06
step_ratio = 0.12
lanes = 128
ghosts = 3
group = 16
plane_batch = 3
tile_batch = 2
flux_scale = 12.0
flux_factor = -0.25 * step_ratio / flux_scale
most_slabs = 8
vmem_bytes = 32 * 1024 * 1024

axial_order = (0, 1, 2, 3, 4)
radial_order = (0, 3, 1, 2, 4)
theta_order = (0, 2, 1, 3, 4)


def inverse(value):
    guess = pl.reciprocal(value, approx=True)
    return guess * (2.0 - value * guess)


def cell_terms(state):
    density, normal, first, second, energy = state
    inv = inverse(density)
    speed = normal * inv
    kinetic = 0.5 * (normal * normal + first * first + second * second) * inv
    pressure = (gamma_ratio - 1.0) * (energy - kinetic)
    square = gamma_ratio * pressure * inv
    wave = jnp.abs(speed) + square * lax.rsqrt(square)
    flux = (normal, normal * speed + pressure, first * speed, second * speed, (energy + pressure) * speed)
    return flux, wave


def interface_terms(left, right):
    (state_l, flux_l, wave_l), (state_r, flux_r, wave_r) = left, right
    return (
        [r - l for l, r in zip(state_l, state_r)]
        + [r - l for l, r in zip(flux_l, flux_r)]
        + [0.5 * flux_scale * (r + l) for l, r in zip(flux_l, flux_r)]
        + [jnp.maximum(wave_l, wave_r)]
    )


def weno_terms(d0, d1, d2, d3, epsilon):
    e0 = d1 - d0
    e1 = d2 - d1
    e2 = d3 - d2
    f0 = e0 - e1
    f1 = e1 - e2
    t1 = 0.75 * d1
    t2 = 0.75 * d2
    shared = t1 * d2 + epsilon
    low = e0 * e0 + (t1 * f0 + shared)
    mid = e1 * e1 + shared
    high = e2 * e2 + (t2 * f1 + shared)
    x = mid * pl.reciprocal(low, approx=True)
    y = mid * pl.reciprocal(high, approx=True)
    weight_low = x * x
    weight_high = 1.5 * (y * y)
    total = 0.5 * weight_low + (weight_high + 3.0)
    return (weight_low * f0 + weight_high * f1) * pl.reciprocal(total, approx=True)


def face_terms(diff_state, diff_flux, sum_state, sum_flux, wave):
    inv = inverse(sum_state(0))
    un, va, vb, specific = (inv * sum_state(k) for k in range(1, 5))
    half = 0.5 * (un * un + va * va + vb * vb)
    internal = specific - half
    square = gamma_ratio * (gamma_ratio - 1.0) * internal
    inv_sound = lax.rsqrt(square)
    sound = square * inv_sound
    factor = (gamma_ratio - 1.0) * inv_sound * inv_sound
    enthalpy = specific + (gamma_ratio - 1.0) * internal

    def project(dens, norm, first, second, energy):
        sn = norm - un * dens
        sa = first - va * dens
        sb = second - vb * dens
        even = factor * (energy - half * dens - un * sn - va * sa - vb * sb)
        odd = inv_sound * sn
        return even - odd, dens - even, sa, sb, even + odd

    def side(vectors):
        chars = [project(*vector) for vector in vectors]
        return [weno_terms(*(c[k] for c in chars), weno_epsilon * (12.0 if k in (0, 4) else 3.0)) for k in range(5)]

    fluxes = [[diff_flux[s](c) for c in range(5)] for s in range(5)]
    damped = [[wave * diff_state[s](c) for c in range(5)] for s in range(5)]
    plus = [[f + d for f, d in zip(fluxes[s], damped[s])] for s in range(4)]
    forward = side(plus)
    minus = [[f - d for f, d in zip(fluxes[s], damped[s])] for s in range(4, 0, -1)]
    backward = side(minus)
    central = [sum_flux(c) + (plus[1][c] - plus[2][c]) + (minus[2][c] - minus[1][c]) for c in range(5)]
    wave_minus, entropy, sa, sb, wave_plus = (f - b for f, b in zip(forward, backward))
    even = 0.5 * (wave_plus + wave_minus)
    odd = sound * (0.5 * (wave_plus - wave_minus))
    carried = even + entropy
    return (
        central[0] + carried,
        central[1] + un * carried + odd,
        central[2] + va * carried + sa,
        central[3] + vb * carried + sb,
        central[4] + enthalpy * even + un * odd + half * entropy + va * sa + vb * sb,
    )


def face_from(load, sum_state):
    return face_terms(
        [functools.partial(lambda s, c: load(c, s), s) for s in range(5)],
        [functools.partial(lambda s, c: load(5 + c, s), s) for s in range(5)],
        sum_state,
        lambda c: load(10 + c, 2),
        load(15, 2),
    )


def with_terms(state):
    return (state, *cell_terms(state))


def lane_index(shape):
    return lax.broadcasted_iota(jnp.int32, shape, len(shape) - 1)


def tile_rows(state):
    components, planes, bands, width = state.shape
    split = state.reshape(components, planes, bands, width // lanes, lanes)
    return split.transpose(0, 1, 3, 2, 4).reshape(components, planes, -1, lanes)


def from_tile_rows(rows, bands):
    components, planes, count, _ = rows.shape
    split = rows.reshape(components, planes, count // bands, bands, lanes)
    return split.transpose(0, 1, 3, 2, 4).reshape(components, planes, bands, -1)


def loop(count, body):
    def step(i, carry):
        body(i)
        return carry

    lax.fori_loop(0, count, step, 0)


def make_order(order):
    tiles = order.shape[0] // lanes
    one, zero = jnp.ones((lanes, lanes), jnp.bfloat16), jnp.zeros((lanes, lanes), jnp.bfloat16)
    row = lax.broadcasted_iota(jnp.int32, (lanes, lanes), 0)
    column = lax.broadcasted_iota(jnp.int32, (lanes, lanes), 1)
    for t in range(tiles):
        meets = column - row // tiles == t * lanes // tiles
        key = jnp.where(meets, row % tiles, -1).astype(jnp.float32).astype(jnp.bfloat16)
        for j in range(tiles):
            block = jnp.where(key == j, one, zero)
            order[t * lanes : (t + 1) * lanes, j * lanes : (j + 1) * lanes] = block


def store_split(split, n, tile, values):
    high = values.astype(jnp.bfloat16)
    low = (values - high.astype(jnp.float32)).astype(jnp.bfloat16)
    flat = values.shape[0]
    start = pl.multiple_of(n * flat, 16)
    split[pl.ds(start, flat), tile * lanes : (tile + 1) * lanes] = high
    split[pl.ds(5 * flat + start, flat), tile * lanes : (tile + 1) * lanes] = low


def reorder(section, cells, split, order):
    _, tiles, planes, bands, _ = cells.shape
    flat = planes * bands
    for n, c in enumerate(theta_order):
        for t in range(tiles):
            store_split(split, n, t, section[c, :, t * bands : (t + 1) * bands].reshape(flat, lanes))
    both = jnp.dot(split[...], order[...], preferred_element_type=jnp.float32)
    both = both[: 5 * flat] + both[5 * flat :]
    for n in range(5):
        for j in range(tiles):
            part = both[n * flat : (n + 1) * flat, j * lanes : (j + 1) * lanes]
            cells[n, j] = part.reshape(planes, bands, lanes)


def restore(split, order, planes, acc):
    tiles = order.shape[0] // lanes
    flat = split.shape[0] // 10
    bands = flat // planes
    both = lax.dot_general(split[...], order[...], (((1,), (1,)), ((), ())), preferred_element_type=jnp.float32)
    both = both[: 5 * flat] + both[5 * flat :]
    for n, c in enumerate(theta_order):
        for t in range(tiles):
            part = both[n * flat : (n + 1) * flat, t * lanes : (t + 1) * lanes]
            acc[c, 1 : planes + 1, t * bands : (t + 1) * bands] = part.reshape(planes, bands, lanes)


def mortar_turn(step, width):
    start = lax.rem(lax.div(step, 4), width)
    return lax.rem(start, width // 2), lax.rem(step, 4), lax.div(start, width // 2)


def pack_kernel(
    bands, rotor_step, section,
    held, even_theta, odd_theta, theta_own, even_radial, odd_radial, whole, part, cells, order, split
):
    planes, rows = section.shape[1:3]
    tiles = rows // bands
    facing = jnp.where(lax.axis_index("blk") == 0, planes - ghosts, 0)
    turn = mortar_turn(rotor_step[0], tiles * lanes)
    part_at = pl.multiple_of(turn[2] * part.shape[2], bands)
    even = lax.rem(lax.axis_index("radial"), 2) == 0
    even_slab = lax.rem(lax.axis_index("theta"), 2) == 0
    lane = lane_index((bands, lanes))

    def component(c):
        held[c] = section[c]
        for i in range(ghosts):
            whole[c, i] = section[c, facing + i]
            part[c, i] = section[c, facing + i, pl.ds(part_at, part.shape[2])]
        own = jnp.full((bands, lanes), (1.0, 0.0, 0.0, 0.0, 3.0)[c], jnp.float32)
        low = high = own
        for p in range(planes):
            at = lane - group * p
            first = section[c, p, 0:bands]
            last = section[c, p, rows - bands : rows]
            own_first = pltpu.roll(first, group * p + ghosts, 1)
            own_last = pltpu.roll(last, group * p + group - ghosts, 1)
            sent_low = pltpu.roll(first, group * p + group - ghosts, 1)
            sent_high = pltpu.roll(last, group * p + ghosts, 1)
            own = jnp.where((at >= ghosts) & (at < group // 2), own_first, own)
            own = jnp.where((at >= group // 2) & (at < group - ghosts), own_last, own)
            low = jnp.where((at >= group - ghosts) & (at < group), sent_low, low)
            high = jnp.where((at >= 0) & (at < ghosts), sent_high, high)
        theta_own[c] = own
        even_theta[c] = jnp.where(even_slab, high, low)
        odd_theta[c] = jnp.where(even_slab, low, high)

        for p in range(planes):
            for k in range(ghosts):
                low = section[c, p, pl.ds(k, tiles, stride=bands)]
                high = section[c, p, pl.ds(bands - ghosts + k, tiles, stride=bands)]
                even_radial[c, p, k] = jnp.where(even, high, low)
                odd_radial[c, p, k] = jnp.where(even, low, high)

    for c in range(5):
        component(c)
    make_order(order)
    reorder(section, cells, split, order)


def pack(rotor_step, section, bands):
    _, planes, rows, _ = section.shape
    smem = pl.BlockSpec(memory_space=pltpu.SMEM)
    vmem = pl.BlockSpec(memory_space=pltpu.VMEM)
    array = lambda *shape: jax.ShapeDtypeStruct(shape, jnp.float32)
    theta = array(5, bands, lanes)
    radial = array(5, planes, ghosts, rows // bands, lanes)
    mortar = [array(5, ghosts, rows, lanes), array(5, ghosts, rows // 2, lanes)]
    width = rows // bands * lanes
    cells = array(5, rows // bands, planes, bands, lanes)
    order = jax.ShapeDtypeStruct((width, width), jnp.bfloat16)
    return pl.pallas_call(
        functools.partial(pack_kernel, bands),
        in_specs=[smem, vmem],
        out_specs=[vmem] * 10,
        out_shape=(array(*section.shape), theta, theta, theta, radial, radial, *mortar, cells, order),
        scratch_shapes=[pltpu.VMEM((10 * planes * bands, width), jnp.bfloat16)],
        compiler_params=pltpu.CompilerParams(vmem_limit_bytes=vmem_bytes),
        name="pack",
    )(rotor_step, section)


def inner_kernel(
    bands, section, cells, even_radial, odd_radial, base_state, acc, split, lead, terms, fluxes, base, sem
):
    planes = section.shape[1]
    loading = pltpu.make_async_copy(base_state, base, sem)
    loading.start()
    radial_pass(bands, section, even_radial, odd_radial, acc, lead, terms, fluxes)
    theta_pass(cells, lead, terms, fluxes, split)
    axial_inner(section, acc, lead, terms)
    loading.wait()
    for c in range(5):
        change = flux_factor * acc[c, 1 : planes + 1]
        acc[c, 1 : planes + 1] = 0.75 * base[c] + (0.25 * section[c] + change)


def lead_faces(lead, cells, columns, batch, terms, emit):
    def column_group(g):
        p = g * batch

        def state(r):
            return [lead[n, r, pl.ds(p, batch)] for n in range(5)]

        def cell(r):
            here = state(r)
            flux, wave = cell_terms(here)
            return here, flux, wave

        def keep(r, values):
            for n, value in enumerate((*values[1], values[2])):
                terms[16 + n, r, 0:batch] = value

        def interface(r, right):
            left = (state(r), [terms[16 + n, r, 0:batch] for n in range(5)], terms[21, r, 0:batch])
            for n, value in enumerate(interface_terms(left, right)):
                terms[n, r, 0:batch] = value

        left = cell(0)
        for r in range(5):
            right = cell(r + 1)
            for n, value in enumerate(interface_terms(left, right)):
                terms[n, r, 0:batch] = value
            left = right
        keep(5, left)

        def face(r):
            flux = face_from(
                lambda n, s: terms[n, r + s, 0:batch],
                lambda n: lead[n, r + 2, pl.ds(p, batch)] + lead[n, r + 3, pl.ds(p, batch)],
            )
            emit(r, p, flux)
            if isinstance(r, int) and r + 6 == cells:
                return
            right = cell(jnp.minimum(r + 6, cells - 1))
            interface(r + 5, right)
            keep(r + 6, right)

        if cells - 5 > ghosts:
            loop(cells - 5, face)
        else:
            for r in range(cells - 5):
                face(r)

    loop(columns // batch, column_group)


def keep_flux(fluxes, r, p, flux):
    for n, value in enumerate(flux):
        fluxes[n, r, pl.ds(p, plane_batch)] = value


def radial_pass(bands, section, even_radial, odd_radial, acc, lead, terms, fluxes):
    planes, rows = section.shape[1:3]
    tiles = rows // bands
    index = lax.axis_index("radial")
    at_inner = index == 0
    at_outer = index == lax.axis_size("radial") - 1
    even = lax.rem(index, 2) == 0

    def spread(p):
        for n, c in enumerate(radial_order):
            band = [section[c, p, pl.ds(r, tiles, stride=bands)] for r in range(bands)]
            sign = -1.0 if c == 3 else 1.0
            for r in range(bands):
                lead[n, r + ghosts, p] = band[r]
            for k in range(ghosts):
                one, two = even_radial[c, p, k], odd_radial[c, p, k]
                low, high = jnp.where(even, two, one), jnp.where(even, one, two)
                lead[n, k, p] = jnp.where(at_inner, sign * band[ghosts - 1 - k], low)
                lead[n, bands + ghosts + k, p] = jnp.where(at_outer, sign * band[bands - 1 - k], high)

    loop(planes, spread)
    lead_faces(lead, bands + 2 * ghosts, planes, plane_batch, terms, functools.partial(keep_flux, fluxes))

    def gather(p):
        for n, c in enumerate(radial_order):
            for r in range(bands):
                acc[c, p + 1, pl.ds(r, tiles, stride=bands)] = fluxes[n, r + 1, p] - fluxes[n, r, p]

    loop(planes, gather)


def theta_pass(cells, lead, terms, fluxes, split):
    _, tiles, planes, bands, _ = cells.shape

    def fill(n):
        for j in range(tiles):
            lead[n, ghosts + j, 0:planes] = cells[n, j]
        for k in range(ghosts):
            lead[n, k, 0:planes] = pltpu.roll(cells[n, tiles - ghosts + k], 1, 2)
            lead[n, ghosts + tiles + k, 0:planes] = pltpu.roll(cells[n, k], lanes - 1, 2)

    loop(5, fill)
    lead_faces(lead, tiles + 2 * ghosts, planes, plane_batch, terms, functools.partial(keep_flux, fluxes))
    lane = lane_index((planes, bands, lanes))

    def changes(n):
        before = None
        for r in range(tiles + 1):
            flux = fluxes[n, r, 0:planes]
            if r < ghosts:
                flux = jnp.where(lane == 0, 0.0, flux)
            if r > tiles - ghosts:
                flux = jnp.where(lane == lanes - 1, 0.0, flux)
            if r > 0:
                store_split(split, n, r - 1, (flux - before).reshape(planes * bands, lanes))
            before = flux

    loop(5, changes)


def axial_faces(count, first, acc, lead, terms):
    tiles, bands = lead.shape[2:4]

    def emit(i, p, flux):
        place = pl.ds(pl.multiple_of(p * bands, bands), tile_batch * bands)
        for c, value in zip(axial_order, flux):
            value = value.reshape(tile_batch * bands, lanes)
            acc[c, first + i, place] += value
            acc[c, first + i + 1, place] -= value

    lead_faces(lead, count + 5, tiles, tile_batch, terms, emit)


def axial_inner(section, acc, lead, terms):
    planes = section.shape[1]
    tiles, bands = lead.shape[2:4]
    first = jnp.where(lax.axis_index("blk") == 0, 0, ghosts)
    count = planes + 1 - ghosts
    for c in range(5):
        acc[c, 0] = jnp.zeros(acc.shape[2:], jnp.float32)
        acc[c, planes + 1] = jnp.zeros(acc.shape[2:], jnp.float32)

    def fill(i):
        plane = jnp.clip(first + i - ghosts, 0, planes - 1)
        for c in axial_order:
            lead[c, i] = section[c, plane].reshape(tiles, bands, lanes)

    loop(count + 5, fill)
    axial_faces(count, first, acc, lead, terms)


def inner(section, cells, bands, even_radial, odd_radial, base):
    _, planes, rows, _ = section.shape
    tiles = rows // bands
    depth = max(bands, tiles) + 2 * ghosts
    across = max(planes, tiles)
    vmem = pl.BlockSpec(memory_space=pltpu.VMEM)
    faces = (planes + 1) * tiles + planes * (tiles + bands + 2)
    return pl.pallas_call(
        functools.partial(inner_kernel, bands),
        in_specs=[vmem] * 4 + [pl.BlockSpec(memory_space=pl.ANY)],
        out_shape=(
            jax.ShapeDtypeStruct((5, planes + 2, rows, lanes), jnp.float32),
            jax.ShapeDtypeStruct((10 * planes * bands, tiles * lanes), jnp.bfloat16),
        ),
        scratch_shapes=[
            pltpu.VMEM((5, depth, across, 8, lanes), jnp.float32),
            pltpu.VMEM((22, depth + 1, max(plane_batch, tile_batch), 8, lanes), jnp.float32),
            pltpu.VMEM((5, depth - 5, planes, 8, lanes), jnp.float32),
            pltpu.VMEM(section.shape, jnp.float32),
            pltpu.SemaphoreType.DMA(()),
        ],
        compiler_params=pltpu.CompilerParams(vmem_limit_bytes=vmem_bytes),
        cost_estimate=pl.CostEstimate(
            flops=faces * 8 * lanes * 700, bytes_accessed=section.size * 16, transcendentals=faces * 8 * lanes * 30
        ),
        name="inner",
    )(section, cells, even_radial, odd_radial, base)


def mortar_planes(turn, window, lead, at):
    tiles, bands = lead.shape[2:4]
    skipped = turn[0] // lanes
    rest = turn[0] % lanes
    fraction = 0.25 * turn[1].astype(jnp.float32)
    source = lax.broadcasted_iota(jnp.int32, (2 * lanes, lanes), 0)
    target = lax.broadcasted_iota(jnp.int32, (2 * lanes, lanes), 1)
    gap = source + target - (lanes - 1 + rest)
    blend = jnp.where(gap == 0, 1.0 - fraction, jnp.where(gap == 1, fraction, 0.0)).astype(jnp.bfloat16)
    blend = jnp.concatenate([blend[:lanes]] * 3 + [blend[lanes:]] * 3, axis=0)

    def parts_of(tile):
        start = pl.multiple_of((tile + skipped) * bands, bands)
        cells = window[:, :, pl.ds(start, bands)].reshape(5 * ghosts * bands, lanes)
        parts = []
        for _ in range(3):
            parts.append(cells.astype(jnp.bfloat16))
            cells = cells - parts[-1].astype(jnp.float32)
        return parts

    after = parts_of(tiles)
    for t in range(tiles):
        here = parts_of(tiles - 1 - t)
        mixed = jnp.dot(jnp.concatenate(here + after, axis=1), blend, preferred_element_type=jnp.float32)
        mixed = mixed.reshape(5, ghosts, bands, lanes)
        for c in range(5):
            lead[c, pl.ds(at, ghosts), t] = -mixed[c] if c == 2 else mixed[c]
        after = here


def theta_edges(even, theta_own, even_theta, odd_theta, acc):
    planes, rows = acc.shape[1] - 2, acc.shape[2]
    bands = theta_own.shape[1]
    lane = lane_index((bands, lanes))
    at = lane % group
    inside = lane < group * planes
    cells = []
    for c in theta_order:
        left = jnp.where(even, odd_theta[c], even_theta[c])
        right = jnp.where(even, even_theta[c], odd_theta[c])
        own = jnp.where(inside & (at >= group - ghosts), right, theta_own[c])
        cells.append(jnp.where(inside & (at < ghosts), left, own))
    turn = lambda value, shift: pltpu.roll(value, -shift % lanes, 1) if shift else value
    after = [turn(v, 1) for v in cells]
    terms = interface_terms(with_terms(cells), with_terms(after))
    flux = face_from(lambda n, s: turn(terms[n], s - 2), lambda n: cells[n] + after[n])
    low, high = ghosts - 1, group // 2 + 2
    wanted = inside & (((at >= low) & (at < low + 3)) | ((at >= high) & (at < high + 3)))
    flux = [jnp.where(wanted, value, 0.0) for value in flux]
    changes = [value - turn(value, -1) for value in flux]

    for p in range(planes):
        for c, change in zip(theta_order, changes):
            first = turn(change, group * p + ghosts)
            last = turn(change, group * p + high + ghosts - lanes)
            acc[c, p + 1, 0:bands] += jnp.where(lane < ghosts, first, 0.0)
            acc[c, p + 1, rows - bands : rows] += jnp.where(lane >= lanes - ghosts, last, 0.0)


def tail_kernel(
    gathered, rotor_step, section, acc, split, order, whole, part, theta_own, even_theta, odd_theta, out_state,
    more, lead, terms, window, out, sems
):
    planes = section.shape[1]
    tiles, bands = lead.shape[2:4]
    turn = mortar_turn(rotor_step[0], tiles * lanes)
    swapped = (turn[2] == 1) & (not gathered)
    whole_at = pl.multiple_of(jnp.where(swapped, part.shape[2], 0), bands)
    part_at = pl.multiple_of(jnp.where(swapped, 0, whole.shape[2]), bands)
    arriving = [
        pltpu.make_async_copy(whole, window.at[:, :, pl.ds(whole_at, whole.shape[2])], sems.at[1]),
        pltpu.make_async_copy(part, window.at[:, :, pl.ds(part_at, part.shape[2])], sems.at[2]),
    ]
    for copy in arriving:
        copy.start()
    front = lax.axis_index("blk") == 0
    kept = planes - 1
    own = jnp.where(front, 1, 0)
    own_at = jnp.where(front, 0, ghosts)
    ghost_at = jnp.where(front, kept, 0)
    first = jnp.where(front, planes + 1 - ghosts, 0)

    def fill(i):
        for c in axial_order:
            lead[c, own_at + i] = section[c, own + i].reshape(tiles, bands, lanes)

    loop(kept, fill)

    for c in range(5):
        more[c, 0] = jnp.zeros(more.shape[2:], jnp.float32)
        more[c, planes + 1] = jnp.zeros(more.shape[2:], jnp.float32)
    restore(split, order, planes, more)
    theta_edges(lax.rem(lax.axis_index("theta"), 2) == 0, theta_own, even_theta, odd_theta, more)
    for copy in arriving:
        copy.wait()
    mortar_planes(turn, window, lead, ghost_at)
    axial_faces(ghosts, first, more, lead, terms)

    storing = [pltpu.make_async_copy(out.at[c], out_state.at[c], sems.at[c]) for c in range(5)]
    for c in range(5):
        out[c] = acc[c, 1 : planes + 1] + flux_factor * more[c, 1 : planes + 1]
        storing[c].start()
    for copy in storing:
        copy.wait()


def tail(gathered, rotor_step, section, acc, split, order, whole, part, theta_own, even_theta, odd_theta):
    _, planes, rows, _ = section.shape
    bands = theta_own.shape[1]
    tiles = rows // bands
    smem = pl.BlockSpec(memory_space=pltpu.SMEM)
    vmem = pl.BlockSpec(memory_space=pltpu.VMEM)
    anywhere = pl.BlockSpec(memory_space=pl.ANY)
    return pl.pallas_call(
        functools.partial(tail_kernel, gathered),
        in_specs=[smem, vmem, vmem, vmem, vmem, anywhere, anywhere, vmem, vmem, vmem],
        out_specs=anywhere,
        out_shape=jax.ShapeDtypeStruct(section.shape, jnp.float32),
        scratch_shapes=[
            pltpu.VMEM(acc.shape, jnp.float32),
            pltpu.VMEM((5, planes - 1 + ghosts, tiles, bands, lanes), jnp.float32),
            pltpu.VMEM((22, 2 * ghosts + 3, tile_batch, bands, lanes), jnp.float32),
            pltpu.VMEM((5, ghosts, whole.shape[2] + part.shape[2], lanes), jnp.float32),
            pltpu.VMEM(section.shape, jnp.float32),
            pltpu.SemaphoreType.DMA((5,)),
        ],
        compiler_params=pltpu.CompilerParams(vmem_limit_bytes=vmem_bytes),
        name="tail",
    )(rotor_step, section, acc, split, order, whole, part, theta_own, even_theta, odd_theta)


def slab_routes(turns, slabs):
    both = []
    for ahead in (1, 0):
        both.append(
            [
                (block * slabs + slab, (1 - block) * slabs + (turns - ahead - slab) % slabs)
                for block in range(2)
                for slab in range(slabs)
            ]
        )
    return both


def shards(base_state, section_state, rotor_step):
    bands, width = section_state.shape[2:]
    rows = width // lanes * bands
    slabs = lax.axis_size("theta")
    slab = lax.axis_index("theta")
    parts = lax.axis_size("radial")
    offset = lax.div(rotor_step[0], 4)
    turns = lax.div(offset, width)
    second_half = lax.div(lax.rem(offset, width), width // 2)
    gathered = slabs > most_slabs
    base, section = tile_rows(base_state), tile_rows(section_state)
    held, even_theta, odd_theta, theta_own, even_radial, odd_radial, whole, part, cells, order = pack(
        rotor_step, section, bands
    )

    def pairs(count, first, closed):
        ends = range(first, count if closed else count - 1, 2)
        return [pair for i in ends for pair in ((i, (i + 1) % count), ((i + 1) % count, i))]

    def halos(even_radial, odd_radial, even_theta, odd_theta):
        return (
            lax.ppermute(even_radial, "radial", pairs(parts, 0, False)),
            lax.ppermute(odd_radial, "radial", pairs(parts, 1, False)),
            lax.ppermute(even_theta, "theta", pairs(slabs, 0, True)),
            lax.ppermute(odd_theta, "theta", pairs(slabs, 1, True)),
        )

    if gathered:
        even_radial, odd_radial, even_theta, odd_theta = halos(even_radial, odd_radial, even_theta, odd_theta)
        facing = lax.ppermute(whole, "blk", [(0, 1), (1, 0)])
        ring = lax.all_gather(facing, "theta", axis=2, tiled=True)
        ring = jnp.concatenate([ring, ring, ring[:, :, : rows // 2]], axis=2)
        begin = (turns - 1 - slab) % slabs * rows + second_half * (rows // 2)
        whole = lax.dynamic_slice_in_dim(ring, begin, rows, 2)
        part = lax.dynamic_slice_in_dim(ring, begin + rows, rows // 2, 2)
        acc, split = inner(held, cells, bands, even_radial, odd_radial, base)
    else:

        def branch(case):
            near, far = slab_routes(case // 2 + 1, slabs)
            whole_route, part_route = (near, far) if case % 2 == 0 else (far, near)

            def run(held, cells, base, whole, part, *ends):
                whole = lax.ppermute(whole, ("blk", "theta"), whole_route)
                part = lax.ppermute(part, ("blk", "theta"), part_route)
                even_radial, odd_radial, *ends = halos(*ends)
                acc, split = inner(held, cells, bands, even_radial, odd_radial, base)
                return acc, split, whole, part, *ends

            return run

        case = (turns - 1) * 2 + second_half
        branches = [branch(i) for i in range((slabs - 1) * 2)]
        ends = (even_radial, odd_radial, even_theta, odd_theta)
        acc, split, whole, part, even_theta, odd_theta = lax.switch(
            case, branches, held, cells, base, whole, part, *ends
        )
    out = tail(gathered, rotor_step, section, acc, split, order, whole, part, theta_own, even_theta, odd_theta)
    return from_tile_rows(out, bands)


def solution(mesh):
    in_specs = (P(None, "blk", "radial", "theta"), P(None, "blk", "radial", "theta"), P())
    out_specs = P(None, "blk", "radial", "theta")
    return jax.shard_map(shards, mesh=mesh, in_specs=in_specs, out_specs=out_specs, check_vma=False)
```

```python
import functools

import jax
import jax.numpy as jnp
from jax import lax
from jax.experimental import pallas as pl
from jax.experimental.pallas import tpu as pltpu
from jax.sharding import PartitionSpec as P

gamma_ratio = 1.4
weno_epsilon = 1e-06
step_ratio = 0.12
lanes = 128
ghosts = 3
group = 16
plane_batch = 3
tile_batch = 2
flux_scale = 12.0
flux_factor = -0.25 * step_ratio / flux_scale
most_slabs = 8
vmem_bytes = 32 * 1024 * 1024

axial_order = (0, 1, 2, 3, 4)
radial_order = (0, 3, 1, 2, 4)
theta_order = (0, 2, 1, 3, 4)


def inverse(value):
    guess = pl.reciprocal(value, approx=True)
    return guess * (2.0 - value * guess)


def cell_terms(state):
    density, normal, first, second, energy = state
    inv = inverse(density)
    speed = normal * inv
    kinetic = 0.5 * (normal * normal + first * first + second * second) * inv
    pressure = (gamma_ratio - 1.0) * (energy - kinetic)
    square = gamma_ratio * pressure * inv
    wave = jnp.abs(speed) + square * lax.rsqrt(square)
    flux = (normal, normal * speed + pressure, first * speed, second * speed, (energy + pressure) * speed)
    return flux, wave


def interface_terms(left, right):
    (state_l, flux_l, wave_l), (state_r, flux_r, wave_r) = left, right
    return (
        [r - l for l, r in zip(state_l, state_r)]
        + [r - l for l, r in zip(flux_l, flux_r)]
        + [0.5 * flux_scale * (r + l) for l, r in zip(flux_l, flux_r)]
        + [jnp.maximum(wave_l, wave_r)]
    )


def weno_terms(d0, d1, d2, d3, epsilon):
    e0 = d1 - d0
    e1 = d2 - d1
    e2 = d3 - d2
    f0 = e0 - e1
    f1 = e1 - e2
    t1 = 0.75 * d1
    t2 = 0.75 * d2
    shared = t1 * d2 + epsilon
    low = e0 * e0 + (t1 * f0 + shared)
    mid = e1 * e1 + shared
    high = e2 * e2 + (t2 * f1 + shared)
    x = mid * pl.reciprocal(low, approx=True)
    y = mid * pl.reciprocal(high, approx=True)
    weight_low = x * x
    weight_high = 1.5 * (y * y)
    total = 0.5 * weight_low + (weight_high + 3.0)
    return (weight_low * f0 + weight_high * f1) * pl.reciprocal(total, approx=True)


def face_terms(diff_state, diff_flux, sum_state, sum_flux, wave):
    inv = pl.reciprocal(sum_state(0), approx=True)
    un, va, vb, specific = (inv * sum_state(k) for k in range(1, 5))
    half = 0.5 * (un * un + va * va + vb * vb)
    internal = specific - half
    square = gamma_ratio * (gamma_ratio - 1.0) * internal
    inv_sound = lax.rsqrt(square)
    sound = square * inv_sound
    factor = (gamma_ratio - 1.0) * inv_sound * inv_sound
    enthalpy = specific + (gamma_ratio - 1.0) * internal

    def project(dens, norm, first, second, energy):
        sn = norm - un * dens
        sa = first - va * dens
        sb = second - vb * dens
        even = factor * (energy - half * dens - un * sn - va * sa - vb * sb)
        odd = inv_sound * sn
        return even - odd, dens - even, sa, sb, even + odd

    def side(vectors):
        chars = [project(*vector) for vector in vectors]
        return [weno_terms(*(c[k] for c in chars), weno_epsilon * (12.0 if k in (0, 4) else 3.0)) for k in range(5)]

    fluxes = [[diff_flux[s](c) for c in range(5)] for s in range(5)]
    damped = [[wave * diff_state[s](c) for c in range(5)] for s in range(5)]
    plus = [[f + d for f, d in zip(fluxes[s], damped[s])] for s in range(4)]
    forward = side(plus)
    minus = [[f - d for f, d in zip(fluxes[s], damped[s])] for s in range(4, 0, -1)]
    backward = side(minus)
    central = [sum_flux(c) + (plus[1][c] - plus[2][c]) + (minus[2][c] - minus[1][c]) for c in range(5)]
    wave_minus, entropy, sa, sb, wave_plus = (f - b for f, b in zip(forward, backward))
    even = 0.5 * (wave_plus + wave_minus)
    odd = sound * (0.5 * (wave_plus - wave_minus))
    carried = even + entropy
    return (
        central[0] + carried,
        central[1] + un * carried + odd,
        central[2] + va * carried + sa,
        central[3] + vb * carried + sb,
        central[4] + enthalpy * even + un * odd + half * entropy + va * sa + vb * sb,
    )


def face_from(load, sum_state):
    return face_terms(
        [functools.partial(lambda s, c: load(c, s), s) for s in range(5)],
        [functools.partial(lambda s, c: load(5 + c, s), s) for s in range(5)],
        sum_state,
        lambda c: load(10 + c, 2),
        load(15, 2),
    )


def with_terms(state):
    return (state, *cell_terms(state))


def lane_index(shape):
    return lax.broadcasted_iota(jnp.int32, shape, len(shape) - 1)


def tile_rows(state):
    components, planes, bands, width = state.shape
    split = state.reshape(components, planes, bands, width // lanes, lanes)
    return split.transpose(0, 1, 3, 2, 4).reshape(components, planes, -1, lanes)


def from_tile_rows(rows, bands):
    components, planes, count, _ = rows.shape
    split = rows.reshape(components, planes, count // bands, bands, lanes)
    return split.transpose(0, 1, 3, 2, 4).reshape(components, planes, bands, -1)


def loop(count, body):
    def step(i, carry):
        body(i)
        return carry

    lax.fori_loop(0, count, step, 0)


def make_order(order):
    tiles = order.shape[0] // lanes
    one, zero = jnp.ones((lanes, lanes), jnp.bfloat16), jnp.zeros((lanes, lanes), jnp.bfloat16)
    row = lax.broadcasted_iota(jnp.int32, (lanes, lanes), 0)
    column = lax.broadcasted_iota(jnp.int32, (lanes, lanes), 1)
    for t in range(tiles):
        meets = column - row // tiles == t * lanes // tiles
        key = jnp.where(meets, row % tiles, -1).astype(jnp.float32).astype(jnp.bfloat16)
        for j in range(tiles):
            block = jnp.where(key == j, one, zero)
            order[t * lanes : (t + 1) * lanes, j * lanes : (j + 1) * lanes] = block


def store_split(split, n, tile, values):
    high = values.astype(jnp.bfloat16)
    low = (values - high.astype(jnp.float32)).astype(jnp.bfloat16)
    flat = values.shape[0]
    start = pl.multiple_of(n * flat, 16)
    split[pl.ds(start, flat), tile * lanes : (tile + 1) * lanes] = high
    split[pl.ds(5 * flat + start, flat), tile * lanes : (tile + 1) * lanes] = low


def reorder(section, cells, split, order):
    _, tiles, planes, bands, _ = cells.shape
    flat = planes * bands
    for n, c in enumerate(theta_order):
        for t in range(tiles):
            store_split(split, n, t, section[c, :, t * bands : (t + 1) * bands].reshape(flat, lanes))
    both = jnp.dot(split[...], order[...], preferred_element_type=jnp.float32)
    both = both[: 5 * flat] + both[5 * flat :]
    for n in range(5):
        for j in range(tiles):
            part = both[n * flat : (n + 1) * flat, j * lanes : (j + 1) * lanes]
            cells[n, j] = part.reshape(planes, bands, lanes)


def restore(split, order, planes, acc):
    tiles = order.shape[0] // lanes
    flat = split.shape[0] // 10
    bands = flat // planes
    both = lax.dot_general(split[...], order[...], (((1,), (1,)), ((), ())), preferred_element_type=jnp.float32)
    both = both[: 5 * flat] + both[5 * flat :]
    for n, c in enumerate(theta_order):
        for t in range(tiles):
            part = both[n * flat : (n + 1) * flat, t * lanes : (t + 1) * lanes]
            acc[c, 1 : planes + 1, t * bands : (t + 1) * bands] = part.reshape(planes, bands, lanes)


def mortar_turn(step, width):
    start = lax.rem(lax.div(step, 4), width)
    return lax.rem(start, width // 2), lax.rem(step, 4), lax.div(start, width // 2)


def pack_kernel(
    bands, rotor_step, section,
    held, even_theta, odd_theta, theta_own, even_radial, odd_radial, whole, part, cells, order, split
):
    planes, rows = section.shape[1:3]
    tiles = rows // bands
    facing = jnp.where(lax.axis_index("blk") == 0, planes - ghosts, 0)
    turn = mortar_turn(rotor_step[0], tiles * lanes)
    part_at = pl.multiple_of(turn[2] * part.shape[2], bands)
    even = lax.rem(lax.axis_index("radial"), 2) == 0
    even_slab = lax.rem(lax.axis_index("theta"), 2) == 0
    lane = lane_index((bands, lanes))

    def component(c):
        held[c] = section[c]
        for i in range(ghosts):
            whole[c, i] = section[c, facing + i]
            part[c, i] = section[c, facing + i, pl.ds(part_at, part.shape[2])]
        own = jnp.full((bands, lanes), (1.0, 0.0, 0.0, 0.0, 3.0)[c], jnp.float32)
        low = high = own
        for p in range(planes):
            at = lane - group * p
            first = section[c, p, 0:bands]
            last = section[c, p, rows - bands : rows]
            own_first = pltpu.roll(first, group * p + ghosts, 1)
            own_last = pltpu.roll(last, group * p + group - ghosts, 1)
            sent_low = pltpu.roll(first, group * p + group - ghosts, 1)
            sent_high = pltpu.roll(last, group * p + ghosts, 1)
            own = jnp.where((at >= ghosts) & (at < group // 2), own_first, own)
            own = jnp.where((at >= group // 2) & (at < group - ghosts), own_last, own)
            low = jnp.where((at >= group - ghosts) & (at < group), sent_low, low)
            high = jnp.where((at >= 0) & (at < ghosts), sent_high, high)
        theta_own[c] = own
        even_theta[c] = jnp.where(even_slab, high, low)
        odd_theta[c] = jnp.where(even_slab, low, high)

        for p in range(planes):
            for k in range(ghosts):
                low = section[c, p, pl.ds(k, tiles, stride=bands)]
                high = section[c, p, pl.ds(bands - ghosts + k, tiles, stride=bands)]
                even_radial[c, p, k] = jnp.where(even, high, low)
                odd_radial[c, p, k] = jnp.where(even, low, high)

    for c in range(5):
        component(c)
    make_order(order)
    reorder(section, cells, split, order)


def pack(rotor_step, section, bands):
    _, planes, rows, _ = section.shape
    smem = pl.BlockSpec(memory_space=pltpu.SMEM)
    vmem = pl.BlockSpec(memory_space=pltpu.VMEM)
    array = lambda *shape: jax.ShapeDtypeStruct(shape, jnp.float32)
    theta = array(5, bands, lanes)
    radial = array(5, planes, ghosts, rows // bands, lanes)
    mortar = [array(5, ghosts, rows, lanes), array(5, ghosts, rows // 2, lanes)]
    width = rows // bands * lanes
    cells = array(5, rows // bands, planes, bands, lanes)
    order = jax.ShapeDtypeStruct((width, width), jnp.bfloat16)
    return pl.pallas_call(
        functools.partial(pack_kernel, bands),
        in_specs=[smem, vmem],
        out_specs=[vmem] * 10,
        out_shape=(array(*section.shape), theta, theta, theta, radial, radial, *mortar, cells, order),
        scratch_shapes=[pltpu.VMEM((10 * planes * bands, width), jnp.bfloat16)],
        compiler_params=pltpu.CompilerParams(vmem_limit_bytes=vmem_bytes),
        name="pack",
    )(rotor_step, section)


def inner_kernel(
    bands, section, cells, even_radial, odd_radial, base_state, acc, split, lead, terms, fluxes, base, sem
):
    planes = section.shape[1]
    loading = pltpu.make_async_copy(base_state, base, sem)
    loading.start()
    radial_pass(bands, section, even_radial, odd_radial, acc, lead, terms, fluxes)
    theta_pass(cells, lead, terms, fluxes, split)
    axial_inner(section, acc, lead, terms)
    loading.wait()
    for c in range(5):
        change = flux_factor * acc[c, 1 : planes + 1]
        acc[c, 1 : planes + 1] = 0.75 * base[c] + (0.25 * section[c] + change)


def lead_faces(lead, cells, columns, batch, terms, emit):
    def column_group(g):
        p = g * batch

        def state(r):
            return [lead[n, r, pl.ds(p, batch)] for n in range(5)]

        def cell(r):
            here = state(r)
            flux, wave = cell_terms(here)
            return here, flux, wave

        def keep(r, values):
            for n, value in enumerate((*values[1], values[2])):
                terms[16 + n, r, 0:batch] = value

        def interface(r, right):
            left = (state(r), [terms[16 + n, r, 0:batch] for n in range(5)], terms[21, r, 0:batch])
            for n, value in enumerate(interface_terms(left, right)):
                terms[n, r, 0:batch] = value

        left = cell(0)
        for r in range(5):
            right = cell(r + 1)
            for n, value in enumerate(interface_terms(left, right)):
                terms[n, r, 0:batch] = value
            left = right
        keep(5, left)

        def face(r):
            flux = face_from(
                lambda n, s: terms[n, r + s, 0:batch],
                lambda n: lead[n, r + 2, pl.ds(p, batch)] + lead[n, r + 3, pl.ds(p, batch)],
            )
            emit(r, p, flux)
            if isinstance(r, int) and r + 6 == cells:
                return
            right = cell(jnp.minimum(r + 6, cells - 1))
            interface(r + 5, right)
            keep(r + 6, right)

        if cells - 5 > ghosts:
            loop(cells - 5, face)
        else:
            for r in range(cells - 5):
                face(r)

    loop(columns // batch, column_group)


def keep_flux(fluxes, r, p, flux):
    for n, value in enumerate(flux):
        fluxes[n, r, pl.ds(p, plane_batch)] = value


def radial_pass(bands, section, even_radial, odd_radial, acc, lead, terms, fluxes):
    planes, rows = section.shape[1:3]
    tiles = rows // bands
    index = lax.axis_index("radial")
    at_inner = index == 0
    at_outer = index == lax.axis_size("radial") - 1
    even = lax.rem(index, 2) == 0

    def spread(p):
        for n, c in enumerate(radial_order):
            band = [section[c, p, pl.ds(r, tiles, stride=bands)] for r in range(bands)]
            sign = -1.0 if c == 3 else 1.0
            for r in range(bands):
                lead[n, r + ghosts, p] = band[r]
            for k in range(ghosts):
                one, two = even_radial[c, p, k], odd_radial[c, p, k]
                low, high = jnp.where(even, two, one), jnp.where(even, one, two)
                lead[n, k, p] = jnp.where(at_inner, sign * band[ghosts - 1 - k], low)
                lead[n, bands + ghosts + k, p] = jnp.where(at_outer, sign * band[bands - 1 - k], high)

    loop(planes, spread)
    lead_faces(lead, bands + 2 * ghosts, planes, plane_batch, terms, functools.partial(keep_flux, fluxes))

    def gather(p):
        for n, c in enumerate(radial_order):
            for r in range(bands):
                acc[c, p + 1, pl.ds(r, tiles, stride=bands)] = fluxes[n, r + 1, p] - fluxes[n, r, p]

    loop(planes, gather)


def theta_pass(cells, lead, terms, fluxes, split):
    _, tiles, planes, bands, _ = cells.shape

    def fill(n):
        for j in range(tiles):
            lead[n, ghosts + j, 0:planes] = cells[n, j]
        for k in range(ghosts):
            lead[n, k, 0:planes] = pltpu.roll(cells[n, tiles - ghosts + k], 1, 2)
            lead[n, ghosts + tiles + k, 0:planes] = pltpu.roll(cells[n, k], lanes - 1, 2)

    loop(5, fill)
    lead_faces(lead, tiles + 2 * ghosts, planes, plane_batch, terms, functools.partial(keep_flux, fluxes))
    lane = lane_index((planes, bands, lanes))

    def changes(n):
        before = None
        for r in range(tiles + 1):
            flux = fluxes[n, r, 0:planes]
            if r < ghosts:
                flux = jnp.where(lane == 0, 0.0, flux)
            if r > tiles - ghosts:
                flux = jnp.where(lane == lanes - 1, 0.0, flux)
            if r > 0:
                store_split(split, n, r - 1, (flux - before).reshape(planes * bands, lanes))
            before = flux

    loop(5, changes)


def axial_faces(count, first, acc, lead, terms):
    tiles, bands = lead.shape[2:4]

    def emit(i, p, flux):
        place = pl.ds(pl.multiple_of(p * bands, bands), tile_batch * bands)
        for c, value in zip(axial_order, flux):
            value = value.reshape(tile_batch * bands, lanes)
            acc[c, first + i, place] += value
            acc[c, first + i + 1, place] -= value

    lead_faces(lead, count + 5, tiles, tile_batch, terms, emit)


def axial_inner(section, acc, lead, terms):
    planes = section.shape[1]
    tiles, bands = lead.shape[2:4]
    first = jnp.where(lax.axis_index("blk") == 0, 0, ghosts)
    count = planes + 1 - ghosts
    for c in range(5):
        acc[c, 0] = jnp.zeros(acc.shape[2:], jnp.float32)
        acc[c, planes + 1] = jnp.zeros(acc.shape[2:], jnp.float32)

    def fill(i):
        plane = jnp.clip(first + i - ghosts, 0, planes - 1)
        for c in axial_order:
            lead[c, i] = section[c, plane].reshape(tiles, bands, lanes)

    loop(count + 5, fill)
    axial_faces(count, first, acc, lead, terms)


def inner(section, cells, bands, even_radial, odd_radial, base):
    _, planes, rows, _ = section.shape
    tiles = rows // bands
    depth = max(bands, tiles) + 2 * ghosts
    across = max(planes, tiles)
    vmem = pl.BlockSpec(memory_space=pltpu.VMEM)
    faces = (planes + 1) * tiles + planes * (tiles + bands + 2)
    return pl.pallas_call(
        functools.partial(inner_kernel, bands),
        in_specs=[vmem] * 4 + [pl.BlockSpec(memory_space=pl.ANY)],
        out_shape=(
            jax.ShapeDtypeStruct((5, planes + 2, rows, lanes), jnp.float32),
            jax.ShapeDtypeStruct((10 * planes * bands, tiles * lanes), jnp.bfloat16),
        ),
        scratch_shapes=[
            pltpu.VMEM((5, depth, across, 8, lanes), jnp.float32),
            pltpu.VMEM((22, depth + 1, max(plane_batch, tile_batch), 8, lanes), jnp.float32),
            pltpu.VMEM((5, depth - 5, planes, 8, lanes), jnp.float32),
            pltpu.VMEM(section.shape, jnp.float32),
            pltpu.SemaphoreType.DMA(()),
        ],
        compiler_params=pltpu.CompilerParams(vmem_limit_bytes=vmem_bytes),
        cost_estimate=pl.CostEstimate(
            flops=faces * 8 * lanes * 700, bytes_accessed=section.size * 16, transcendentals=faces * 8 * lanes * 30
        ),
        name="inner",
    )(section, cells, even_radial, odd_radial, base)


def mortar_planes(turn, window, lead, at):
    tiles, bands = lead.shape[2:4]
    skipped = turn[0] // lanes
    rest = turn[0] % lanes
    fraction = 0.25 * turn[1].astype(jnp.float32)
    source = lax.broadcasted_iota(jnp.int32, (2 * lanes, lanes), 0)
    target = lax.broadcasted_iota(jnp.int32, (2 * lanes, lanes), 1)
    gap = source + target - (lanes - 1 + rest)
    blend = jnp.where(gap == 0, 1.0 - fraction, jnp.where(gap == 1, fraction, 0.0)).astype(jnp.bfloat16)
    blend = jnp.concatenate([blend[:lanes]] * 3 + [blend[lanes:]] * 3, axis=0)

    def parts_of(tile):
        start = pl.multiple_of((tile + skipped) * bands, bands)
        cells = window[:, :, pl.ds(start, bands)].reshape(5 * ghosts * bands, lanes)
        parts = []
        for _ in range(3):
            parts.append(cells.astype(jnp.bfloat16))
            cells = cells - parts[-1].astype(jnp.float32)
        return parts

    after = parts_of(tiles)
    for t in range(tiles):
        here = parts_of(tiles - 1 - t)
        mixed = jnp.dot(jnp.concatenate(here + after, axis=1), blend, preferred_element_type=jnp.float32)
        mixed = mixed.reshape(5, ghosts, bands, lanes)
        for c in range(5):
            lead[c, pl.ds(at, ghosts), t] = -mixed[c] if c == 2 else mixed[c]
        after = here


def theta_edges(even, theta_own, even_theta, odd_theta, acc):
    planes, rows = acc.shape[1] - 2, acc.shape[2]
    bands = theta_own.shape[1]
    lane = lane_index((bands, lanes))
    at = lane % group
    inside = lane < group * planes
    cells = []
    for c in theta_order:
        left = jnp.where(even, odd_theta[c], even_theta[c])
        right = jnp.where(even, even_theta[c], odd_theta[c])
        own = jnp.where(inside & (at >= group - ghosts), right, theta_own[c])
        cells.append(jnp.where(inside & (at < ghosts), left, own))
    turn = lambda value, shift: pltpu.roll(value, -shift % lanes, 1) if shift else value
    after = [turn(v, 1) for v in cells]
    terms = interface_terms(with_terms(cells), with_terms(after))
    flux = face_from(lambda n, s: turn(terms[n], s - 2), lambda n: cells[n] + after[n])
    low, high = ghosts - 1, group // 2 + 2
    wanted = inside & (((at >= low) & (at < low + 3)) | ((at >= high) & (at < high + 3)))
    flux = [jnp.where(wanted, value, 0.0) for value in flux]
    changes = [value - turn(value, -1) for value in flux]

    for p in range(planes):
        for c, change in zip(theta_order, changes):
            first = turn(change, group * p + ghosts)
            last = turn(change, group * p + high + ghosts - lanes)
            acc[c, p + 1, 0:bands] += jnp.where(lane < ghosts, first, 0.0)
            acc[c, p + 1, rows - bands : rows] += jnp.where(lane >= lanes - ghosts, last, 0.0)


def tail_kernel(
    gathered, rotor_step, section, acc, split, order, whole, part, theta_own, even_theta, odd_theta, out_state,
    more, lead, terms, window, out, sems
):
    planes = section.shape[1]
    tiles, bands = lead.shape[2:4]
    turn = mortar_turn(rotor_step[0], tiles * lanes)
    swapped = (turn[2] == 1) & (not gathered)
    whole_at = pl.multiple_of(jnp.where(swapped, part.shape[2], 0), bands)
    part_at = pl.multiple_of(jnp.where(swapped, 0, whole.shape[2]), bands)
    arriving = [
        pltpu.make_async_copy(whole, window.at[:, :, pl.ds(whole_at, whole.shape[2])], sems.at[1]),
        pltpu.make_async_copy(part, window.at[:, :, pl.ds(part_at, part.shape[2])], sems.at[2]),
    ]
    for copy in arriving:
        copy.start()
    front = lax.axis_index("blk") == 0
    kept = planes - 1
    own = jnp.where(front, 1, 0)
    own_at = jnp.where(front, 0, ghosts)
    ghost_at = jnp.where(front, kept, 0)
    first = jnp.where(front, planes + 1 - ghosts, 0)

    def fill(i):
        for c in axial_order:
            lead[c, own_at + i] = section[c, own + i].reshape(tiles, bands, lanes)

    loop(kept, fill)

    for c in range(5):
        more[c, 0] = jnp.zeros(more.shape[2:], jnp.float32)
        more[c, planes + 1] = jnp.zeros(more.shape[2:], jnp.float32)
    restore(split, order, planes, more)
    theta_edges(lax.rem(lax.axis_index("theta"), 2) == 0, theta_own, even_theta, odd_theta, more)
    for copy in arriving:
        copy.wait()
    mortar_planes(turn, window, lead, ghost_at)
    axial_faces(ghosts, first, more, lead, terms)

    storing = [pltpu.make_async_copy(out.at[c], out_state.at[c], sems.at[c]) for c in range(5)]
    for c in range(5):
        out[c] = acc[c, 1 : planes + 1] + flux_factor * more[c, 1 : planes + 1]
        storing[c].start()
    for copy in storing:
        copy.wait()


def tail(gathered, rotor_step, section, acc, split, order, whole, part, theta_own, even_theta, odd_theta):
    _, planes, rows, _ = section.shape
    bands = theta_own.shape[1]
    tiles = rows // bands
    smem = pl.BlockSpec(memory_space=pltpu.SMEM)
    vmem = pl.BlockSpec(memory_space=pltpu.VMEM)
    anywhere = pl.BlockSpec(memory_space=pl.ANY)
    return pl.pallas_call(
        functools.partial(tail_kernel, gathered),
        in_specs=[smem, vmem, vmem, vmem, vmem, anywhere, anywhere, vmem, vmem, vmem],
        out_specs=anywhere,
        out_shape=jax.ShapeDtypeStruct(section.shape, jnp.float32),
        scratch_shapes=[
            pltpu.VMEM(acc.shape, jnp.float32),
            pltpu.VMEM((5, planes - 1 + ghosts, tiles, bands, lanes), jnp.float32),
            pltpu.VMEM((22, 2 * ghosts + 3, tile_batch, bands, lanes), jnp.float32),
            pltpu.VMEM((5, ghosts, whole.shape[2] + part.shape[2], lanes), jnp.float32),
            pltpu.VMEM(section.shape, jnp.float32),
            pltpu.SemaphoreType.DMA((5,)),
        ],
        compiler_params=pltpu.CompilerParams(vmem_limit_bytes=vmem_bytes),
        name="tail",
    )(rotor_step, section, acc, split, order, whole, part, theta_own, even_theta, odd_theta)


def slab_routes(turns, slabs):
    both = []
    for ahead in (1, 0):
        both.append(
            [
                (block * slabs + slab, (1 - block) * slabs + (turns - ahead - slab) % slabs)
                for block in range(2)
                for slab in range(slabs)
            ]
        )
    return both


def shards(base_state, section_state, rotor_step):
    bands, width = section_state.shape[2:]
    rows = width // lanes * bands
    slabs = lax.axis_size("theta")
    slab = lax.axis_index("theta")
    parts = lax.axis_size("radial")
    offset = lax.div(rotor_step[0], 4)
    turns = lax.div(offset, width)
    second_half = lax.div(lax.rem(offset, width), width // 2)
    gathered = slabs > most_slabs
    base, section = tile_rows(base_state), tile_rows(section_state)
    held, even_theta, odd_theta, theta_own, even_radial, odd_radial, whole, part, cells, order = pack(
        rotor_step, section, bands
    )

    def pairs(count, first, closed):
        ends = range(first, count if closed else count - 1, 2)
        return [pair for i in ends for pair in ((i, (i + 1) % count), ((i + 1) % count, i))]

    def halos(even_radial, odd_radial, even_theta, odd_theta):
        return (
            lax.ppermute(even_radial, "radial", pairs(parts, 0, False)),
            lax.ppermute(odd_radial, "radial", pairs(parts, 1, False)),
            lax.ppermute(even_theta, "theta", pairs(slabs, 0, True)),
            lax.ppermute(odd_theta, "theta", pairs(slabs, 1, True)),
        )

    if gathered:
        even_radial, odd_radial, even_theta, odd_theta = halos(even_radial, odd_radial, even_theta, odd_theta)
        facing = lax.ppermute(whole, "blk", [(0, 1), (1, 0)])
        ring = lax.all_gather(facing, "theta", axis=2, tiled=True)
        ring = jnp.concatenate([ring, ring, ring[:, :, : rows // 2]], axis=2)
        begin = (turns - 1 - slab) % slabs * rows + second_half * (rows // 2)
        whole = lax.dynamic_slice_in_dim(ring, begin, rows, 2)
        part = lax.dynamic_slice_in_dim(ring, begin + rows, rows // 2, 2)
        acc, split = inner(held, cells, bands, even_radial, odd_radial, base)
    else:

        def branch(case):
            near, far = slab_routes(case // 2 + 1, slabs)
            whole_route, part_route = (near, far) if case % 2 == 0 else (far, near)

            def run(held, cells, base, whole, part, *ends):
                whole = lax.ppermute(whole, ("blk", "theta"), whole_route)
                part = lax.ppermute(part, ("blk", "theta"), part_route)
                even_radial, odd_radial, *ends = halos(*ends)
                acc, split = inner(held, cells, bands, even_radial, odd_radial, base)
                return acc, split, whole, part, *ends

            return run

        case = (turns - 1) * 2 + second_half
        branches = [branch(i) for i in range((slabs - 1) * 2)]
        ends = (even_radial, odd_radial, even_theta, odd_theta)
        acc, split, whole, part, even_theta, odd_theta = lax.switch(
            case, branches, held, cells, base, whole, part, *ends
        )
    out = tail(gathered, rotor_step, section, acc, split, order, whole, part, theta_own, even_theta, odd_theta)
    return from_tile_rows(out, bands)


def solution(mesh):
    in_specs = (P(None, "blk", "radial", "theta"), P(None, "blk", "radial", "theta"), P())
    out_specs = P(None, "blk", "radial", "theta")
    return jax.shard_map(shards, mesh=mesh, in_specs=in_specs, out_specs=out_specs, check_vma=False)
```
